32 devices in a mesh: dp: 16 (over z, y, x), mp: 2 (over core).
Axes of the slice: x: 2, y: 2, z: 4, core: 2. Of those that a mesh axis runs over, the one named last changes fastest.
Arguments:
- tokens: bfloat16 [128, 288, 768], P('dp', None, 'mp'), may hold values from -6 to 6
- segment_ids: int32 [128, 288], P('dp'), may hold values from 0 to 3, never falling along the last dimension, each value on 1 to 144 neighbouring positions
- positions: int32 [128, 288], P('dp'), may hold values from 0 to 511
- query_vectors: float32 [16, 128], P('dp'), may hold values from -3 to 3
- doc_owner: int32 [16, 8], P('dp'), may hold values from 0 to 15, as said below
- doc_slot: int32 [16, 8], P('dp'), may hold values from 0 to 15
- doc_store: bfloat16 [256, 288, 768], P('dp', None, 'mp'), may hold values from -3 to 3
- pos_table: bfloat16 [512, 768], P(None, 'mp'), may hold values from -3 to 3
- w_query: bfloat16 [768, 768], P(None, 'mp'), may hold values from -0.21875 to 0.21875
- w_key: bfloat16 [768, 768], P(None, 'mp'), may hold values from -0.21875 to 0.21875
- w_value: bfloat16 [768, 768], P(None, 'mp'), may hold values from -0.21875 to 0.21875
- b_query: float32 [768], P('mp'), may hold values from -3 to 3
- b_value: float32 [768], P('mp'), may hold values from -3 to 3
- w_out: bfloat16 [768, 768], P('mp'), may hold values from -0.4375 to 0.4375
- b_out: float32 [768], P('mp'), may hold values from -2 to 2
- gain_attn: float32 [768], P('mp'), may hold values from 0.5 to 1.5
- shift_attn: float32 [768], P('mp'), may hold values from -2 to 2
- w_inner: bfloat16 [768, 3072], P(None, 'mp'), may hold values from -0.21875 to 0.21875
- b_inner: float32 [3072], P('mp'), may hold values from -3 to 3
- w_outer: bfloat16 [3072, 768], P('mp'), may hold values from -0.15625 to 0.15625
- b_outer: float32 [768], P('mp'), may hold values from -2 to 2
- gain_ffn: float32 [768], P('mp'), may hold values from 0.5 to 1.5
- shift_ffn: float32 [768], P('mp'), may hold values from -2 to 2
- w_cls: bfloat16 [768, 128], P('mp'), may hold values from -0.21875 to 0.21875
- cotangent: bfloat16 [16, 288, 768], P('dp', None, 'mp'), may hold values from -6 to 6
Outputs:
- mixed: bfloat16 [16, 288, 768], P('dp', None, 'mp')
- grad_tokens: bfloat16 [128, 288, 768], P('dp', None, 'mp')
- grad_query: float32 [16, 128], P('dp')
- grad_docs: float32 [256, 288, 768], P('dp', None, 'mp')
- grad_pos: float32 [512, 768], P('dp', 'mp')
- grad_wq: float32 [768, 768], P('dp', 'mp')
- grad_wk: float32 [768, 768], P('dp', 'mp')
- grad_wv: float32 [768, 768], P('dp', 'mp')
- grad_bq: float32 [768], P('mp')
- grad_bv: float32 [768], P('mp')
- grad_wo: float32 [768, 768], P('mp', 'dp')
- grad_bo: float32 [768], P('mp')
- grad_gain_attn: float32 [768], P('mp')
- grad_shift_attn: float32 [768], P('mp')
- grad_w_inner: float32 [768, 3072], P('dp', 'mp')
- grad_b_inner: float32 [3072], P('mp')
- grad_w_outer: float32 [3072, 768], P('mp', 'dp')
- grad_b_outer: float32 [768], P('mp')
- grad_gain_ffn: float32 [768], P('mp')
- grad_shift_ffn: float32 [768], P('mp')
- grad_w_cls: float32 [768, 128], P('mp', 'dp')
The draws below stay inside these ranges and needn't reach their ends.
Inputs may be any that keep to these rules, and one draw needn't show every extreme that they name: `doc_owner`: the 8 owners in the row of dp index i are distinct and each is (i + o) mod 16 for an offset o with -6 <= o < 6. `segment_ids`: segment numbers never fall along a block; a segment holds at most 144 tokens.
All inputs are finite; a program needn't handle non-finite values.
Results may differ from the reference program's by a relative error of at most 0.019.
Values may be sent and summed in bfloat16 or wider, within the bound.
A program may use at most 256 MiB of HBM per device.

```python
import math
import jax
import jax.numpy as jnp
import numpy as np
from jax import lax

D = 768
HEADS = 12
HEAD_DIM = 64
FF = 3072
PROJ = 128
MAXPOS = 512
TOPK = 8
SEQ = 288
REACH = 6
DOCS_DEV = 16
ROWS_DEV = 8
QUERIES = 16
BLOCKS = 128
DOCS = 256
N_DP = 16


def draw_doc_owner(key, part):
    key = jax.random.fold_in(key, 11)
    row_keys = jax.random.split(key, N_DP)
    picks = jax.vmap(lambda one_key: jax.random.permutation(one_key, 2 * REACH)[:ROWS_DEV])(row_keys)
    offsets = picks.astype(jnp.int32) - REACH
    return ((jnp.arange(N_DP, dtype=jnp.int32)[:, None] + offsets) % N_DP).astype(jnp.int32)


def draw_query_vectors(key, part):
    key = jax.random.fold_in(key, 17)
    drawn = jnp.clip(0.75 * jax.random.normal(key, (QUERIES, PROJ), jnp.float32), -3.0, 3.0)
    return drawn.astype(jnp.float32)


def set_ends(values, key, least, high):
    spot = [jax.random.randint(jax.random.fold_in(key, axis), (), 0, length) for axis, length in enumerate(values.shape)]
    main_axis = values.shape.index(max(values.shape))
    next_to = spot[:main_axis] + [(spot[main_axis] + 1) % values.shape[main_axis]] + spot[main_axis + 1:]
    return values.at[tuple(spot)].set(least).at[tuple(next_to)].set(high)


def level_of(own_key, dims, cuts, least, largest):
    def one(dim, parts):
        draws = jax.random.uniform(jax.random.fold_in(jax.random.fold_in(own_key, 6), dim), (parts,), jnp.float32, least / len(cuts), largest / len(cuts))
        return jnp.repeat(jnp.exp(draws), dims[dim] // parts).reshape((-1,) + (1,) * (len(dims) - dim - 1))

    factor_of = one(*cuts[0])
    for cut in cuts[1:]:
        factor_of = factor_of * one(*cut)
    return factor_of


def length_profile(number_of, total, reach, slope):
    loads = [(1 << 20) // math.isqrt(rank ** slope) + 1 for rank in range(2, number_of + 1)]
    rest, holding = total - reach - (number_of - 1), [1] * (number_of - 1)
    while rest > 0:
        movable = [i for i in range(number_of - 1) if holding[i] < reach]
        mass, budget = sum([loads[i] for i in movable]), rest
        for i in movable:
            extra = min(reach - holding[i], max(1, budget * loads[i] // mass), rest)
            holding[i] = holding[i] + extra
            rest = rest - extra
    return np.array([reach] + holding)


def uneven_parts(key, number_of, total, reach, slope):
    if number_of == 2:
        one = jax.random.randint(key, (), max(1, total - reach), min(reach, total - 1) + 1)
        return jnp.stack([one, total - one])
    tallies = jnp.asarray(length_profile(number_of, total, reach, slope), jnp.int32)
    pairs = (number_of - 1) // 2
    source_of, sink = tallies[1:1 + 2 * pairs:2], tallies[2:2 + 2 * pairs:2]
    slack = jnp.minimum(source_of - 1, reach - sink)
    passed = jax.random.randint(jax.random.fold_in(key, 1), (pairs,), 0, 1 << 20) % (slack + 1)
    tallies = tallies.at[1:1 + 2 * pairs:2].set(source_of - passed).at[2:2 + 2 * pairs:2].set(sink + passed)
    return tallies[jax.random.permutation(jax.random.fold_in(key, 2), number_of)]


def centred(key, shape, scale, reach, cuts=(), held_as=jnp.bfloat16):
    entries = scale * jax.random.normal(key, shape, jnp.float32)
    if cuts:
        entries = entries * level_of(key, shape, cuts, -0.22, 0.18)
    return jnp.clip(entries, -reach, reach).astype(held_as)


def setup_inputs(seed: int = 0) -> dict:
    key_of = jax.random.split(jax.random.key(seed), 26)
    tokens = centred(key_of[0], (BLOCKS, SEQ, D), 1.0, 6.0, ((0, 16), (2, 2)))
    segment_ids = jax.vmap(lambda own: jnp.searchsorted(jnp.cumsum(uneven_parts(own, 4, SEQ, SEQ // 2, 2)), jnp.arange(SEQ), side="right"))(jax.random.split(key_of[1], BLOCKS)).reshape((BLOCKS, SEQ)).astype(jnp.int32)
    positions = set_ends(jax.random.randint(key_of[2], (BLOCKS, SEQ), 0, MAXPOS), jax.random.fold_in(key_of[2], 1), 0, MAXPOS - 1).astype(jnp.int32)
    query_vectors = draw_query_vectors(jax.random.fold_in(key_of[25], 71), 0)
    doc_owner = draw_doc_owner(jax.random.fold_in(key_of[25], 71), 0)
    doc_slot = set_ends(jax.random.randint(key_of[5], (N_DP, ROWS_DEV), 0, DOCS_DEV), jax.random.fold_in(key_of[5], 1), 0, DOCS_DEV - 1).astype(jnp.int32)
    doc_store = centred(key_of[6], (DOCS, SEQ, D), 0.5, 3.0, ((0, 16), (2, 2)))
    pos_table = centred(key_of[7], (MAXPOS, D), 0.5, 3.0, ((1, 2),))
    w_query = centred(key_of[8], (D, D), D ** -0.5, 0.21875, ((1, 2),))
    w_key = centred(key_of[9], (D, D), D ** -0.5, 0.21875, ((1, 2),))
    w_value = centred(key_of[10], (D, D), D ** -0.5, 0.21875, ((1, 2),))
    b_query = centred(key_of[11], (D,), 0.5, 3.0, ((0, 2),), jnp.float32)
    b_value = centred(key_of[12], (D,), 0.5, 3.0, ((0, 2),), jnp.float32)
    w_out = centred(key_of[13], (D, D), (D // 4) ** -0.5, 0.4375, ((0, 2),))
    b_out = centred(key_of[14], (D,), 0.3, 2.0, ((0, 2),), jnp.float32)
    gain_attn = jnp.clip(1.0 + 0.1 * jax.random.normal(key_of[15], (D,), jnp.float32), 0.5, 1.5)
    shift_attn = centred(key_of[16], (D,), 0.3, 2.0, ((0, 2),), jnp.float32)
    w_inner = centred(key_of[17], (D, FF), D ** -0.5, 0.21875, ((1, 2),))
    b_inner = centred(key_of[18], (FF,), 0.5, 3.0, ((0, 2),), jnp.float32)
    w_outer = centred(key_of[19], (FF, D), (FF // 2) ** -0.5, 0.15625, ((0, 2),))
    b_outer = centred(key_of[20], (D,), 0.3, 2.0, ((0, 2),), jnp.float32)
    gain_ffn = jnp.clip(1.0 + 0.1 * jax.random.normal(key_of[21], (D,), jnp.float32), 0.5, 1.5)
    shift_ffn = centred(key_of[22], (D,), 0.3, 2.0, ((0, 2),), jnp.float32)
    w_cls = centred(key_of[23], (D, PROJ), D ** -0.5, 0.21875, ((0, 2),))
    cotangent = centred(key_of[24], (QUERIES, SEQ, D), 1.0, 6.0, ((0, 16), (2, 2)))
    return {"tokens": tokens, "segment_ids": segment_ids, "positions": positions, "query_vectors": query_vectors, "doc_owner": doc_owner, "doc_slot": doc_slot, "doc_store": doc_store, "pos_table": pos_table, "w_query": w_query, "w_key": w_key, "w_value": w_value, "b_query": b_query, "b_value": b_value, "w_out": w_out, "b_out": b_out, "gain_attn": gain_attn, "shift_attn": shift_attn, "w_inner": w_inner, "b_inner": b_inner, "w_outer": w_outer, "b_outer": b_outer, "gain_ffn": gain_ffn, "shift_ffn": shift_ffn, "w_cls": w_cls, "cotangent": cotangent}


EPSILON = 1e-05
PRECISE = lax.Precision.HIGHEST
NEGATIVE = -1e+30

@jax.custom_vjp
def low(v):
    return lax.optimization_barrier(v.astype(jnp.bfloat16)).astype(jnp.float32)

@jax.custom_vjp
def low_back(v):
    return v

def low_keep(v):
    return (low(v), None)

def low_pass(kept, grad):
    return (grad,)

def back_keep(v):
    return (v, None)

def back_low(kept, grad):
    return (low(grad),)
low.defvjp(low_keep, low_pass)
low_back.defvjp(back_keep, back_low)

def layer_norm(hidden, gain, offset):
    average = lax.optimization_barrier(jnp.mean(hidden, axis=-1, keepdims=True))
    centered = hidden - average
    spread = lax.optimization_barrier(jnp.mean(centered * centered, axis=-1, keepdims=True))
    return centered * lax.rsqrt(spread + EPSILON) * gain + offset

def project(left, weight):
    return jnp.einsum('tsd,de->tse', left, weight, precision=PRECISE)

def query_block(inputs_tok, seg_keys, places, doc_ids, query_vec, tables):
    pos_table, doc_store, w_query, w_key, w_value, b_query, b_value, w_out, b_out, gain_attn, shift_attn, w_inner, b_inner, w_outer, b_outer, gain_ffn, shift_ffn, w_cls = tables
    embedded = low_back(inputs_tok + pos_table[places] + doc_store[doc_ids])
    embedded_low = low(embedded)
    head_shape = (TOPK, SEQ, HEADS, HEAD_DIM)
    queries = low(low_back(project(embedded_low, w_query) + b_query)).reshape(head_shape)
    key_heads = low(low_back(project(embedded_low, w_key))).reshape(head_shape)
    values = low(low_back(project(embedded_low, w_value) + b_value)).reshape(head_shape)
    scores = jnp.einsum('bqhd,bkhd->bhqk', queries, key_heads, precision=PRECISE) * HEAD_DIM ** (-0.5)
    same_seg = seg_keys[:, None, :, None] == seg_keys[:, None, None, :]
    scores = low_back(jnp.where(same_seg, scores, NEGATIVE))
    weights = jax.nn.softmax(scores, axis=-1)
    context = jnp.einsum('bhqk,bkhd->bqhd', low(weights), values, precision=PRECISE).reshape(TOPK, SEQ, D)
    context = low(low_back(context))
    middle = layer_norm(embedded + low_back(project(context, w_out)) + b_out, gain_attn, shift_attn)
    inner_pre = low_back(project(low(middle), w_inner)) + b_inner
    outer_sum = low_back(project(low(jax.nn.gelu(inner_pre, approximate=False)), w_outer)) + b_outer
    result = low(low_back(layer_norm(middle + outer_sum, gain_ffn, shift_ffn)))
    summary = jnp.dot(result[:, 0, :], w_cls, precision=PRECISE)
    logits = lax.optimization_barrier(jnp.sum(summary * query_vec[None, :], axis=-1)) * PROJ ** (-0.5)
    shares = jax.nn.softmax(logits)
    return jnp.einsum('k,ksd->sd', shares, result, precision=PRECISE)

def reference(tokens, segment_ids, positions, query_vectors, doc_owner, doc_slot, doc_store, pos_table, w_query, w_key, w_value, b_query, b_value, w_out, b_out, gain_attn, shift_attn, w_inner, b_inner, w_outer, b_outer, gain_ffn, shift_ffn, w_cls, cotangent):
    doc_ids = (doc_owner * DOCS_DEV + doc_slot).astype(jnp.int32).reshape(QUERIES, TOPK)
    seg_keys = segment_ids.reshape(QUERIES, TOPK, SEQ)
    places = positions.reshape(QUERIES, TOPK, SEQ).astype(jnp.int32)
    floats = tuple((element.astype(jnp.float32) for element in (tokens, query_vectors, pos_table, doc_store, w_query, w_key, w_value, b_query, b_value, w_out, b_out, gain_attn, shift_attn, w_inner, b_inner, w_outer, b_outer, gain_ffn, shift_ffn, w_cls)))

    def forward(arrays):
        inputs_tok = arrays[0].reshape(QUERIES, TOPK, SEQ, D)
        tables = arrays[2:]

        def one_query(pieces):
            return query_block(pieces[0], pieces[1], pieces[2], pieces[3], pieces[4], tables)
        return lax.map(jax.checkpoint(one_query), (inputs_tok, seg_keys, places, doc_ids, arrays[1]))
    mixed_out, pullback = jax.vjp(forward, floats)
    gradient = pullback(cotangent.astype(jnp.float32))[0]
    return (mixed_out.astype(jnp.bfloat16), gradient[0].reshape(BLOCKS, SEQ, D).astype(jnp.bfloat16), gradient[1], gradient[3], gradient[2], gradient[4], gradient[5], gradient[6], gradient[7], gradient[8], gradient[9], gradient[10], gradient[11], gradient[12], gradient[13], gradient[14], gradient[15], gradient[16], gradient[17], gradient[18], gradient[19])
```

```python
import functools

import jax
import jax.numpy as jnp
from jax import lax
from jax.experimental import pallas as pl
from jax.experimental.pallas import tpu as pltpu
from jax.sharding import PartitionSpec as P

HEAD_DIM = 64
PROJ = 128
REACH = 6
SLOTS = 2 * REACH
EPSILON = 1e-05
NEGATIVE = -1e30
PRECISE = lax.Precision.HIGHEST
MESH = pl.DeviceIdType.MESH
BF = jnp.bfloat16
F32 = jnp.float32
VMEM_LIMIT = 60 * 1024 * 1024
VQ, VV, VO, VGA, VSA, VBO, VGF, VSF, VIN = range(9)
VROWS = 16


def any_spec(count):
    return [pl.BlockSpec(memory_space=pl.ANY)] * count


def vmem_spec(count):
    return [pl.BlockSpec(memory_space=pltpu.VMEM)] * count


def nt(left, right):
    return lax.dot_general(left, right, (((1,), (1,)), ((), ())), preferred_element_type=F32)


def tn(left, right):
    return lax.dot_general(left, right, (((0,), (0,)), ((), ())), preferred_element_type=F32)


def mm(left, right):
    return jnp.dot(left, right, preferred_element_type=F32)


def greet(targets):
    barrier = pltpu.get_barrier_semaphore()
    for target in targets:
        pl.semaphore_signal(barrier, inc=1, device_id=target, device_id_type=MESH)
    pl.semaphore_wait(barrier, len(targets))


def ring_partners(me, core, n):
    return [(lax.rem(me + step + n, n), core) for step in range(-REACH, REACH + 1) if step != 0]


def fetch_kernel(
    n, req, docs_in, tok_in, cot_in, wq_in, wk_in, wv_in, wo_in, wi_in, wu_in, wc_in, pos_in, vec_in,
    docs, tok, cot, wqkv, wo, wi, wu, wc, pos, vec, got,
    doc_buf, stage, got_s,
    req_send, req_recv, doc_send, doc_recv, fwd_send, fwd_recv, own_sem, sib_send, sib_recv, misc_sem,
):
    me = lax.axis_index("dp")
    core = lax.axis_index("mp")
    other = 1 - core
    sibling = (me, other)
    greet(ring_partners(me, core, n) + [sibling])
    half = tok_in.shape[2]
    rows = tok_in.shape[0] // 2
    inner = wi_in.shape[1]
    mine = pl.ds(pl.multiple_of(core * half, half), half)
    asked = []
    for slot in range(SLOTS):
        if slot == REACH:
            asked.append(None)
            continue
        copy = pltpu.make_async_remote_copy(
            src_ref=req.at[slot], dst_ref=got.at[slot], send_sem=req_send.at[slot],
            recv_sem=req_recv.at[slot],
            device_id=(lax.rem(me + slot - REACH + n, n), core), device_id_type=MESH,
        )
        copy.start()
        asked.append(copy)
    load = pltpu.make_async_copy(docs_in, doc_buf, misc_sem.at[0])
    load.start()
    pairs = [
        (tok_in.at[pl.ds(core * rows, rows)], tok_in.at[pl.ds(other * rows, rows)], tok.at[:, :, mine]),
        (cot_in.at[0], cot_in.at[0], cot.at[:, mine]),
        (pos_in, pos_in, pos.at[:, mine]),
        (vec_in, vec_in, vec.at[core]),
    ]
    for index, source in enumerate((wq_in, wk_in, wv_in)):
        begin = pl.multiple_of(index * 2 * half + core * half, half)
        pairs.append((source, source, wqkv.at[:, pl.ds(begin, half)]))
    pairs += [
        (wo_in, wo_in, wo.at[mine]),
        (wi_in, wi_in, wi.at[:, pl.ds(pl.multiple_of(core * inner, inner), inner)]),
        (wu_in, wu_in, wu.at[pl.ds(pl.multiple_of(core * inner, inner), inner)]),
        (wc_in, wc_in, wc.at[mine]),
    ]
    moves = []
    for index, (own_src, sib_src, dst) in enumerate(pairs):
        far = pltpu.make_async_remote_copy(
            src_ref=sib_src, dst_ref=dst, send_sem=sib_send.at[index], recv_sem=sib_recv.at[index],
            device_id=sibling, device_id_type=MESH,
        )
        far.start()
        near = pltpu.make_async_copy(own_src, dst, own_sem.at[index])
        near.start()
        moves += [far, near]
    got[REACH] = req[REACH]
    for copy in asked:
        if copy is not None:
            copy.wait_recv()
    to_scalar = pltpu.make_async_copy(got, got_s, misc_sem.at[1])
    to_scalar.start()
    load.wait()
    to_scalar.wait()
    sent = [None] * SLOTS
    order = sorted(range(SLOTS), key=lambda s: -abs(s - REACH))
    for slot in order:
        stage[slot] = doc_buf[jnp.maximum(got_s[slot, 0, 0], 0)]
        if slot == REACH:
            copy = pltpu.make_async_copy(stage.at[slot], docs.at[slot, :, mine], misc_sem.at[2])
        else:
            copy = pltpu.make_async_remote_copy(
                src_ref=stage.at[slot], dst_ref=docs.at[slot, :, mine], send_sem=doc_send.at[slot],
                recv_sem=doc_recv.at[slot],
                device_id=(lax.rem(me - slot + REACH + n, n), core), device_id_type=MESH,
            )
        copy.start()
        sent[slot] = copy
    passed = []
    for slot in reversed(order):
        if slot == REACH:
            sent[slot].wait()
        else:
            sent[slot].wait_recv()
        copy = pltpu.make_async_remote_copy(
            src_ref=docs.at[slot, :, mine], dst_ref=docs.at[slot, :, mine], send_sem=fwd_send.at[slot],
            recv_sem=fwd_recv.at[slot], device_id=sibling, device_id_type=MESH,
        )
        copy.start()
        passed.append(copy)
    for copy in moves + passed:
        copy.wait()
    for slot in range(SLOTS):
        if slot != REACH:
            asked[slot].wait_send()
            sent[slot].wait_send()


def fetch(n, req, doc_store, tokens, cot, wq, wk, wv, wo, wi, wu, wc, pos, vec):
    rows, seq, half = tokens.shape
    full = 2 * half
    inner = wi.shape[1]
    shape = jax.ShapeDtypeStruct
    out_shape = (
        shape((SLOTS, seq, full), BF),
        shape((rows // 2, seq, full), BF),
        shape((seq, full), BF),
        shape((full, 3 * full), BF),
        shape((full, full), BF),
        shape((full, 2 * inner), BF),
        shape((2 * inner, full), BF),
        shape((full, wc.shape[1]), BF),
        shape((pos.shape[0], full), BF),
        shape((2,) + vec.shape, F32),
        shape(req.shape, jnp.int32),
    )
    dma = pltpu.SemaphoreType.DMA
    return pl.pallas_call(
        functools.partial(fetch_kernel, n),
        out_shape=out_shape,
        in_specs=vmem_spec(1) + any_spec(12),
        out_specs=tuple(any_spec(10) + vmem_spec(1)),
        scratch_shapes=[
            pltpu.VMEM(doc_store.shape, BF),
            pltpu.VMEM((SLOTS, seq, half), BF),
            pltpu.SMEM(req.shape, jnp.int32),
            dma((SLOTS,)), dma((SLOTS,)), dma((SLOTS,)), dma((SLOTS,)), dma((SLOTS,)), dma((SLOTS,)),
            dma((11,)), dma((11,)), dma((11,)), dma((3,)),
        ],
        compiler_params=pltpu.CompilerParams(
            collective_id=0, has_side_effects=True, vmem_limit_bytes=VMEM_LIMIT
        ),
        name="fetch",
    )(req, doc_store, tokens, cot, wq, wk, wv, wo, wi, wu, wc, pos, vec)


def wide(vec, row):
    return jnp.concatenate([vec[0, row:row + 1, :], vec[1, row:row + 1, :]], axis=1)


def inner_bias(vec):
    return jnp.concatenate([vec[h, VIN + j:VIN + j + 1, :] for h in range(2) for j in range(4)], axis=1)


def normalize(hidden):
    average = jnp.mean(hidden, axis=-1, keepdims=True)
    centered = hidden - average
    spread = jnp.mean(centered * centered, axis=-1, keepdims=True)
    inverse = lax.rsqrt(spread + EPSILON)
    return centered * inverse, inverse


def head_masks():
    lane = lax.broadcasted_iota(jnp.int32, (1, 2 * HEAD_DIM), 1)
    first = (lane < HEAD_DIM).astype(F32)
    return [first.astype(BF), (1.0 - first).astype(BF)]


def forward_kernel(
    slot_ref, tok, doc, place, seg_col, seg_row, pos, wqkv, wo, wi, wu, wc, vec, cot,
    xlow, qkv, lse, ctx, nmid, imid, mlow, act, slope, nout, iout, res, summ, prod,
    bias, stats, acc,
):
    seq, full = tok.shape[1], tok.shape[2]
    table = pos.shape[0]
    one_hot = (place[0] == lax.broadcasted_iota(jnp.int32, (seq, table), 1)).astype(F32).astype(BF)
    embedded = tok[0].astype(F32) + mm(one_hot, pos[...]) + doc[0].astype(F32)
    low = embedded.astype(BF)
    xlow[0] = low
    acc[...] = embedded
    q = (mm(low, wqkv[:, 0:full]) + wide(vec, VQ)).astype(BF)
    qkv[0, :, 0:full] = q * jnp.asarray(HEAD_DIM ** -0.5, BF)
    qkv[0, :, full:2 * full] = mm(low, wqkv[:, full:2 * full]).astype(BF)
    qkv[0, :, 2 * full:] = (mm(low, wqkv[:, 2 * full:]) + wide(vec, VV)).astype(BF)
    bias[...] = jnp.where(seg_col[0] == seg_row[0], 0.0, NEGATIVE)
    masks = head_masks()
    pair = 2 * HEAD_DIM
    stats[...] = jnp.zeros_like(stats)

    def heads(p, carry):
        at = pl.multiple_of(p * pair, pair)
        queries = qkv[0, :, pl.ds(at, pair)]
        keys = qkv[0, :, pl.ds(full + at, pair)]
        values = qkv[0, :, pl.ds(2 * full + at, pair)]
        lane = lax.broadcasted_iota(jnp.int32, (seq, pair), 1)
        parts = []
        for h in range(2):
            s = nt(queries * masks[h], keys) + bias[...]
            top = jnp.max(s, axis=1, keepdims=True)
            e = jnp.exp(s - top)
            total = jnp.sum(e, axis=1, keepdims=True)
            parts.append(mm((e * (1.0 / total)).astype(BF), values))
            stats[0:seq, :] = jnp.where(lane == 2 * p + h, top + jnp.log(total), stats[0:seq, :])
        ctx[0, :, pl.ds(at, pair)] = jnp.where(lane < HEAD_DIM, parts[0], parts[1]).astype(BF)
        return carry

    lax.fori_loop(0, full // pair, heads, 0)
    lse[0] = jnp.transpose(stats[...])[0:lse.shape[1], 0:seq]
    normed, inverse = normalize(acc[...] + mm(ctx[0], wo[...]) + wide(vec, VO))
    middle = normed * wide(vec, VGA) + wide(vec, VSA)
    nmid[0] = normed.astype(BF)
    imid[0] = inverse
    acc[...] = middle + wide(vec, VBO)
    mlow[0] = middle.astype(BF)
    hidden = wi.shape[1]
    chunk = hidden // 4
    bin_all = inner_bias(vec)
    for j in range(4):
        cols = slice(j * chunk, (j + 1) * chunk)
        pre = mm(mlow[0], wi[:, cols]) + bin_all[:, cols]
        phi = 0.5 + 0.5 * lax.erf(pre * (0.5 ** 0.5))
        act[0, :, cols] = (pre * phi).astype(BF)
        slope[0, :, cols] = (phi + pre * (jnp.exp(-0.5 * pre * pre) * 0.3989422804014327)).astype(BF)
        acc[...] += mm(act[0, :, cols], wu[cols, :])
    normed, inverse = normalize(acc[...])
    nout[0] = normed.astype(BF)
    iout[0] = inverse
    result = (normed * wide(vec, VGF) + wide(vec, VSF)).astype(BF)
    res[0] = result
    summ[0] = mm(res[0, 0:16, :], wc[...])[0:8]
    product = jnp.sum(cot[...].astype(F32) * result.astype(F32))
    prod[0] = jnp.full(prod.shape[1:], product, F32)


def forward(slots, tok, docs, place, seg_col, seg_row, pos, wqkv, wo, wi, wu, wc, vec, cot):
    rows, seq, full = tok.shape
    hidden = wi.shape[1]
    shape = jax.ShapeDtypeStruct
    heads = full // HEAD_DIM
    lse_rows = (heads + 7) // 8 * 8

    def row_block(*dims):
        return pl.BlockSpec((1,) + dims, lambda b, s: (b,) + (0,) * len(dims))

    def whole(*dims):
        return pl.BlockSpec(dims, lambda b, s: (0,) * len(dims), pipeline_mode=pl.Buffered(1))

    outs = [
        ((seq, full), BF), ((seq, 3 * full), BF), ((lse_rows, seq), F32), ((seq, full), BF),
        ((seq, full), BF), ((seq, 1), F32), ((seq, full), BF), ((seq, hidden), BF), ((seq, hidden), BF),
        ((seq, full), BF), ((seq, 1), F32), ((seq, full), BF), ((8, PROJ), F32), ((8, PROJ), F32),
    ]
    return pl.pallas_call(
        forward_kernel,
        out_shape=tuple(shape((rows,) + dims, kind) for dims, kind in outs),
        grid_spec=pltpu.PrefetchScalarGridSpec(
            num_scalar_prefetch=1,
            grid=(rows,),
            in_specs=[
                row_block(seq, full),
                pl.BlockSpec((1, seq, full), lambda b, s: (s[b], 0, 0)),
                row_block(seq, 1), row_block(seq, 1), row_block(1, seq),
                whole(*pos.shape), whole(*wqkv.shape), whole(*wo.shape), whole(*wi.shape),
                whole(*wu.shape), whole(*wc.shape), whole(*vec.shape), whole(*cot.shape),
            ],
            out_specs=tuple(row_block(*dims) for dims, _ in outs),
            scratch_shapes=[
                pltpu.VMEM((seq, seq), F32), pltpu.VMEM((384, 128), F32), pltpu.VMEM((seq, full), F32),
            ],
        ),
        compiler_params=pltpu.CompilerParams(vmem_limit_bytes=VMEM_LIMIT),
        name="forward",
    )(slots, tok, docs, place, seg_col, seg_row, pos, wqkv, wo, wi, wu, wc, vec, cot)


def shares_kernel(summ, prod, qv, shares, dsum, gq, mine, theirs, send_sem, recv_sem):
    me = lax.axis_index("dp")
    core = lax.axis_index("mp")
    sibling = (me, 1 - core)
    greet([sibling])
    rows = summ.shape[0]
    mine[...] = jnp.concatenate([summ[b, 0:1, :] for b in range(rows)] + [prod[b, 0:1, :] for b in range(rows)], axis=0)
    copy = pltpu.make_async_remote_copy(
        src_ref=mine, dst_ref=theirs, send_sem=send_sem, recv_sem=recv_sem,
        device_id=sibling, device_id_type=MESH,
    )
    copy.start()
    copy.wait()
    first = core == 0
    low = jnp.where(first, mine[...], theirs[...])
    high = jnp.where(first, theirs[...], mine[...])
    summary = jnp.concatenate([low[:rows], high[:rows]], axis=0)
    product = jnp.concatenate([low[rows:], high[rows:]], axis=0)
    inv_root = PROJ ** (-0.5)
    logits = jnp.sum(summary * qv[...], axis=1, keepdims=True) * inv_root
    e = jnp.exp(logits - jnp.max(logits, axis=0, keepdims=True))
    share = e / jnp.sum(e, axis=0, keepdims=True)
    dlogits = share * (product - jnp.sum(share * product, axis=0, keepdims=True))
    gq[...] = jnp.sum(dlogits * summary, axis=0, keepdims=True) * inv_root
    ds = dlogits * qv[...] * inv_root
    wide_share = share + jnp.zeros_like(ds)
    shares[...] = jnp.where(first, wide_share, jnp.concatenate([wide_share[rows:], wide_share[:rows]], axis=0))
    dsum[...] = jnp.where(first, ds, jnp.concatenate([ds[rows:], ds[:rows]], axis=0))


def share_out(summ, prod, qv):
    rows = summ.shape[0]
    shape = jax.ShapeDtypeStruct
    return pl.pallas_call(
        shares_kernel,
        out_shape=(shape((2 * rows, PROJ), F32), shape((2 * rows, PROJ), F32), shape((1, PROJ), F32)),
        in_specs=vmem_spec(3),
        out_specs=tuple(vmem_spec(3)),
        scratch_shapes=[
            pltpu.VMEM((2 * rows, PROJ), F32), pltpu.VMEM((2 * rows, PROJ), F32),
            pltpu.SemaphoreType.DMA, pltpu.SemaphoreType.DMA,
        ],
        compiler_params=pltpu.CompilerParams(collective_id=1, has_side_effects=True),
        name="shares",
    )(summ, prod, qv)


def norm_back(upstream, normed, inverse, gain):
    scaled = upstream * gain
    first = jnp.mean(scaled, axis=-1, keepdims=True)
    second = jnp.mean(scaled * normed, axis=-1, keepdims=True)
    return inverse * (scaled - first - normed * second)


def add_vec(vecs, row, value):
    half = value.shape[1] // 2
    vecs[0, row:row + 1, :] += value[:, :half]
    vecs[1, row:row + 1, :] += value[:, half:]


def token_sum(values):
    return jnp.sum(values, axis=0, keepdims=True)


def backward_kernel(
    shares, dsum, cot, res, nout, iout, slope, nmid, imid, qkv, lse, seg_col, seg_row,
    wqkv, wo, wi, wu, wc, vec,
    douter, dinner, dattn, dqkv, dstart, mixed, vecs,
    bias, grads, acc,
):
    b = pl.program_id(0)
    seq, full = cot.shape
    half = full // 2
    hidden = wi.shape[1]

    @pl.when(b == 0)
    def _():
        mixed[...] = jnp.zeros_like(mixed)
        vecs[...] = jnp.zeros_like(vecs)

    share = shares[pl.ds(b, 1), 0:1]
    mixed[...] += share * res[0].astype(F32)
    extra = lax.dot_general(
        jnp.broadcast_to(dsum[pl.ds(b, 1), :], (8, PROJ)), wc[...].astype(F32), (((1,), (1,)), ((), ())),
        preferred_element_type=F32, precision=PRECISE,
    )[0:1]
    row = lax.broadcasted_iota(jnp.int32, (seq, 1), 0)
    upstream = share * cot[...].astype(F32) + jnp.where(row == 0, extra, 0.0)
    upstream = upstream.astype(BF).astype(F32)
    normed = nout[0].astype(F32)
    dout = norm_back(upstream, normed, iout[0], wide(vec, VGF))
    add_vec(vecs, VGF, token_sum(upstream * normed))
    add_vec(vecs, VSF, token_sum(upstream))
    add_vec(vecs, VBO, token_sum(dout))
    douter[0] = dout.astype(BF)
    acc[...] = dout
    chunk = hidden // 4
    for j in range(4):
        cols = slice(j * chunk, (j + 1) * chunk)
        part = nt(douter[0], wu[cols, :]) * slope[0, :, cols].astype(F32)
        dinner[0, :, cols] = part.astype(BF)
        sums = token_sum(part)
        for i in range(2):
            quarter = 2 * j + i
            vecs[quarter // 4, VIN + quarter % 4:VIN + quarter % 4 + 1, :] += sums[:, i * half:(i + 1) * half]
        acc[...] += nt(dinner[0, :, cols], wi[:, cols])
    upstream = acc[...]
    normed = nmid[0].astype(F32)
    dmid = norm_back(upstream, normed, imid[0], wide(vec, VGA))
    add_vec(vecs, VGA, token_sum(upstream * normed))
    add_vec(vecs, VSA, token_sum(upstream))
    add_vec(vecs, VO, token_sum(dmid))
    dattn[0] = dmid.astype(BF)
    acc[...] = dmid
    grads[:, 0:full] = nt(dattn[0], wo[...]).astype(BF)
    bias[...] = jnp.where(seg_col[0] == seg_row[0], 0.0, NEGATIVE)
    masks = head_masks()
    pair = 2 * HEAD_DIM
    per_half = half // pair

    def heads(p, carry):
        at = pl.multiple_of(p * pair, pair)
        out_at = pl.multiple_of((p // per_half) * (3 * half) + (p % per_half) * pair, pair)
        queries = qkv[0, :, pl.ds(at, pair)]
        keys = qkv[0, :, pl.ds(full + at, pair)]
        values = qkv[0, :, pl.ds(2 * full + at, pair)]
        dctx = grads[:, pl.ds(at, pair)]
        lane = lax.broadcasted_iota(jnp.int32, (seq, pair), 1)
        parts = []
        for h in range(2):
            s = nt(keys * masks[h], queries) + bias[...]
            w = jnp.exp(s - lse[0, pl.ds(2 * p + h, 1), :])
            dv = mm(w.astype(BF), dctx)
            prod = w * nt(values * masks[h], dctx)
            ds = (prod - w * token_sum(prod)).astype(BF)
            dk = mm(ds, queries)
            dq = tn(ds, keys) * HEAD_DIM ** -0.5
            parts.append((dq, dk, dv))
        for t in range(3):
            joined = jnp.where(lane < HEAD_DIM, parts[0][t], parts[1][t]).astype(BF)
            dqkv[0, :, pl.ds(out_at + t * half, pair)] = joined
        return carry

    lax.fori_loop(0, full // pair, heads, 0)
    total = acc[...]
    for h in range(2):
        for t in range(3):
            source = dqkv[0, :, (3 * h + t) * half:(3 * h + t + 1) * half]
            total += nt(source, wqkv[:, t * full + h * half:t * full + (h + 1) * half])
            if t != 1:
                at = VQ if t == 0 else VV
                vecs[h, at:at + 1, :] += token_sum(source.astype(F32))
    dstart[0] = total.astype(BF)


def backward(shares, dsum, cot, res, nout, iout, slope, nmid, imid, qkv, lse, seg_col, seg_row, wqkv, wo, wi, wu, wc, vec):
    rows, seq, full = res.shape
    hidden = wi.shape[1]
    shape = jax.ShapeDtypeStruct

    def row_block(array):
        dims = array.shape[1:]
        return pl.BlockSpec((1,) + dims, lambda b: (b,) + (0,) * len(dims))

    def whole(array):
        dims = array.shape
        return pl.BlockSpec(dims, lambda b: (0,) * len(dims), pipeline_mode=pl.Buffered(1))

    outs = (
        shape((rows, seq, full), BF), shape((rows, seq, hidden), BF), shape((rows, seq, full), BF),
        shape((rows, seq, 3 * full), BF), shape((rows, seq, full), BF),
    )
    sums = (shape((seq, full), F32), shape((2, VROWS, full // 2), F32))
    by_row = (res, nout, iout, slope, nmid, imid, qkv, lse, seg_col, seg_row)
    fixed = (wqkv, wo, wi, wu, wc, vec)
    return pl.pallas_call(
        backward_kernel,
        out_shape=outs + sums,
        grid=(rows,),
        in_specs=[whole(shares), whole(dsum), whole(cot)] + [row_block(a) for a in by_row] + [whole(a) for a in fixed],
        out_specs=tuple([row_block(a) for a in outs] + [whole(a) for a in sums]),
        scratch_shapes=[
            pltpu.VMEM((seq, seq), F32), pltpu.VMEM((seq, full), BF), pltpu.VMEM((seq, full), F32),
        ],
        compiler_params=pltpu.CompilerParams(vmem_limit_bytes=VMEM_LIMIT),
        name="backward",
    )(shares, dsum, cot, *by_row, *fixed)


def with_bit(index, position, bit):
    low = 1 << position
    return (index // low) * (2 * low) + bit * low + index % low


def reduce_kernel(n, groups, mats, *refs):
    refs = list(refs)

    def take(count):
        taken = refs[:count]
        del refs[:count]
        return taken

    slot_row, vec_in, mixed_in, dstart = take(4)
    grads_in = take(mats)
    gt, arrived, mixed, vec_out = take(4)
    grads_out = take(mats)
    gt_v, stage, mix_own, mix_got, vec_bufs = take(5)
    levels = n.bit_length() - 1
    bufs = [take(2 + 3 * levels) for _ in groups]
    (own_sem, sib_send, sib_recv, doc_send, doc_recv, vec_send, vec_recv, m_sem, m_send, m_recv, x_send, x_recv) = take(12)
    me = lax.axis_index("dp")
    core = lax.axis_index("mp")
    other = 1 - core
    sibling = (me, other)

    def across(bit):
        here = (me // (1 << bit)) % 2
        return here, (me + (1 - 2 * here) * (1 << bit), core)

    far = [across(bit)[1] for bit in range(levels) if (1 << bit) > REACH]
    greet(ring_partners(me, core, n) + [sibling] + (far if mats else []))
    rows, seq, full = dstart.shape
    half = full // 2
    here_cols = pl.ds(pl.multiple_of(core * half, half), half)
    there_cols = pl.ds(pl.multiple_of(other * half, half), half)
    my_rows = pl.ds(core * rows, rows)

    tok_far = pltpu.make_async_remote_copy(
        src_ref=dstart.at[:, :, there_cols], dst_ref=gt_v.at[my_rows], send_sem=sib_send.at[0],
        recv_sem=sib_recv.at[0], device_id=sibling, device_id_type=MESH,
    )
    tok_far.start()
    tok_own = pltpu.make_async_copy(dstart.at[:, :, here_cols], gt_v.at[my_rows], own_sem.at[0])
    tok_own.start()
    mix_far = pltpu.make_async_remote_copy(
        src_ref=mixed_in.at[:, there_cols], dst_ref=mix_got, send_sem=sib_send.at[1],
        recv_sem=sib_recv.at[1], device_id=sibling, device_id_type=MESH,
    )
    mix_far.start()
    mix_load = pltpu.make_async_copy(mixed_in.at[:, here_cols], mix_own, own_sem.at[1])
    mix_load.start()
    vec_copy = pltpu.make_async_remote_copy(
        src_ref=vec_in.at[other], dst_ref=vec_bufs.at[0], send_sem=vec_send.at[0],
        recv_sem=vec_recv.at[0], device_id=sibling, device_id_type=MESH,
    )
    vec_copy.start()

    first = []
    for g, (mat, begin, width, _) in enumerate(groups):
        half_width = grads_in[mat].shape[2] // 2
        mine, theirs = bufs[g][0], bufs[g][1]
        there = pl.ds(pl.multiple_of(other * half_width + begin, 128), width)
        here = pl.ds(pl.multiple_of(core * half_width + begin, 128), width)
        send = pltpu.make_async_remote_copy(
            src_ref=grads_in[mat].at[:, :, there], dst_ref=theirs, send_sem=m_send.at[g],
            recv_sem=m_recv.at[g], device_id=sibling, device_id_type=MESH,
        )
        send.start()
        load = pltpu.make_async_copy(grads_in[mat].at[:, :, here], mine, m_sem.at[g])
        load.start()
        first.append((send, load))

    tok_own.wait()
    tok_far.wait()
    tok_out = pltpu.make_async_copy(gt_v, gt, own_sem.at[2])
    tok_out.start()
    sent = []
    order = sorted(range(SLOTS), key=lambda s: -abs(s - REACH))
    for slot in order:
        stage[slot] = gt_v[slot_row[slot]]
        if slot == REACH:
            copy = pltpu.make_async_copy(stage.at[slot], arrived.at[slot], own_sem.at[3])
        else:
            copy = pltpu.make_async_remote_copy(
                src_ref=stage.at[slot], dst_ref=arrived.at[slot], send_sem=doc_send.at[slot],
                recv_sem=doc_recv.at[slot],
                device_id=(lax.rem(me + slot - REACH + n, n), core), device_id_type=MESH,
            )
        copy.start()
        sent.append(copy)

    pending = [None] * len(groups)
    vec_total = None
    for level in range(levels + 1):
        for g, (mat, begin, width, bits) in enumerate(groups):
            base = bufs[g]
            if level == 0:
                for copy in first[g]:
                    copy.wait()
                held, came = base[0], base[1]
            else:
                pending[g].wait()
                held, came = base[2 + 3 * (level - 1) + 1], base[2 + 3 * (level - 1) + 2]
            if level == levels:
                grads_out[mat][:, begin:begin + width] = held[0].astype(F32) + came[0].astype(F32)
                continue
            to_send, to_keep, to_get = base[2 + 3 * level:5 + 3 * level]
            bit = bits[level]
            place = sum(1 for earlier in range(bit) if earlier not in bits[:level])
            here, partner = across(bit)

            def add(t, carry, held=held, came=came, to_send=to_send, to_keep=to_keep, place=place, here=here):
                gone = with_bit(t, place, 1 - here)
                kept = with_bit(t, place, here)
                to_send[t] = (held[gone].astype(F32) + came[gone].astype(F32)).astype(BF)
                to_keep[t] = (held[kept].astype(F32) + came[kept].astype(F32)).astype(BF)
                return carry

            lax.fori_loop(0, n >> (level + 1), add, 0)
            pending[g] = pltpu.make_async_remote_copy(
                src_ref=to_send, dst_ref=to_get, send_sem=x_send.at[g, level], recv_sem=x_recv.at[g, level],
                device_id=partner, device_id_type=MESH,
            )
            pending[g].start()
        if mats:
            vec_copy.wait()
            if level == 0:
                vec_total = vec_in[core] + vec_bufs[0]
            else:
                vec_total = vec_total + vec_bufs[2 * level]
            if level < levels:
                vec_bufs[2 * level + 1] = vec_total
                vec_copy = pltpu.make_async_remote_copy(
                    src_ref=vec_bufs.at[2 * level + 1], dst_ref=vec_bufs.at[2 * level + 2],
                    send_sem=vec_send.at[level + 1], recv_sem=vec_recv.at[level + 1],
                    device_id=across(level)[1], device_id_type=MESH,
                )
                vec_copy.start()
            else:
                vec_out[...] = vec_total
    if not mats:
        vec_copy.wait()
        vec_out[...] = vec_in[core] + vec_bufs[0]
    mix_load.wait()
    mix_far.wait()
    mixed[...] = (mix_own[...] + mix_got[...]).astype(BF)
    tok_out.wait()
    for copy in sent:
        copy.wait()


def deliver(n, groups, slot_row, vecs, mixed, dstart, grads):
    rows, seq, full = dstart.shape
    half = full // 2
    levels = n.bit_length() - 1
    shape = jax.ShapeDtypeStruct
    outs = [
        shape((2 * rows, seq, half), BF), shape((SLOTS, seq, half), BF), shape((seq, half), BF),
        shape(vecs.shape[1:], F32),
    ] + [shape((g.shape[1], g.shape[2] // 2), F32) for g in grads]
    scratch = [
        pltpu.VMEM((2 * rows, seq, half), BF), pltpu.VMEM((SLOTS, seq, half), BF),
        pltpu.VMEM((seq, half), F32), pltpu.VMEM((seq, half), F32),
        pltpu.VMEM((2 * levels + 2,) + vecs.shape[1:], F32),
    ]
    for mat, _, width, _ in groups:
        depth = grads[mat].shape[1]
        scratch += [pltpu.VMEM((n, depth, width), BF)] * 2
        for level in range(levels):
            scratch += [pltpu.VMEM((n >> (level + 1), depth, width), BF)] * 3
    dma = pltpu.SemaphoreType.DMA
    count = max(1, len(groups))
    scratch += [
        dma((4,)), dma((2,)), dma((2,)), dma((SLOTS,)), dma((SLOTS,)), dma((levels + 1,)), dma((levels + 1,)),
        dma((count,)), dma((count,)), dma((count,)), dma((count, levels)), dma((count, levels)),
    ]
    return pl.pallas_call(
        functools.partial(reduce_kernel, n, groups, len(grads)),
        out_shape=tuple(outs),
        in_specs=[pl.BlockSpec(memory_space=pltpu.SMEM)] + vmem_spec(1) + any_spec(2 + len(grads)),
        out_specs=tuple(any_spec(2) + vmem_spec(2 + len(grads))),
        scratch_shapes=scratch,
        compiler_params=pltpu.CompilerParams(
            collective_id=2, has_side_effects=True, vmem_limit_bytes=VMEM_LIMIT
        ),
        name="deliver",
    )(slot_row, vecs, mixed, dstart, *grads)


def place_kernel(want, arrived, out):
    d = pl.program_id(0)
    out[...] = jnp.zeros_like(out)
    for slot in range(SLOTS):

        @pl.when(want[slot] == d)
        def _(slot=slot):
            out[0] += arrived[slot].astype(F32)


def place_docs(want, arrived, docs):
    _, seq, half = arrived.shape
    return pl.pallas_call(
        place_kernel,
        out_shape=jax.ShapeDtypeStruct((docs, seq, half), F32),
        grid_spec=pltpu.PrefetchScalarGridSpec(
            num_scalar_prefetch=1,
            grid=(docs,),
            in_specs=[pl.BlockSpec(arrived.shape, lambda d, w: (0, 0, 0), pipeline_mode=pl.Buffered(1))],
            out_specs=pl.BlockSpec((1, seq, half), lambda d, w: (d, 0, 0)),
        ),
        compiler_params=pltpu.CompilerParams(vmem_limit_bytes=VMEM_LIMIT),
        name="place_docs",
    )(want, arrived)


def cut_groups(widths, levels):
    plain = tuple(range(levels))
    swapped = (1, 0) + plain[2:]
    groups = []
    for mat, width in enumerate(widths):
        begin = 0
        while begin < width:
            size = min(768, width - begin)
            groups.append((mat, begin, size, plain if len(groups) % 2 == 0 else swapped))
            begin += size
    return tuple(groups)


def body(
    tokens, segment_ids, positions, query_vectors, doc_owner, doc_slot, doc_store, pos_table,
    w_query, w_key, w_value, b_query, b_value, w_out, b_out, gain_attn, shift_attn,
    w_inner, b_inner, w_outer, b_outer, gain_ffn, shift_ffn, w_cls, cotangent,
):
    n = lax.axis_size("dp")
    me = lax.axis_index("dp")
    core = lax.axis_index("mp")
    row_count, seq, half = tokens.shape
    rows = row_count // 2
    full = 2 * half
    doc_count = doc_store.shape[0]
    place_slot = (doc_owner[0] - me + REACH) % n
    match = (place_slot[None, :] == jnp.arange(SLOTS, dtype=jnp.int32)[:, None]).astype(jnp.int32)
    req = jnp.sum(match * (doc_slot[0] + 1)[None, :], axis=1) - 1
    slot_row = jnp.sum(match * jnp.arange(row_count, dtype=jnp.int32)[None, :], axis=1)
    req = jnp.broadcast_to(req[:, None, None], (SLOTS, 8, 128))
    vec_in = jnp.concatenate(
        [v.reshape(-1, half) for v in (b_query, b_value, b_out, gain_attn, shift_attn, b_outer, gain_ffn, shift_ffn, b_inner)]
        + [jnp.zeros((VROWS - 12, half), F32)], axis=0,
    )
    docs, tok, cot, wqkv, wo, wi, wu, wc, pos, vec, got = fetch(
        n, req, doc_store, tokens, cotangent, w_query, w_key, w_value, w_out, w_inner, w_outer, w_cls, pos_table, vec_in
    )
    want = got[:, 0, 0]
    seg = lax.dynamic_slice_in_dim(segment_ids, core * rows, rows, 0)
    place = lax.dynamic_slice_in_dim(positions, core * rows, rows, 0)
    my_slots = lax.dynamic_slice_in_dim(place_slot, core * rows, rows, 0)
    seg_col, seg_row = seg[:, :, None], seg[:, None, :]
    xlow, qkv, lse, ctx, nmid, imid, mlow, act, slope, nout, iout, res, summ, prod = forward(
        my_slots, tok, docs, place[:, :, None], seg_col, seg_row, pos, wqkv, wo, wi, wu, wc, vec, cot
    )
    shares, dsum, grad_query = share_out(summ, prod, query_vectors)
    douter, dinner, dattn, dqkv, dstart, mixed, vecs = backward(
        shares, dsum, cot, res, nout, iout, slope, nmid, imid, qkv, lse, seg_col, seg_row, wqkv, wo, wi, wu, wc, vec
    )

    def cross(left, right):
        left = left.reshape(-1, left.shape[-1])
        right = right.reshape(-1, right.shape[-1])
        return tn(left, right)

    one_hot = (place.reshape(-1)[:, None] == jnp.arange(pos_table.shape[0], dtype=jnp.int32)[None, :]).astype(BF)
    dw_cls = lax.dot_general(
        dsum[:rows], res[:, 0, :].astype(F32), (((0,), (0,)), ((), ())), preferred_element_type=F32, precision=PRECISE
    )
    dpos = cross(one_hot, dstart)
    pieces = [cross(douter, act), cross(mlow, dinner), cross(dattn, ctx), cross(xlow, dqkv)]
    if full // n % 16 == 0:
        small = jnp.concatenate(
            [dw_cls.reshape(n, -1, full), dpos.reshape(n, -1, full)], axis=1
        )
        small = jnp.pad(small, ((0, 0), (0, full // n - small.shape[1]), (0, 0)))
        grads = [p.astype(BF).reshape(n, full // n, -1) for p in pieces] + [small.astype(BF)]
        groups = cut_groups([g.shape[2] // 2 for g in grads], n.bit_length() - 1)
        out = deliver(n, groups, slot_row, vecs, mixed, dstart, grads)
        grad_tokens, arrived, mixed_out, vec_sum = out[:4]
        g_outer, g_inner, g_wo, g_qkv, g_small = out[4:]
        g_cls = g_small[:PROJ // n]
        g_pos = g_small[PROJ // n:(PROJ + pos_table.shape[0]) // n]
    else:
        grad_tokens, arrived, mixed_out, vec_sum = deliver(n, (), slot_row, vecs, mixed, dstart, [])
        vec_sum = lax.psum(vec_sum, "dp")

        def scatter(part):
            part = lax.psum_scatter(part.astype(F32), "mp", scatter_dimension=1, tiled=True)
            return lax.psum_scatter(part, "dp", scatter_dimension=0, tiled=True)

        g_outer, g_inner, g_wo, g_qkv, g_cls, g_pos = [scatter(p) for p in pieces + [dw_cls, dpos]]
    grad_docs = place_docs(want, arrived, doc_count)

    def row(index):
        return vec_sum[index]

    return (
        mixed_out[None],
        grad_tokens,
        grad_query,
        grad_docs,
        g_pos,
        g_qkv[:, :half],
        g_qkv[:, half:2 * half],
        g_qkv[:, 2 * half:],
        row(VQ),
        row(VV),
        g_wo.T,
        row(VO),
        row(VGA),
        row(VSA),
        g_inner,
        vec_sum[VIN:VIN + 4].reshape(-1),
        g_outer.T,
        row(VBO),
        row(VGF),
        row(VSF),
        g_cls.T,
    )


def solution(mesh):
    rows = P("dp", None, "mp")
    ids = P("dp", None)
    cols = P(None, "mp")
    vec = P("mp")
    deep = P("mp", None)
    in_specs = (
        rows, ids, ids, ids, ids, ids, rows, cols, cols, cols, cols, vec, vec, deep, vec, vec, vec,
        cols, vec, deep, vec, vec, vec, deep, rows,
    )
    near = P("dp", "mp")
    turned = P("mp", "dp")
    out_specs = (
        rows, rows, ids, rows, near, near, near, near, vec, vec, turned, vec, vec, vec, near, vec,
        turned, vec, vec, vec, turned,
    )
    return jax.shard_map(body, mesh=mesh, in_specs=in_specs, out_specs=out_specs, check_vma=False)
```

```python
import functools

import jax
import jax.numpy as jnp
from jax import lax
from jax.experimental import pallas as pl
from jax.experimental.pallas import tpu as pltpu
from jax.sharding import PartitionSpec as P

HEAD_DIM = 64
PROJ = 128
REACH = 6
SLOTS = 2 * REACH
EPSILON = 1e-05
NEGATIVE = -1e30
PRECISE = lax.Precision.HIGHEST
MESH = pl.DeviceIdType.MESH
BF = jnp.bfloat16
F32 = jnp.float32
VMEM_LIMIT = 60 * 1024 * 1024
VQ, VV, VO, VGA, VSA, VBO, VGF, VSF, VIN = range(9)
VROWS = 16
GANG = 2


def any_spec(count):
    return [pl.BlockSpec(memory_space=pl.ANY)] * count


def vmem_spec(count):
    return [pl.BlockSpec(memory_space=pltpu.VMEM)] * count


def nt(left, right):
    return lax.dot_general(left, right, (((1,), (1,)), ((), ())), preferred_element_type=F32)


def tn(left, right):
    return lax.dot_general(left, right, (((0,), (0,)), ((), ())), preferred_element_type=F32)


def mm(left, right):
    return jnp.dot(left, right, preferred_element_type=F32)


def greet(targets):
    barrier = pltpu.get_barrier_semaphore()
    for target in targets:
        pl.semaphore_signal(barrier, inc=1, device_id=target, device_id_type=MESH)
    pl.semaphore_wait(barrier, len(targets))


def ring_partners(me, core, n):
    return [(lax.rem(me + step + n, n), core) for step in range(-REACH, REACH + 1) if step != 0]


def fetch_kernel(
    n, req, docs_in, tok_in, cot_in, wq_in, wk_in, wv_in, wo_in, wi_in, wu_in, wc_in, pos_in, vec_in,
    docs, docs_sib, tok, cot, pos, vec, wq, wk, wv, wo, wi, wu, wc, got,
    doc_buf, stage, got_s,
    req_send, req_recv, doc_send, doc_recv, fwd_send, fwd_recv, sib_send, sib_recv, misc_sem,
):
    me = lax.axis_index("dp")
    core = lax.axis_index("mp")
    other = 1 - core
    sibling = (me, other)
    greet(ring_partners(me, core, n) + [sibling])
    rows = tok_in.shape[0] // 2
    asked = []
    for slot in range(SLOTS):
        if slot == REACH:
            asked.append(None)
            continue
        copy = pltpu.make_async_remote_copy(
            src_ref=req.at[slot], dst_ref=got.at[slot], send_sem=req_send.at[slot],
            recv_sem=req_recv.at[slot],
            device_id=(lax.rem(me + slot - REACH + n, n), core), device_id_type=MESH,
        )
        copy.start()
        asked.append(copy)
    load = pltpu.make_async_copy(docs_in, doc_buf, misc_sem.at[0])
    load.start()
    pairs = [
        (tok_in.at[pl.ds(other * rows, rows)], tok), (cot_in.at[0], cot), (pos_in, pos), (vec_in, vec),
        (wq_in, wq), (wk_in, wk), (wv_in, wv), (wo_in, wo), (wi_in, wi), (wu_in, wu), (wc_in, wc),
    ]
    moves = []
    for index, (src, dst) in enumerate(pairs):
        far = pltpu.make_async_remote_copy(
            src_ref=src, dst_ref=dst, send_sem=sib_send.at[index], recv_sem=sib_recv.at[index],
            device_id=sibling, device_id_type=MESH,
        )
        far.start()
        moves.append(far)
    got[REACH] = req[REACH]
    for copy in asked:
        if copy is not None:
            copy.wait_recv()
    to_scalar = pltpu.make_async_copy(got, got_s, misc_sem.at[1])
    to_scalar.start()
    load.wait()
    to_scalar.wait()
    sent = [None] * SLOTS
    order = sorted(range(SLOTS), key=lambda s: -abs(s - REACH))
    for slot in order:
        stage[slot] = doc_buf[jnp.maximum(got_s[slot, 0, 0], 0)]
        if slot == REACH:
            copy = pltpu.make_async_copy(stage.at[slot], docs.at[slot], misc_sem.at[2])
        else:
            copy = pltpu.make_async_remote_copy(
                src_ref=stage.at[slot], dst_ref=docs.at[slot], send_sem=doc_send.at[slot],
                recv_sem=doc_recv.at[slot],
                device_id=(lax.rem(me - slot + REACH + n, n), core), device_id_type=MESH,
            )
        copy.start()
        sent[slot] = copy
    passed = []
    for slot in reversed(order):
        if slot == REACH:
            sent[slot].wait()
        else:
            sent[slot].wait_recv()
        copy = pltpu.make_async_remote_copy(
            src_ref=docs.at[slot], dst_ref=docs_sib.at[slot], send_sem=fwd_send.at[slot],
            recv_sem=fwd_recv.at[slot], device_id=sibling, device_id_type=MESH,
        )
        copy.start()
        passed.append(copy)
    for copy in moves + passed:
        copy.wait()
    for slot in range(SLOTS):
        if slot != REACH:
            asked[slot].wait_send()
            sent[slot].wait_send()


def fetch(n, req, doc_store, tokens, cot, *fixed):
    rows, seq, half = tokens.shape
    shape = jax.ShapeDtypeStruct
    out_shape = (
        shape((SLOTS, seq, half), BF),
        shape((SLOTS, seq, half), BF),
        shape((rows // 2, seq, half), BF),
        shape((seq, half), BF),
    ) + tuple(shape(f.shape, f.dtype) for f in (fixed[-2:] + fixed[:-2])) + (shape(req.shape, jnp.int32),)
    dma = pltpu.SemaphoreType.DMA
    return pl.pallas_call(
        functools.partial(fetch_kernel, n),
        out_shape=out_shape,
        in_specs=vmem_spec(1) + any_spec(12),
        out_specs=tuple(any_spec(13) + vmem_spec(1)),
        scratch_shapes=[
            pltpu.VMEM(doc_store.shape, BF),
            pltpu.VMEM((SLOTS, seq, half), BF),
            pltpu.SMEM(req.shape, jnp.int32),
            dma((SLOTS,)), dma((SLOTS,)), dma((SLOTS,)), dma((SLOTS,)), dma((SLOTS,)), dma((SLOTS,)),
            dma((11,)), dma((11,)), dma((3,)),
        ],
        compiler_params=pltpu.CompilerParams(
            collective_id=0, has_side_effects=True, vmem_limit_bytes=VMEM_LIMIT
        ),
        name="fetch",
    )(req, doc_store, tokens, cot, *fixed)


class Halves:
    def __init__(self, sems):
        self.sems, self.copies, self.names = sems, [], {}

    def add(self, name, own, theirs, whole, axis, offset=0):
        core = lax.axis_index("mp")
        size = own.shape[axis] if axis is not None else 1
        for source, side in ((own, core), (theirs, 1 - core)):
            if axis is None:
                target = whole.at[side]
            else:
                begin = offset + side * size
                at = pl.ds(pl.multiple_of(begin, 128), size)
                target = whole.at[at] if axis == 0 else whole.at[:, at]
            copy = pltpu.make_async_copy(source, target, self.sems.at[len(self.copies)])
            self.copies.append(copy)
            self.names.setdefault(name, []).append(copy)

    def start(self):
        for copy in self.copies:
            copy.start()

    def wait(self, name):
        for copy in self.names[name]:
            copy.wait()


def wide(vec, row):
    return jnp.concatenate([vec[0, row:row + 1, :], vec[1, row:row + 1, :]], axis=1)


def inner_bias(vec):
    return jnp.concatenate([vec[h, VIN + j:VIN + j + 1, :] for h in range(2) for j in range(4)], axis=1)


def normalize(hidden):
    average = jnp.mean(hidden, axis=-1, keepdims=True)
    centered = hidden - average
    spread = jnp.mean(centered * centered, axis=-1, keepdims=True)
    inverse = lax.rsqrt(spread + EPSILON)
    return centered * inverse, inverse


def head_masks(count):
    lane = lax.broadcasted_iota(jnp.int32, (1, count * HEAD_DIM), 1) // HEAD_DIM
    return [(lane == h).astype(F32).astype(BF) for h in range(count)]


def spread_halves(halves, own, theirs, **whole):
    places = {"cot": (0, 1), "pos": (1, 1), "vec": (2, None), "wo": (6, 0), "wi": (7, 1), "wu": (8, 0), "wc": (9, 0)}
    for name, ref in whole.items():
        if name == "wqkv":
            for index in range(3):
                halves.add("qkv", own[3 + index], theirs[3 + index], ref, 1, index * ref.shape[0])
        else:
            at, axis = places[name]
            halves.add(name, own[at], theirs[at], ref, axis)


def whole_scratch(own, *names):
    cot, pos, vec, wq, _, _, wo, wi, wu, wc = own
    full = wq.shape[0]
    shapes = {
        "cot": ((cot.shape[0], full), BF), "pos": ((pos.shape[0], full), BF), "vec": ((2,) + vec.shape, F32),
        "wqkv": ((full, 3 * full), BF), "wo": ((full, full), BF), "wi": ((full, 2 * wi.shape[1]), BF),
        "wu": ((2 * wu.shape[0], full), BF), "wc": ((full, wc.shape[1]), BF),
    }
    return [pltpu.VMEM(*shapes[name]) for name in names] + [pltpu.SemaphoreType.DMA((20,))]


def forward_kernel(
    slot_ref, tok, tok_sib, doc, doc_sib, place, seg_col, seg_row, *refs
):
    own, theirs = refs[:10], refs[10:20]
    xlow, qkv, lse, ctx, nmid, imid, mlow, act, slope, nout, iout, res, summ, prod = refs[20:34]
    bias, stats, acc, cot, pos, vec, wqkv, wo, wi, wu, wc, sems = refs[34:]
    seq, full = acc.shape
    halves = Halves(sems)
    spread_halves(halves, own, theirs, pos=pos, vec=vec, wqkv=wqkv, wo=wo, wi=wi, wu=wu, wc=wc, cot=cot)
    fresh = pl.program_id(0) == 0

    def need(*names):
        @pl.when(fresh)
        def _():
            for name in names:
                halves.wait(name)

    @pl.when(fresh)
    def _():
        halves.start()

    first = lax.axis_index("mp") == 0

    def join(a, b):
        a, b = a.astype(F32), b.astype(F32)
        return jnp.concatenate([jnp.where(first, a, b), jnp.where(first, b, a)], axis=1)

    need("pos", "vec")
    table = pos.shape[0]
    one_hot = (place[0] == lax.broadcasted_iota(jnp.int32, (seq, table), 1)).astype(F32).astype(BF)
    embedded = join(tok[0], tok_sib[0]) + mm(one_hot, pos[...]) + join(doc[0], doc_sib[0])
    low = embedded.astype(BF)
    xlow[0] = low
    acc[...] = embedded
    need("qkv")
    q = (mm(low, wqkv[:, 0:full]) + wide(vec, VQ)).astype(BF)
    qkv[0, :, 0:full] = q * jnp.asarray(HEAD_DIM ** -0.5, BF)
    qkv[0, :, full:2 * full] = mm(low, wqkv[:, full:2 * full]).astype(BF)
    qkv[0, :, 2 * full:] = (mm(low, wqkv[:, 2 * full:]) + wide(vec, VV)).astype(BF)
    bias[...] = jnp.where(seg_col[0] == seg_row[0], 0.0, NEGATIVE)
    stats[...] = jnp.zeros_like(stats)
    masks = head_masks(GANG)
    wide_gang = GANG * HEAD_DIM

    def heads(p, carry):
        at = pl.multiple_of(p * wide_gang, wide_gang)
        queries = qkv[0, :, pl.ds(at, wide_gang)]
        keys = qkv[0, :, pl.ds(full + at, wide_gang)]
        values = qkv[0, :, pl.ds(2 * full + at, wide_gang)]
        lane = lax.broadcasted_iota(jnp.int32, (seq, wide_gang), 1)
        small_lane = lax.broadcasted_iota(jnp.int32, (seq, 128), 1)
        s = nt(jnp.concatenate([queries * m for m in masks], axis=0), keys)
        es, totals = [], []
        for h in range(GANG):
            sh = s[h * seq:(h + 1) * seq] + bias[...]
            top = jnp.max(sh, axis=1, keepdims=True)
            e = jnp.exp(sh - top)
            total = jnp.sum(e, axis=1, keepdims=True)
            es.append(e.astype(BF))
            totals.append(1.0 / total)
            stats[0:seq, :] = jnp.where(small_lane == GANG * p + h, top + jnp.log(total), stats[0:seq, :])
        out = mm(jnp.concatenate(es, axis=0), values)
        joined = out[0:seq] * totals[0]
        for h in range(1, GANG):
            joined = jnp.where(lane < h * HEAD_DIM, joined, out[h * seq:(h + 1) * seq] * totals[h])
        ctx[0, :, pl.ds(at, wide_gang)] = joined.astype(BF)
        return carry

    lax.fori_loop(0, full // wide_gang, heads, 0, unroll=3)
    lse[0] = jnp.transpose(stats[...])[0:lse.shape[1], 0:seq]
    need("wo")
    normed, inverse = normalize(acc[...] + mm(ctx[0], wo[...]) + wide(vec, VO))
    middle = normed * wide(vec, VGA) + wide(vec, VSA)
    nmid[0] = normed.astype(BF)
    imid[0] = inverse
    acc[...] = middle + wide(vec, VBO)
    mlow[0] = middle.astype(BF)
    need("wi", "wu", "wc", "cot")
    hidden = wi.shape[1]
    chunk = hidden // 4
    bin_all = inner_bias(vec)
    for j in range(4):
        cols = slice(j * chunk, (j + 1) * chunk)
        pre = mm(mlow[0], wi[:, cols]) + bin_all[:, cols]
        phi = 0.5 + 0.5 * lax.erf(pre * (0.5 ** 0.5))
        act[0, :, cols] = (pre * phi).astype(BF)
        slope[0, :, cols] = (phi + pre * (jnp.exp(-0.5 * pre * pre) * 0.3989422804014327)).astype(BF)
        acc[...] += mm(act[0, :, cols], wu[cols, :])
    normed, inverse = normalize(acc[...])
    nout[0] = normed.astype(BF)
    iout[0] = inverse
    result = (normed * wide(vec, VGF) + wide(vec, VSF)).astype(BF)
    res[0] = result
    summ[0] = mm(res[0, 0:16, :], wc[...])[0:8]
    product = jnp.sum(cot[...].astype(F32) * result.astype(F32))
    prod[0] = jnp.full(prod.shape[1:], product, F32)


def forward(slots, tokens, tok_sib, docs, docs_sib, place, seg_col, seg_row, own, theirs):
    rows, seq, half = tok_sib.shape
    full = 2 * half
    hidden = 2 * own[7].shape[1]
    shape = jax.ShapeDtypeStruct
    heads = full // HEAD_DIM
    lse_rows = (heads + 7) // 8 * 8

    def row_block(*dims):
        return pl.BlockSpec((1,) + dims, lambda b, s: (b,) + (0,) * len(dims))

    picked = pl.BlockSpec((1, seq, half), lambda b, s: (s[b], 0, 0))
    outs = [
        ((seq, full), BF), ((seq, 3 * full), BF), ((lse_rows, seq), F32), ((seq, full), BF),
        ((seq, full), BF), ((seq, 1), F32), ((seq, full), BF), ((seq, hidden), BF), ((seq, hidden), BF),
        ((seq, full), BF), ((seq, 1), F32), ((seq, full), BF), ((8, PROJ), F32), ((8, PROJ), F32),
    ]
    return pl.pallas_call(
        forward_kernel,
        out_shape=tuple(shape((rows,) + dims, kind) for dims, kind in outs),
        grid_spec=pltpu.PrefetchScalarGridSpec(
            num_scalar_prefetch=1,
            grid=(rows,),
            in_specs=[
                pl.BlockSpec((1, seq, half), lambda b, s: (s[rows] * rows + b, 0, 0)),
                row_block(seq, half), picked, picked,
                row_block(seq, 1), row_block(seq, 1), row_block(1, seq),
            ] + any_spec(20),
            out_specs=tuple(row_block(*dims) for dims, _ in outs),
            scratch_shapes=[
                pltpu.VMEM((seq, seq), F32), pltpu.VMEM((384, 128), F32), pltpu.VMEM((seq, full), F32),
            ] + whole_scratch(own, "cot", "pos", "vec", "wqkv", "wo", "wi", "wu", "wc"),
        ),
        compiler_params=pltpu.CompilerParams(vmem_limit_bytes=VMEM_LIMIT),
        name="forward",
    )(slots, tokens, tok_sib, docs, docs_sib, place, seg_col, seg_row, *own, *theirs)


def norm_back(upstream, normed, inverse, gain):
    scaled = upstream * gain
    first = jnp.mean(scaled, axis=-1, keepdims=True)
    second = jnp.mean(scaled * normed, axis=-1, keepdims=True)
    return inverse * (scaled - first - normed * second)


def add_vec(vecs, row, value):
    half = value.shape[1] // 2
    vecs[0, row:row + 1, :] += value[:, :half]
    vecs[1, row:row + 1, :] += value[:, half:]


def token_sum(values):
    return jnp.sum(values, axis=0, keepdims=True)


def shares_kernel(summ, prod, qv, iout, nout_in, res_in, *refs):
    own, theirs = refs[:10], refs[10:20]
    douter, mixed, vecs, dw_cls, gq = refs[20:25]
    mine, got, nout, res, cot, vec, wc, halves_sem, send_sem, recv_sem, load_sem = refs[25:]
    me = lax.axis_index("dp")
    core = lax.axis_index("mp")
    sibling = (me, 1 - core)
    rows = summ.shape[0]
    halves = Halves(halves_sem)
    spread_halves(halves, own, theirs, vec=vec, cot=cot, wc=wc)
    halves.start()
    loads = [
        pltpu.make_async_copy(res_in, res, load_sem.at[0]),
        pltpu.make_async_copy(nout_in, nout, load_sem.at[1]),
    ]
    for load in loads:
        load.start()
    greet([sibling])
    mine[...] = jnp.concatenate([summ[b, 0:1, :] for b in range(rows)] + [prod[b, 0:1, :] for b in range(rows)], axis=0)
    copy = pltpu.make_async_remote_copy(
        src_ref=mine, dst_ref=got, send_sem=send_sem, recv_sem=recv_sem,
        device_id=sibling, device_id_type=MESH,
    )
    copy.start()
    vecs[...] = jnp.zeros_like(vecs)
    copy.wait()
    first = core == 0
    low = jnp.where(first, mine[...], got[...])
    high = jnp.where(first, got[...], mine[...])
    summary = jnp.concatenate([low[:rows], high[:rows]], axis=0)
    product = jnp.concatenate([low[rows:], high[rows:]], axis=0)
    inv_root = PROJ ** (-0.5)
    logits = jnp.sum(summary * qv[...], axis=1, keepdims=True) * inv_root
    e = jnp.exp(logits - jnp.max(logits, axis=0, keepdims=True))
    share = e / jnp.sum(e, axis=0, keepdims=True)
    dlogits = share * (product - jnp.sum(share * product, axis=0, keepdims=True))
    gq[...] = jnp.sum(dlogits * summary, axis=0, keepdims=True) * inv_root
    ds = dlogits * qv[...] * inv_root
    wide_share = share + jnp.zeros_like(ds)
    shares = jnp.where(first, wide_share, jnp.concatenate([wide_share[rows:], wide_share[:rows]], axis=0))
    dsum = jnp.where(first, ds, jnp.concatenate([ds[rows:], ds[:rows]], axis=0))
    halves.wait("vec")
    halves.wait("cot")
    halves.wait("wc")
    extra = lax.dot_general(
        dsum, wc[...].astype(F32), (((1,), (1,)), ((), ())), preferred_element_type=F32, precision=PRECISE
    )
    for load in loads:
        load.wait()
    seq, full = cot.shape
    heads = jnp.concatenate([res[b, 0:1, :].astype(F32) for b in range(rows)], axis=0)
    heads = jnp.concatenate([heads, jnp.zeros_like(heads)], axis=0)
    dw_cls[...] = lax.dot_general(dsum, heads, (((0,), (0,)), ((), ())), preferred_element_type=F32, precision=PRECISE)
    row = lax.broadcasted_iota(jnp.int32, (seq, 1), 0)
    for b in range(rows):
        share_b = shares[b:b + 1, 0:1]
        part = share_b * res[b].astype(F32)
        mixed[...] = part if b == 0 else mixed[...] + part
        upstream = share_b * cot[...].astype(F32) + jnp.where(row == 0, extra[b:b + 1], 0.0)
        upstream = upstream.astype(BF).astype(F32)
        normed = nout[b].astype(F32)
        dout = norm_back(upstream, normed, iout[b], wide(vec, VGF))
        add_vec(vecs, VGF, token_sum(upstream * normed))
        add_vec(vecs, VSF, token_sum(upstream))
        add_vec(vecs, VBO, token_sum(dout))
        douter[b] = dout.astype(BF)


def share_out(summ, prod, qv, iout, nout, res, own, theirs):
    rows, seq, full = res.shape
    shape = jax.ShapeDtypeStruct
    return pl.pallas_call(
        shares_kernel,
        out_shape=(
            shape((rows, seq, full), BF), shape((seq, full), F32), shape((2, VROWS, full // 2), F32),
            shape((PROJ, full), F32), shape((1, PROJ), F32),
        ),
        in_specs=vmem_spec(4) + any_spec(22),
        out_specs=tuple(vmem_spec(5)),
        scratch_shapes=[
            pltpu.VMEM((2 * rows, PROJ), F32), pltpu.VMEM((2 * rows, PROJ), F32),
            pltpu.VMEM(nout.shape, BF), pltpu.VMEM(res.shape, BF),
        ] + whole_scratch(own, "cot", "vec", "wc") + [
            pltpu.SemaphoreType.DMA, pltpu.SemaphoreType.DMA, pltpu.SemaphoreType.DMA((2,)),
        ],
        compiler_params=pltpu.CompilerParams(collective_id=1, has_side_effects=True, vmem_limit_bytes=VMEM_LIMIT),
        name="shares",
    )(summ, prod, qv, iout, nout, res, *own, *theirs)


def row_block(array):
    dims = array.shape[1:]
    return pl.BlockSpec((1,) + dims, lambda b: (b,) + (0,) * len(dims))


def whole_block(array):
    dims = array.shape
    return pl.BlockSpec(dims, lambda b: (0,) * len(dims), pipeline_mode=pl.Buffered(1))


def with_bit(index, position, bit):
    low = 1 << position
    return (index // low) * (2 * low) + bit * low + index % low


def across(bit):
    me = lax.axis_index("dp")
    here = (me // (1 << bit)) % 2
    return here, (me + (1 - 2 * here) * (1 << bit), lax.axis_index("mp"))


class Group:
    def __init__(self, n, bits, bufs, sems, index, near):
        self.n, self.bits, self.bufs, self.near = n, bits, list(bufs), near
        self.send_sem, self.recv_sem, self.own_sem, self.index = sems[0], sems[1], sems[2], index
        self.levels = len(bits)

    @staticmethod
    def scratch(n, rows, width, kind):
        levels = n.bit_length() - 1
        shapes = [(n, rows, width)] * 2
        for level in range(levels):
            shapes += [(n >> (level + 1), rows, width)] * 3
        return [pltpu.VMEM(s, kind) for s in shapes]

    def remote(self, level, src, dst, target):
        return pltpu.make_async_remote_copy(
            src_ref=src, dst_ref=dst, send_sem=self.send_sem.at[self.index, level],
            recv_sem=self.recv_sem.at[self.index, level], device_id=target, device_id_type=MESH,
        )

    def first(self, src):
        return self.remote(0, src, self.bufs[1], self.near["sibling"])

    def load_own(self, src):
        return pltpu.make_async_copy(src, self.bufs[0], self.own_sem.at[self.index])

    def hop(self, level):
        return self.remote(level + 1, self.bufs[2 + 3 * level], self.bufs[4 + 3 * level], self.near[self.bits[level]][1])

    def advance(self, level):
        if level == 0:
            held, came = self.bufs[0], self.bufs[1]
        else:
            held, came = self.bufs[3 * level], self.bufs[3 * level + 1]
        to_send, to_keep = self.bufs[2 + 3 * level], self.bufs[3 + 3 * level]
        bit = self.bits[level]
        place = sum(1 for earlier in range(bit) if earlier not in self.bits[:level])
        here, _ = self.near[bit]
        count = self.n >> (level + 1)

        for t in range(count):
            gone = with_bit(t, place, 1 - here)
            to_send[t] = held[gone] + came[gone]
        self.hop(level).start()
        for t in range(count):
            kept = with_bit(t, place, here)
            to_keep[t] = held[kept] + came[kept]

    def total(self):
        last = self.levels - 1
        return self.bufs[3 + 3 * last][0].astype(F32) + self.bufs[4 + 3 * last][0].astype(F32)


def bit_orders(n):
    rest = tuple(range(3, n.bit_length() - 1))
    return (0, 1, 2) + rest, (1, 2, 0) + rest, (2, 0, 1) + rest


def neighbours(n):
    near = {bit: across(bit) for bit in range(n.bit_length() - 1)}
    near["core"] = lax.axis_index("mp")
    near["sibling"] = (lax.axis_index("dp"), 1 - near["core"])
    return near


def bit_partners(n, near):
    return [near["sibling"]] + [near[bit][1] for bit in range(n.bit_length() - 1)]


class Reducer:
    @staticmethod
    def plan(mats):
        pieces = []
        for index, mat in enumerate(mats):
            half = mat.shape[2] // 2
            width = 256 if half % 768 == 0 else 128
            pieces += [(index, begin, width) for begin in range(0, half, width)]
        return pieces

    @staticmethod
    def scratch(n, mats):
        shapes = []
        pieces = Reducer.plan(mats)
        for index, _, width in pieces:
            shapes += Group.scratch(n, mats[index].shape[1], width, mats[index].dtype)
        dma = pltpu.SemaphoreType.DMA
        levels = n.bit_length()
        return shapes + [dma((len(pieces), levels)), dma((len(pieces), levels)), dma((len(pieces),))]

    def __init__(self, n, mats, outs, refs, times):
        self.mats, self.outs, self.n = mats, outs, n
        self.pieces = Reducer.plan(mats)
        self.near = neighbours(n)
        orders = bit_orders(n)
        size = 2 + 3 * len(orders[0])
        sems = refs[-3:]
        self.groups = [
            Group(n, orders[index % 3], refs[index * size:(index + 1) * size], sems, index, self.near)
            for index in range(len(self.pieces))
        ]
        self.events = {}
        for index in range(len(self.pieces)):
            turn = times[min(index // 3, len(times) - 1)]
            for level in range(len(orders[0]) + 1):
                step = turn[level] if level < len(turn) else None
                self.events.setdefault(step, []).append((level, index))
        for step in self.events:
            self.events[step].sort(key=lambda e: (-e[0], e[1]) if step is not None else e)

    def source(self, index, side):
        mat, begin, width = self.pieces[index]
        at = side * (self.mats[mat].shape[2] // 2) + begin
        return self.mats[mat].at[:, :, pl.ds(pl.multiple_of(at, 128), width)]

    def start(self):
        core = self.near["core"]
        for index, group in enumerate(self.groups):
            group.first(self.source(index, 1 - core)).start()
            group.load_own(self.source(index, core)).start()

    def move(self, index, level):
        group = self.groups[index]
        core = self.near["core"]
        if level == 0:
            group.load_own(self.source(index, core)).wait()
            group.first(self.source(index, 1 - core)).wait()
        else:
            group.hop(level - 1).wait()
        if level < group.levels:
            group.advance(level)
        else:
            mat, begin, width = self.pieces[index]
            self.outs[mat][:, begin:begin + width] = group.total()

    def at(self, base, offset, period):
        step = base + offset
        for at_step, moves in self.events.items():
            if at_step is None or isinstance(offset, int) and at_step % period != offset:
                continue

            @pl.when(step == at_step)
            def _(moves=moves):
                for level, index in moves:
                    self.move(index, level)

    def finish(self):
        for level, index in self.events.get(None, []):
            self.move(index, level)


FEED_TIMES = ((2, 5, 10, 12, 15), (5, 10, 12, 15))


def feed_back_kernel(n, mat_count, douter, slope, nmid, imid, vecs_in, *refs):
    refs = list(refs)

    def take(count):
        taken = refs[:count]
        del refs[:count]
        return taken

    own, theirs, mats = take(10), take(10), take(mat_count)
    dinner, dattn, vecs = take(3)
    sums_out = take(mat_count)
    acc, vec, wi, wu, sems = take(5)
    summer = Reducer(n, mats, sums_out, refs, FEED_TIMES) if mats else None
    b = pl.program_id(0)
    rows = pl.num_programs(0)
    halves = Halves(sems)
    spread_halves(halves, own, theirs, vec=vec, wu=wu, wi=wi)

    def need(*names):
        @pl.when(b == 0)
        def _():
            for name in names:
                halves.wait(name)

    full = acc.shape[1]
    half = full // 2
    hidden = wi.shape[1]

    @pl.when(b == 0)
    def _():
        halves.start()
        vecs[...] = vecs_in[...]
        if summer:
            greet(bit_partners(n, summer.near))
            summer.start()

    need("vec", "wu", "wi")
    acc[...] = douter[0].astype(F32)
    parts = 4
    chunk = hidden // parts
    for j in range(parts):
        if summer:
            summer.at(b * parts, j, parts)
        cols = slice(j * chunk, (j + 1) * chunk)
        part = nt(douter[0], wu[cols, :]) * slope[0, :, cols].astype(F32)
        dinner[0, :, cols] = part.astype(BF)
        sums = token_sum(part)
        for i in range(2):
            quarter = 2 * j + i
            vecs[quarter // 4, VIN + quarter % 4:VIN + quarter % 4 + 1, :] += sums[:, i * half:(i + 1) * half]
        acc[...] += nt(dinner[0, :, cols], wi[:, cols])
    upstream = acc[...]
    normed = nmid[0].astype(F32)
    middle = norm_back(upstream, normed, imid[0], wide(vec, VGA))
    add_vec(vecs, VGA, token_sum(upstream * normed))
    add_vec(vecs, VSA, token_sum(upstream))
    add_vec(vecs, VO, token_sum(middle))
    dattn[0] = middle.astype(BF)

    @pl.when(b == rows - 1)
    def _():
        if summer:
            summer.finish()


def summed_shapes(mats):
    return tuple(jax.ShapeDtypeStruct((m.shape[1], m.shape[2] // 2), F32) for m in mats)


def feed_back(n, douter, slope, nmid, imid, vecs, own, theirs, mats):
    rows, seq, full = douter.shape
    hidden = slope.shape[2]
    shape = jax.ShapeDtypeStruct
    outs = (shape((rows, seq, hidden), BF), shape((rows, seq, full), BF))
    sums = (shape(vecs.shape, F32),) + summed_shapes(mats)
    by_row = (douter, slope, nmid, imid)
    scratch = [pltpu.VMEM((seq, full), F32)] + whole_scratch(own, "vec", "wi", "wu")
    params = dict(vmem_limit_bytes=VMEM_LIMIT)
    if mats:
        scratch += Reducer.scratch(n, mats)
        params.update(collective_id=4, has_side_effects=True)
    return pl.pallas_call(
        functools.partial(feed_back_kernel, n, len(mats)),
        out_shape=outs + sums,
        grid=(rows,),
        in_specs=[row_block(a) for a in by_row] + [whole_block(vecs)] + any_spec(20 + len(mats)),
        out_specs=tuple([row_block(a) for a in outs] + [whole_block(a) for a in sums]),
        scratch_shapes=scratch,
        compiler_params=pltpu.CompilerParams(**params),
        name="feed_back",
    )(*by_row, vecs, *own, *theirs, *mats)


ATTEND_TIMES = ((2, 5, 10, 13, 16), (5, 10, 13, 16, 19), (10, 13, 16, 19, 22))


def attend_back_kernel(n, mat_count, dattn, qkv, lse, seg_col, seg_row, vecs_in, *refs):
    refs = list(refs)

    def take(count):
        taken = refs[:count]
        del refs[:count]
        return taken

    own, theirs, mats = take(10), take(10), take(mat_count)
    dqkv, dstart, vecs = take(3)
    sums_out = take(mat_count)
    bias, grads, wqkv, wo, halves_sem = take(5)
    summer = Reducer(n, mats, sums_out, refs, ATTEND_TIMES) if mats else None
    b = pl.program_id(0)
    rows = pl.num_programs(0)
    seq, full = grads.shape
    half = full // 2
    gang = GANG
    pair = gang * HEAD_DIM
    pairs = full // pair
    halves = Halves(halves_sem)
    spread_halves(halves, own, theirs, wo=wo, wqkv=wqkv)

    @pl.when(b == 0)
    def _():
        halves.start()
        vecs[...] = vecs_in[...]
        if summer:
            greet(bit_partners(n, summer.near))
            summer.start()
        halves.wait("wo")
        halves.wait("qkv")

    grads[...] = nt(dattn[0], wo[...]).astype(BF)
    bias[...] = jnp.where(seg_col[0] == seg_row[0], 0.0, NEGATIVE)
    masks = head_masks(gang)

    def heads(p):
        if summer:
            summer.at(b * pairs, p, pairs)
        at = p * pair
        queries = qkv[0, :, pl.ds(at, pair)]
        keys = qkv[0, :, pl.ds(full + at, pair)]
        values = qkv[0, :, pl.ds(2 * full + at, pair)]
        dctx = grads[:, pl.ds(at, pair)]
        lane = lax.broadcasted_iota(jnp.int32, (seq, pair), 1)
        keys_all = jnp.concatenate([keys * m for m in masks], axis=0)
        s = nt(keys_all, queries)
        dw = nt(jnp.concatenate([values * m for m in masks], axis=0), dctx)
        ws, dss = [], []
        for h in range(gang):
            w = jnp.exp(s[h * seq:(h + 1) * seq] + bias[...] - lse[0, gang * p + h:gang * p + h + 1, :])
            prod = w * dw[h * seq:(h + 1) * seq]
            dss.append((prod - w * token_sum(prod)).astype(BF))
            ws.append(w.astype(BF))
        ds = jnp.concatenate(dss, axis=0)
        dv = mm(jnp.concatenate(ws, axis=0), dctx)
        dk = mm(ds, queries)
        dq = tn(ds, keys_all) * HEAD_DIM ** -0.5

        def join(parts):
            joined = parts[0:seq]
            for h in range(1, gang):
                joined = jnp.where(lane < h * HEAD_DIM, joined, parts[h * seq:(h + 1) * seq])
            return joined

        for t, value in enumerate((dq, join(dk), join(dv))):
            for i in range(0, pair, 128):
                column = p * pair + i
                out_at = (column // half) * (3 * half) + column % half + t * half
                dqkv[0, :, pl.ds(out_at, 128)] = value[:, i:i + 128].astype(BF)

    for p in range(pairs):
        heads(p)
    total = dattn[0].astype(F32)
    for h in range(2):
        for t in range(3):
            source = dqkv[0, :, (3 * h + t) * half:(3 * h + t + 1) * half]
            total += nt(source, wqkv[:, t * full + h * half:t * full + (h + 1) * half])
            if t != 1:
                at = VQ if t == 0 else VV
                vecs[h, at:at + 1, :] += token_sum(source.astype(F32))
    dstart[0] = total.astype(BF)

    @pl.when(b == rows - 1)
    def _():
        if summer:
            summer.finish()


def attend_back(n, dattn, qkv, lse, seg_col, seg_row, vecs, own, theirs, mats):
    rows, seq, full = dattn.shape
    shape = jax.ShapeDtypeStruct
    outs = (shape((rows, seq, 3 * full), BF), shape((rows, seq, full), BF))
    sums = (shape(vecs.shape, F32),) + summed_shapes(mats)
    by_row = (dattn, qkv, lse, seg_col, seg_row)
    scratch = [pltpu.VMEM((seq, seq), F32), pltpu.VMEM((seq, full), BF)] + whole_scratch(own, "wqkv", "wo")
    params = dict(vmem_limit_bytes=VMEM_LIMIT)
    if mats:
        scratch += Reducer.scratch(n, mats)
        params.update(collective_id=3, has_side_effects=True)
    return pl.pallas_call(
        functools.partial(attend_back_kernel, n, len(mats)),
        out_shape=outs + sums,
        grid=(rows,),
        in_specs=[row_block(a) for a in by_row] + [whole_block(vecs)] + any_spec(20 + len(mats)),
        out_specs=tuple([row_block(a) for a in outs] + [whole_block(a) for a in sums]),
        scratch_shapes=scratch,
        compiler_params=pltpu.CompilerParams(**params),
        name="attend_back",
    )(*by_row, vecs, *own, *theirs, *mats)


def deliver_kernel(n, summed, slot_row, vec_in, place, mixed_in, dstart, xlow, dqkv, *refs):
    refs = list(refs)

    def take(count):
        taken = refs[:count]
        del refs[:count]
        return taken

    gt, arrived, mixed, vec_out = take(4)
    sums_out = take(4) if summed else []
    gt_v, stage, mix_own, mix_got, vec_bufs = take(5)
    (own_sem, sib_send, sib_recv, doc_send, doc_recv, vec_send, vec_recv) = take(7)
    me = lax.axis_index("dp")
    core = lax.axis_index("mp")
    other = 1 - core
    sibling = (me, other)
    levels = n.bit_length() - 1
    far = [across(bit)[1] for bit in range(levels) if (1 << bit) > REACH]
    greet(ring_partners(me, core, n) + [sibling] + (far if summed else []))
    rows, seq, full = dstart.shape
    half = full // 2
    here_cols = pl.ds(pl.multiple_of(core * half, half), half)
    there_cols = pl.ds(pl.multiple_of(other * half, half), half)
    my_rows = pl.ds(core * rows, rows)

    tok_far = pltpu.make_async_remote_copy(
        src_ref=dstart.at[:, :, there_cols], dst_ref=gt_v.at[my_rows], send_sem=sib_send.at[0],
        recv_sem=sib_recv.at[0], device_id=sibling, device_id_type=MESH,
    )
    tok_far.start()
    tok_own = pltpu.make_async_copy(dstart.at[:, :, here_cols], gt_v.at[my_rows], own_sem.at[0])
    tok_own.start()
    vec_copy = pltpu.make_async_remote_copy(
        src_ref=vec_in.at[other], dst_ref=vec_bufs.at[0], send_sem=vec_send.at[0],
        recv_sem=vec_recv.at[0], device_id=sibling, device_id_type=MESH,
    )
    vec_copy.start()
    loads = []
    if summed:
        x_v, dqkv_v, dstart_v = take(3)
        for index, (src, dst) in enumerate(((xlow, x_v), (dqkv, dqkv_v), (dstart, dstart_v))):
            for r in range(rows):
                load = pltpu.make_async_copy(src.at[r], dst.at[pl.ds(r * seq, seq)], own_sem.at[4 + index * rows + r])
                load.start()
                loads.append(load)
    mix_far = pltpu.make_async_remote_copy(
        src_ref=mixed_in.at[:, there_cols], dst_ref=mix_got, send_sem=sib_send.at[1],
        recv_sem=sib_recv.at[1], device_id=sibling, device_id_type=MESH,
    )
    mix_far.start()
    mix_load = pltpu.make_async_copy(mixed_in.at[:, here_cols], mix_own, own_sem.at[1])
    mix_load.start()

    tok_own.wait()
    tok_far.wait()
    tok_out = pltpu.make_async_copy(gt_v, gt, own_sem.at[2])
    tok_out.start()
    sent = []
    order = sorted(range(SLOTS), key=lambda s: -abs(s - REACH))
    for slot in order:
        stage[slot] = gt_v[slot_row[slot]]
        if slot == REACH:
            copy = pltpu.make_async_copy(stage.at[slot], arrived.at[slot], own_sem.at[3])
        else:
            copy = pltpu.make_async_remote_copy(
                src_ref=stage.at[slot], dst_ref=arrived.at[slot], send_sem=doc_send.at[slot],
                recv_sem=doc_recv.at[slot],
                device_id=(lax.rem(me + slot - REACH + n, n), core), device_id_type=MESH,
            )
        copy.start()
        sent.append(copy)

    if summed:
        for load in loads:
            load.wait()
        outgoing = take(4)
        near = neighbours(n)
        orders = bit_orders(n)
        size = 2 + 3 * levels
        sems = refs[-3:]
        groups = [Group(n, orders[(0, 1, 0, 1)[index]], take(size), sems, index, near) for index in range(4)]
        table = sums_out[3].shape[0] * n
        one_hot = (
            place[...] == lax.broadcasted_iota(jnp.int32, (table, rows * seq), 0)
        ).astype(F32).astype(BF)

        def product(index, side, target):
            if index < 3:
                at = pl.ds(pl.multiple_of(side * 3 * half + index * half, half), half)
                value = tn(x_v[...], dqkv_v[:, at])
            else:
                at = pl.ds(pl.multiple_of(side * half, half), half)
                value = mm(one_hot, dstart_v[:, at])
            depth = target.shape[1]
            for i in range(n):
                target[i] = value[i * depth:(i + 1) * depth].astype(target.dtype)

        firsts = []
        for index, group in enumerate(groups):
            product(index, other, outgoing[index])
            copy = group.first(outgoing[index])
            copy.start()
            firsts.append(copy)
            product(index, core, group.bufs[0])
            if index > 0:
                firsts[index - 1].wait()
                groups[index - 1].advance(0)
        firsts[-1].wait()
        groups[-1].advance(0)
        for level in range(levels + 1):
            for index, group in enumerate(groups):
                if level == 0:
                    continue
                group.hop(level - 1).wait()
                if level < levels:
                    group.advance(level)
                else:
                    sums_out[index][...] = group.total()
            vec_copy.wait()
            if level == 0:
                vec_total = vec_in[core] + vec_bufs[0]
            else:
                vec_total = vec_total + vec_bufs[2 * level]
            if level < levels:
                vec_bufs[2 * level + 1] = vec_total
                vec_copy = pltpu.make_async_remote_copy(
                    src_ref=vec_bufs.at[2 * level + 1], dst_ref=vec_bufs.at[2 * level + 2],
                    send_sem=vec_send.at[level + 1], recv_sem=vec_recv.at[level + 1],
                    device_id=across(level)[1], device_id_type=MESH,
                )
                vec_copy.start()
            else:
                vec_out[...] = vec_total
    else:
        vec_copy.wait()
        vec_out[...] = vec_in[core] + vec_bufs[0]
    mix_load.wait()
    mix_far.wait()
    mixed[...] = (mix_own[...] + mix_got[...]).astype(BF)
    tok_out.wait()
    for copy in sent:
        copy.wait()


def deliver(n, summed, table, slot_row, vecs, place, mixed, dstart, xlow, dqkv):
    rows, seq, full = dstart.shape
    half = full // 2
    levels = n.bit_length() - 1
    shape = jax.ShapeDtypeStruct
    outs = [
        shape((2 * rows, seq, half), BF), shape((SLOTS, seq, half), BF), shape((seq, half), BF),
        shape(vecs.shape[1:], F32),
    ]
    dma = pltpu.SemaphoreType.DMA
    scratch = [
        pltpu.VMEM((2 * rows, seq, half), BF), pltpu.VMEM((SLOTS, seq, half), BF),
        pltpu.VMEM((seq, half), F32), pltpu.VMEM((seq, half), F32),
        pltpu.VMEM((2 * levels + 2,) + vecs.shape[1:], F32),
        dma((4 + 3 * rows,)), dma((2,)), dma((2,)), dma((SLOTS,)), dma((SLOTS,)), dma((levels + 1,)), dma((levels + 1,)),
    ]
    if summed:
        tokens = rows * seq
        scratch += [pltpu.VMEM((tokens, a.shape[2]), BF) for a in (xlow, dqkv, dstart)]
        depths = [full // n] * 3 + [table // n]
        scratch += [pltpu.VMEM((n, depth, half), BF) for depth in depths]
        for depth in depths:
            scratch += Group.scratch(n, depth, half, BF)
        scratch += [dma((4, levels + 1)), dma((4, levels + 1)), dma((4,))]
        outs += [shape((depth, half), F32) for depth in depths]
    return pl.pallas_call(
        functools.partial(deliver_kernel, n, summed),
        out_shape=tuple(outs),
        in_specs=[pl.BlockSpec(memory_space=pltpu.SMEM)] + vmem_spec(2) + any_spec(4),
        out_specs=tuple(any_spec(2) + vmem_spec(len(outs) - 2)),
        scratch_shapes=scratch,
        compiler_params=pltpu.CompilerParams(
            collective_id=2, has_side_effects=True, vmem_limit_bytes=VMEM_LIMIT
        ),
        name="deliver",
    )(slot_row, vecs, place, mixed, dstart, xlow, dqkv)


def place_kernel(want, arrived, out, got, total, sems):
    docs = out.shape[0]
    loads = [pltpu.make_async_copy(arrived.at[slot], got.at[slot], sems.at[slot]) for slot in range(SLOTS)]
    for load in loads:
        load.start()

    def clear(d, carry):
        total[d] = jnp.zeros(total.shape[1:], F32)
        return carry

    lax.fori_loop(0, docs, clear, 0)
    for slot in range(SLOTS):
        loads[slot].wait()
        at = jnp.where(want[slot] < 0, docs, want[slot])
        total[at] += got[slot].astype(F32)
    done = pltpu.make_async_copy(total.at[pl.ds(0, docs)], out, sems.at[SLOTS])
    done.start()
    done.wait()


def place_docs(want, arrived, docs):
    _, seq, half = arrived.shape
    return pl.pallas_call(
        place_kernel,
        out_shape=jax.ShapeDtypeStruct((docs, seq, half), F32),
        in_specs=[pl.BlockSpec(memory_space=pltpu.SMEM)] + any_spec(1),
        out_specs=pl.BlockSpec(memory_space=pl.ANY),
        scratch_shapes=[
            pltpu.VMEM(arrived.shape, BF), pltpu.VMEM((docs + 1, seq, half), F32), pltpu.SemaphoreType.DMA((SLOTS + 1,)),
        ],
        compiler_params=pltpu.CompilerParams(vmem_limit_bytes=VMEM_LIMIT),
        name="place_docs",
    )(want, arrived)


def body(
    tokens, segment_ids, positions, query_vectors, doc_owner, doc_slot, doc_store, pos_table,
    w_query, w_key, w_value, b_query, b_value, w_out, b_out, gain_attn, shift_attn,
    w_inner, b_inner, w_outer, b_outer, gain_ffn, shift_ffn, w_cls, cotangent,
):
    n = lax.axis_size("dp")
    me = lax.axis_index("dp")
    core = lax.axis_index("mp")
    row_count, seq, half = tokens.shape
    rows = row_count // 2
    full = 2 * half
    doc_count = doc_store.shape[0]
    place_slot = (doc_owner[0] - me + REACH) % n
    match = (place_slot[None, :] == jnp.arange(SLOTS, dtype=jnp.int32)[:, None]).astype(jnp.int32)
    req = jnp.sum(match * (doc_slot[0] + 1)[None, :], axis=1) - 1
    slot_row = jnp.sum(match * jnp.arange(row_count, dtype=jnp.int32)[None, :], axis=1)
    req = jnp.broadcast_to(req[:, None, None], (SLOTS, 8, 128))
    vec_in = jnp.concatenate(
        [v.reshape(-1, half) for v in (b_query, b_value, b_out, gain_attn, shift_attn, b_outer, gain_ffn, shift_ffn, b_inner)]
        + [jnp.zeros((VROWS - 12, half), F32)], axis=0,
    )
    weights = (w_query, w_key, w_value, w_out, w_inner, w_outer, w_cls)
    docs, docs_sib, tok_sib, *theirs, got = fetch(
        n, req, doc_store, tokens, cotangent, *weights, pos_table, vec_in
    )
    own = (cotangent[0], pos_table, vec_in) + weights
    want = got[:, 0, 0]
    seg = lax.dynamic_slice_in_dim(segment_ids, core * rows, rows, 0)
    place = lax.dynamic_slice_in_dim(positions, core * rows, rows, 0)
    my_slots = lax.dynamic_slice_in_dim(place_slot, core * rows, rows, 0)
    my_slots = jnp.concatenate([my_slots, core[None].astype(jnp.int32)])
    seg_col, seg_row = seg[:, :, None], seg[:, None, :]
    xlow, qkv, lse, ctx, nmid, imid, mlow, act, slope, nout, iout, res, summ, prod = forward(
        my_slots, tokens, tok_sib, docs, docs_sib, place[:, :, None], seg_col, seg_row, own, theirs
    )
    douter, mixed, vecs, dw_cls, grad_query = share_out(summ, prod, query_vectors, iout, nout, res, own, theirs)

    def cross(left, right):
        left = left.reshape(-1, left.shape[-1])
        right = right.reshape(-1, right.shape[-1])
        return tn(left, right)

    def cut(part, kind):
        return part.astype(kind).reshape(n, part.shape[0] // n, part.shape[1])

    summed = full // n % 16 == 0
    table = pos_table.shape[0]
    dw_outer = cross(douter, act)
    dinner, dattn, vecs, *done = feed_back(
        n, douter, slope, nmid, imid, vecs, own, theirs, [cut(dw_outer, BF), cut(dw_cls, F32)] if summed else []
    )
    dw_inner, dw_out = cross(mlow, dinner), cross(dattn, ctx)
    dqkv, dstart, vecs, *more = attend_back(
        n, dattn, qkv, lse, seg_col, seg_row, vecs, own, theirs, [cut(dw_inner, BF), cut(dw_out, BF)] if summed else []
    )
    grad_tokens, arrived, mixed_out, vec_sum, *small = deliver(
        n, summed, table, slot_row, vecs, place.reshape(1, -1), mixed, dstart, xlow, dqkv
    )
    if summed:
        g_outer, g_cls = done
        g_inner, g_wo = more
        g_q, g_k, g_v, g_pos = small
    else:
        vec_sum = lax.psum(vec_sum, "dp")
        one_hot = (place.reshape(-1)[:, None] == jnp.arange(table, dtype=jnp.int32)[None, :]).astype(BF)

        def scatter(part):
            part = lax.psum_scatter(part.astype(F32), "mp", scatter_dimension=1, tiled=True)
            return lax.psum_scatter(part, "dp", scatter_dimension=0, tiled=True)

        g_outer, g_inner, g_wo, g_qkv, g_cls, g_pos = [
            scatter(p) for p in (dw_outer, dw_inner, dw_out, cross(xlow, dqkv), dw_cls, cross(one_hot, dstart))
        ]
        g_q, g_k, g_v = g_qkv[:, :half], g_qkv[:, half:2 * half], g_qkv[:, 2 * half:]
    grad_docs = place_docs(want, arrived, doc_count)

    def row(index):
        return vec_sum[index]

    return (
        mixed_out[None],
        grad_tokens,
        grad_query,
        grad_docs,
        g_pos,
        g_q,
        g_k,
        g_v,
        row(VQ),
        row(VV),
        g_wo.T,
        row(VO),
        row(VGA),
        row(VSA),
        g_inner,
        vec_sum[VIN:VIN + 4].reshape(-1),
        g_outer.T,
        row(VBO),
        row(VGF),
        row(VSF),
        g_cls.T,
    )


def solution(mesh):
    rows = P("dp", None, "mp")
    ids = P("dp", None)
    cols = P(None, "mp")
    vec = P("mp")
    deep = P("mp", None)
    in_specs = (
        rows, ids, ids, ids, ids, ids, rows, cols, cols, cols, cols, vec, vec, deep, vec, vec, vec,
        cols, vec, deep, vec, vec, vec, deep, rows,
    )
    near = P("dp", "mp")
    turned = P("mp", "dp")
    out_specs = (
        rows, rows, ids, rows, near, near, near, near, vec, vec, turned, vec, vec, vec, near, vec,
        turned, vec, vec, vec, turned,
    )
    return jax.shard_map(body, mesh=mesh, in_specs=in_specs, out_specs=out_specs, check_vma=False)
```

```python
import functools

import jax
import jax.numpy as jnp
from jax import lax
from jax.experimental import pallas as pl
from jax.experimental.pallas import tpu as pltpu
from jax.sharding import PartitionSpec as P

HEAD_DIM = 64
PROJ = 128
REACH = 6
SLOTS = 2 * REACH
OFFSETS = (0, 1, -1, 2, -2, 4, 3, -3, -4, 5, -5, -6)
LOCAL = 0
REMOTE = tuple(range(1, SLOTS))
EPSILON = 1e-05
NEGATIVE = -1e30
PRECISE = lax.Precision.HIGHEST
MESH = pl.DeviceIdType.MESH
BF = jnp.bfloat16
F32 = jnp.float32
VMEM_LIMIT = 60 * 1024 * 1024
VQ, VV, VO, VGA, VSA, VBO, VGF, VSF, VIN = range(9)
VROWS = 16
GANG = 2


def any_spec(count):
    return [pl.BlockSpec(memory_space=pl.ANY)] * count


def vmem_spec(count):
    return [pl.BlockSpec(memory_space=pltpu.VMEM)] * count


def row_block(array):
    dims = array.shape[1:]
    return pl.BlockSpec((1,) + dims, lambda b: (b,) + (0,) * len(dims))


def row_back(array):
    dims = array.shape[1:]
    last = array.shape[0] - 1
    return pl.BlockSpec((1,) + dims, lambda b: (last - b,) + (0,) * len(dims))


def whole_block(array):
    dims = array.shape
    return pl.BlockSpec(dims, lambda b: (0,) * len(dims), pipeline_mode=pl.Buffered(1))


def nt(left, right):
    return lax.dot_general(left, right, (((1,), (1,)), ((), ())), preferred_element_type=F32)


def tn(left, right):
    return lax.dot_general(left, right, (((0,), (0,)), ((), ())), preferred_element_type=F32)


def mm(left, right):
    return jnp.dot(left, right, preferred_element_type=F32)


def greet(targets):
    barrier = pltpu.get_barrier_semaphore()
    for target in targets:
        pl.semaphore_signal(barrier, inc=1, device_id=target, device_id_type=MESH)
    pl.semaphore_wait(barrier, len(targets))


def ring_partners(me, core, n):
    return [(lax.rem(me + step + n, n), core) for step in range(-REACH, REACH + 1) if step != 0]


class Halves:
    def __init__(self, sems):
        self.sems, self.copies, self.names = sems, [], {}

    def add(self, name, own, theirs, whole, axis, offset=0, stride=None):
        core = lax.axis_index("mp")
        size = own.shape[axis] if axis is not None else 1
        for source, side in ((own, core), (theirs, 1 - core)):
            if axis is None:
                target = whole.at[side]
            else:
                begin = offset + side * (stride or size)
                at = pl.ds(pl.multiple_of(begin, 128), size)
                target = whole.at[at] if axis == 0 else whole.at[:, at]
            copy = pltpu.make_async_copy(source, target, self.sems.at[len(self.copies)])
            self.copies.append(copy)
            self.names.setdefault(name, []).append(copy)

    def start(self):
        self.start_own()
        self.start_theirs()

    def start_own(self):
        for copy in self.copies[0::2]:
            copy.start()

    def start_theirs(self):
        for copy in self.copies[1::2]:
            copy.start()

    def wait(self, name):
        for copy in self.names[name]:
            copy.wait()


def wide(vec, row):
    return jnp.concatenate([vec[0, row:row + 1, :], vec[1, row:row + 1, :]], axis=1)


def inner_bias(vec):
    return jnp.concatenate([vec[h, VIN + j:VIN + j + 1, :] for h in range(2) for j in range(4)], axis=1)


def normalize(hidden):
    average = jnp.mean(hidden, axis=-1, keepdims=True)
    centered = hidden - average
    spread = jnp.mean(centered * centered, axis=-1, keepdims=True)
    inverse = lax.rsqrt(spread + EPSILON)
    return centered * inverse, inverse


def column(row):
    size = row.shape[1]
    here = lax.broadcasted_iota(jnp.int32, (size, size), 0) == lax.broadcasted_iota(jnp.int32, (size, size), 1)
    return jnp.sum(jnp.where(here, row, 0), axis=1, keepdims=True)


def head_masks(count):
    lane = lax.broadcasted_iota(jnp.int32, (1, count * HEAD_DIM), 1) // HEAD_DIM
    return [(lane == h).astype(F32).astype(BF) for h in range(count)]


def spread_halves(halves, own, theirs, **whole):
    places = {"cot": (0, 1), "pos": (1, 1), "vec": (2, None), "wo": (6, 0), "wi": (7, 1), "wu": (8, 0), "wc": (9, 0)}
    for name, ref in whole.items():
        if name == "wqkv":
            for index in range(3):
                halves.add("qkv", own[3 + index], theirs[3 + index], ref, 1, index * ref.shape[0])
        else:
            at, axis = places[name]
            halves.add(name, own[at], theirs[at], ref, axis)


def whole_scratch(own, *names):
    cot, pos, vec, wq, _, _, wo, wi, wu, wc = own
    full = wq.shape[0]
    shapes = {
        "cot": ((cot.shape[0], full), BF), "pos": ((pos.shape[0], full), BF), "vec": ((2,) + vec.shape, F32),
        "wqkv": ((full, 3 * full), BF), "wo": ((full, full), BF), "wi": ((full, 2 * wi.shape[1]), BF),
        "wu": ((2 * wu.shape[0], full), BF), "wc": ((full, wc.shape[1]), BF),
    }
    return [pltpu.VMEM(*shapes[name]) for name in names] + [pltpu.SemaphoreType.DMA((20,))]


LATE_START = 5
LATE_AT = 2


def forward_kernel(n, owner, doc_slot, places, segments, *refs):
    refs = list(refs)

    def take(count):
        taken = refs[:count]
        del refs[:count]
        return taken

    vectors = take(9)
    docs_in, tok_in, cot_in, pos_in = take(4)
    weights_in = take(7)
    theirs = take(10)
    vec_own, want, rank_out, slot_of, picks = take(5)
    xlow, qkv, lse, ctx, nmid, imid, mlow, act, slope, nout, iout, res, summ, prod = take(14)
    bias, stats, acc, cot, pos, vec, wqkv, wo, wi, wu, wc, sems = take(12)
    doc_buf, stage, docs, docs_sib, tok, tok_sib, req, got, got_s = take(9)
    req_send, req_recv, doc_send, doc_recv, fwd_send, fwd_recv, sib_send, sib_recv, misc_sem = take(9)
    own = [cot_in, pos_in, vec_own] + weights_in
    b = pl.program_id(0)
    rows = pl.num_programs(0)
    me = lax.axis_index("dp")
    core = lax.axis_index("mp")
    sibling = (me, 1 - core)
    seq, full = acc.shape
    row_count, _, half = tok_in.shape
    all_rows = row_count // 2
    early = SLOTS - row_count + 2
    halves = Halves(sems)
    spread_halves(halves, own, theirs, pos=pos, vec=vec, wqkv=wqkv, wo=wo, wi=wi, wu=wu, wc=wc, cot=cot)
    fresh = b == 0

    def request(slot):
        return pltpu.make_async_remote_copy(
            src_ref=req.at[slot], dst_ref=got.at[slot], send_sem=req_send.at[slot], recv_sem=req_recv.at[slot],
            device_id=(lax.rem(me + OFFSETS[slot] + n, n), core), device_id_type=MESH,
        )

    def document(slot):
        return pltpu.make_async_remote_copy(
            src_ref=stage.at[slot], dst_ref=docs.at[slot], send_sem=doc_send.at[slot], recv_sem=doc_recv.at[slot],
            device_id=(lax.rem(me - OFFSETS[slot] + n, n), core), device_id_type=MESH,
        )

    def pass_on(slot):
        return pltpu.make_async_remote_copy(
            src_ref=docs.at[slot], dst_ref=docs_sib.at[slot], send_sem=fwd_send.at[slot], recv_sem=fwd_recv.at[slot],
            device_id=sibling, device_id_type=MESH,
        )

    sources = [tok_in, pos_in, vec_own] + weights_in + [cot_in]
    targets = [tok_sib] + theirs[1:] + [theirs[0]]

    def share(index):
        return pltpu.make_async_remote_copy(
            src_ref=sources[index], dst_ref=targets[index], send_sem=sib_send.at[index], recv_sem=sib_recv.at[index],
            device_id=sibling, device_id_type=MESH,
        )

    doc_load = pltpu.make_async_copy(docs_in, doc_buf, misc_sem.at[0])
    tok_load = pltpu.make_async_copy(tok_in, tok, misc_sem.at[1])
    to_scalar = pltpu.make_async_copy(got, got_s, misc_sem.at[2])

    @pl.when(fresh)
    def _():
        doc_load.start()
        one = jnp.int32(1)
        zero = jnp.int32(0)
        offsets = [lax.rem(owner[0, k] - me + REACH + n, n) - REACH for k in range(row_count)]
        slots = [sum(jnp.where(o == OFFSETS[slot], slot * one, zero) for slot in range(SLOTS)) for o in offsets]
        ranks = []
        for k in range(row_count):
            ranks.append(sum(jnp.where(slots[j] < slots[k], one, zero) for j in range(row_count) if j != k))
            rank_out[k] = ranks[k]
        for slot in range(SLOTS):
            asked_for = sum(jnp.where(slots[k] == slot, doc_slot[0, k] + 1, zero) for k in range(row_count)) - 1
            req[slot] = jnp.full(req.shape[1:], asked_for, jnp.int32)
        vec_own[...] = jnp.zeros_like(vec_own)
        for index, vector in enumerate(vectors):
            for i in range(vector.shape[0] // half):
                vec_own[index + i] = vector[i * half:(i + 1) * half]
        greet(ring_partners(me, core, n) + [sibling])
        for slot in REMOTE:
            request(slot).start()
        for index in range(len(sources)):
            share(index).start()
        tok_load.start()
        halves.start_own()
        for rank in range(row_count):
            slot = sum(jnp.where(ranks[k] == rank, slots[k], zero) for k in range(row_count))
            row = sum(jnp.where(ranks[k] == rank, k * one, zero) for k in range(row_count))
            slot_of[rank] = slot
            picks[rank] = slot
            picks[row_count + rank] = jnp.minimum(row, row_count - 1)
        got[LOCAL] = req[LOCAL]
        for slot in REMOTE:
            request(slot).wait()
        to_scalar.start()
        doc_load.wait()
        to_scalar.wait()
        for slot in range(SLOTS):
            want[slot] = got_s[slot, 0, 0]
        for slot in REMOTE[:early - 1]:
            stage[slot] = doc_buf[jnp.clip(got_s[slot, 0, 0], 0, doc_buf.shape[0] - 1)]
            document(slot).start()
        docs[LOCAL] = doc_buf[jnp.clip(got_s[LOCAL, 0, 0], 0, doc_buf.shape[0] - 1)]
        pass_on(LOCAL).start()
        for slot in range(early, SLOTS):
            stage[slot] = doc_buf[jnp.clip(got_s[slot, 0, 0], 0, doc_buf.shape[0] - 1)]
        for index in range(len(sources)):
            share(index).wait()
        halves.start_theirs()
        tok_load.wait()
        for slot in REMOTE[:early - 1]:
            document(slot).wait_recv()
            pass_on(slot).start()
            if slot == LATE_START:
                for late in range(early, SLOTS):
                    document(late).start()
        for slot in range(early):
            pass_on(slot).wait_recv()

    for step in range(1, all_rows):

        @pl.when(b == step)
        def _(step=step):
            for slot in range(early + 2 * step - 2, early + 2 * step):
                pass_on(slot).wait_recv()

    def take_late(step):
        for slot in range(early + 2 * step, early + 2 * step + 2):
            document(slot).wait_recv()
            pass_on(slot).start()

    def need(*names):
        @pl.when(fresh)
        def _():
            for name in names:
                halves.wait(name)

    first = core == 0
    my_rank = 2 * b + core

    def join(a, b):
        a, b = a.astype(F32), b.astype(F32)
        return jnp.concatenate([jnp.where(first, a, b), jnp.where(first, b, a)], axis=1)

    def chosen(held):
        value = held[my_rank]
        for i in range(1, SLOTS - row_count + 1):
            value = jnp.where(picks[my_rank] == my_rank + i, held[my_rank + i], value)
        return value

    need("pos", "vec")
    table = pos.shape[0]
    row = picks[row_count + my_rank]
    seg_row = segments[pl.ds(row, 1), :]
    one_hot = (column(places[pl.ds(row, 1), :]) == lax.broadcasted_iota(jnp.int32, (seq, table), 1)).astype(F32).astype(BF)
    embedded = join(tok[row], tok_sib[row]) + mm(one_hot, pos[...]) + join(chosen(docs), chosen(docs_sib))
    low = embedded.astype(BF)
    xlow[0] = low
    acc[...] = embedded
    need("qkv")
    q = (mm(low, wqkv[:, 0:full]) + wide(vec, VQ)).astype(BF)
    qkv[0, :, 0:full] = q * jnp.asarray(HEAD_DIM ** -0.5, BF)
    qkv[0, :, full:2 * full] = mm(low, wqkv[:, full:2 * full]).astype(BF)
    qkv[0, :, 2 * full:] = (mm(low, wqkv[:, 2 * full:]) + wide(vec, VV)).astype(BF)
    bias[...] = jnp.where(column(seg_row) == seg_row, 0.0, NEGATIVE)
    stats[...] = jnp.zeros_like(stats)
    masks = head_masks(GANG)
    wide_gang = GANG * HEAD_DIM

    def heads(p, carry):
        at = pl.multiple_of(p * wide_gang, wide_gang)
        queries = qkv[0, :, pl.ds(at, wide_gang)]
        keys = qkv[0, :, pl.ds(full + at, wide_gang)]
        values = qkv[0, :, pl.ds(2 * full + at, wide_gang)]
        lane = lax.broadcasted_iota(jnp.int32, (seq, wide_gang), 1)
        small_lane = lax.broadcasted_iota(jnp.int32, (seq, 128), 1)
        s = nt(jnp.concatenate([queries * m for m in masks], axis=0), keys)
        es, totals = [], []
        for h in range(GANG):
            sh = s[h * seq:(h + 1) * seq] + bias[...]
            top = jnp.max(sh, axis=1, keepdims=True)
            e = jnp.exp(sh - top)
            total = jnp.sum(e, axis=1, keepdims=True)
            es.append(e.astype(BF))
            totals.append(1.0 / total)
            stats[0:seq, :] = jnp.where(small_lane == GANG * p + h, top + jnp.log(total), stats[0:seq, :])
        out = mm(jnp.concatenate(es, axis=0), values)
        joined = out[0:seq] * totals[0]
        for h in range(1, GANG):
            joined = jnp.where(lane < h * HEAD_DIM, joined, out[h * seq:(h + 1) * seq] * totals[h])
        ctx[0, :, pl.ds(at, wide_gang)] = joined.astype(BF)
        return carry

    lax.fori_loop(0, full // wide_gang, heads, 0, unroll=3)
    lse[0] = jnp.transpose(stats[...])[0:lse.shape[1], 0:seq]
    need("wo")
    normed, inverse = normalize(acc[...] + mm(ctx[0], wo[...]) + wide(vec, VO))
    middle = normed * wide(vec, VGA) + wide(vec, VSA)
    nmid[0] = normed.astype(BF)
    imid[0] = inverse
    acc[...] = middle + wide(vec, VBO)
    mlow[0] = middle.astype(BF)
    need("wi", "wu", "wc", "cot")
    hidden = wi.shape[1]
    chunk = hidden // 4
    bin_all = inner_bias(vec)
    for j in range(4):
        if j == LATE_AT:
            for step in range(all_rows - 1):

                @pl.when(b == step)
                def _(step=step):
                    take_late(step)

        cols = slice(j * chunk, (j + 1) * chunk)
        pre = mm(mlow[0], wi[:, cols]) + bin_all[:, cols]
        phi = 0.5 + 0.5 * lax.erf(pre * (0.5 ** 0.5))
        act[0, :, cols] = (pre * phi).astype(BF)
        slope[0, :, cols] = (phi + pre * (jnp.exp(-0.5 * pre * pre) * 0.3989422804014327)).astype(BF)
        acc[...] += mm(act[0, :, cols], wu[cols, :])
    normed, inverse = normalize(acc[...])
    nout[0] = normed.astype(BF)
    iout[0] = inverse
    result = (normed * wide(vec, VGF) + wide(vec, VSF)).astype(BF)
    res[0] = result
    summ[0] = mm(res[0, 0:16, :], wc[...])[0:8]
    product = jnp.sum(cot[...].astype(F32) * result.astype(F32))
    prod[0] = jnp.full(prod.shape[1:], product, F32)

    @pl.when(b == rows - 1)
    def _():
        for slot in REMOTE:
            document(slot).wait_send()
        for slot in range(SLOTS):
            pass_on(slot).wait_send()


def forward(n, owner, doc_slot, places, segments, vectors, doc_store, tokens, cot, pos, weights):
    all_rows, seq, half = tokens.shape
    rows = all_rows // 2
    full = 2 * half
    hidden = 2 * weights[4].shape[1]
    shape = jax.ShapeDtypeStruct
    heads = full // HEAD_DIM
    lse_rows = (heads + 7) // 8 * 8
    vec = shape((VROWS, half), F32)
    own = (cot, pos, vec) + weights
    acts = [
        ((seq, full), BF), ((seq, 3 * full), BF), ((lse_rows, seq), F32), ((seq, full), BF),
        ((seq, full), BF), ((seq, 1), F32), ((seq, full), BF), ((seq, hidden), BF), ((seq, hidden), BF),
        ((seq, full), BF), ((seq, 1), F32), ((seq, full), BF), ((8, PROJ), F32), ((8, PROJ), F32),
    ]
    acts = [shape((rows,) + dims, kind) for dims, kind in acts]
    smem = pl.BlockSpec(memory_space=pltpu.SMEM)
    dma = pltpu.SemaphoreType.DMA
    outs = [shape(o.shape, o.dtype) for o in own] + [vec]
    outs += [shape((count,), jnp.int32) for count in (SLOTS, all_rows, all_rows, 2 * all_rows)]
    result = pl.pallas_call(
        functools.partial(forward_kernel, n),
        out_shape=tuple(outs + acts),
        grid=(rows,),
        in_specs=[smem, smem] + [whole_block(a) for a in (places, segments) + tuple(vectors)] + any_spec(11),
        out_specs=tuple(any_spec(10) + [whole_block(vec)] + [smem] * 4 + [row_block(a) for a in acts]),
        scratch_shapes=[
            pltpu.VMEM((seq, seq), F32), pltpu.VMEM((384, 128), F32), pltpu.VMEM((seq, full), F32),
        ] + whole_scratch(own, "cot", "pos", "vec", "wqkv", "wo", "wi", "wu", "wc") + [
            pltpu.VMEM(doc_store.shape, BF), pltpu.VMEM((SLOTS, seq, half), BF),
            pltpu.VMEM((SLOTS, seq, half), BF), pltpu.VMEM((SLOTS, seq, half), BF),
            pltpu.VMEM(tokens.shape, BF), pltpu.VMEM(tokens.shape, BF),
            pltpu.VMEM((SLOTS, 8, 128), jnp.int32), pltpu.VMEM((SLOTS, 8, 128), jnp.int32),
            pltpu.SMEM((SLOTS, 8, 128), jnp.int32),
            dma((SLOTS,)), dma((SLOTS,)), dma((SLOTS,)), dma((SLOTS,)), dma((SLOTS,)), dma((SLOTS,)),
            dma((11,)), dma((11,)), dma((3,)),
        ],
        compiler_params=pltpu.CompilerParams(
            collective_id=0, has_side_effects=True, vmem_limit_bytes=VMEM_LIMIT
        ),
        name="forward",
    )(owner, doc_slot, places, segments, *vectors, doc_store, tokens, cot, pos, *weights)
    return result[:10], result[10], result[11:15], result[15:]


def norm_back(upstream, normed, inverse, gain):
    scaled = upstream * gain
    first = jnp.mean(scaled, axis=-1, keepdims=True)
    second = jnp.mean(scaled * normed, axis=-1, keepdims=True)
    return inverse * (scaled - first - normed * second)


def add_vec(vecs, row, value):
    half = value.shape[1] // 2
    vecs[0, row:row + 1, :] += value[:, :half]
    vecs[1, row:row + 1, :] += value[:, half:]


def token_sum(values):
    return jnp.sum(values, axis=0, keepdims=True)


def shares_kernel(summ, prod, qv, iout, nout_in, res_in, *refs):
    own, theirs = refs[:10], refs[10:20]
    douter, mixed, vecs, dw_cls, gq = refs[20:25]
    mine, got, nout, res, cot, vec, wc, halves_sem, send_sem, recv_sem, load_sem = refs[25:]
    me = lax.axis_index("dp")
    core = lax.axis_index("mp")
    sibling = (me, 1 - core)
    rows = summ.shape[0]
    halves = Halves(halves_sem)
    spread_halves(halves, own, theirs, vec=vec, cot=cot, wc=wc)
    halves.start()
    loads = [
        pltpu.make_async_copy(res_in, res, load_sem.at[0]),
        pltpu.make_async_copy(nout_in, nout, load_sem.at[1]),
    ]
    for load in loads:
        load.start()
    greet([sibling])
    mine[...] = jnp.concatenate([summ[b, 0:1, :] for b in range(rows)] + [prod[b, 0:1, :] for b in range(rows)], axis=0)
    copy = pltpu.make_async_remote_copy(
        src_ref=mine, dst_ref=got, send_sem=send_sem, recv_sem=recv_sem,
        device_id=sibling, device_id_type=MESH,
    )
    copy.start()
    vecs[...] = jnp.zeros_like(vecs)
    copy.wait()
    first = core == 0
    low = jnp.where(first, mine[...], got[...])
    high = jnp.where(first, got[...], mine[...])
    summary = jnp.concatenate([low[:rows], high[:rows]], axis=0)
    product = jnp.concatenate([low[rows:], high[rows:]], axis=0)
    inv_root = PROJ ** (-0.5)
    logits = jnp.sum(summary * qv[...], axis=1, keepdims=True) * inv_root
    e = jnp.exp(logits - jnp.max(logits, axis=0, keepdims=True))
    share = e / jnp.sum(e, axis=0, keepdims=True)
    dlogits = share * (product - jnp.sum(share * product, axis=0, keepdims=True))
    gq[...] = jnp.sum(dlogits * summary, axis=0, keepdims=True) * inv_root
    ds = dlogits * qv[...] * inv_root
    wide_share = share + jnp.zeros_like(ds)
    shares = jnp.where(first, wide_share, jnp.concatenate([wide_share[rows:], wide_share[:rows]], axis=0))
    dsum = jnp.where(first, ds, jnp.concatenate([ds[rows:], ds[:rows]], axis=0))
    halves.wait("vec")
    halves.wait("cot")
    halves.wait("wc")
    extra = lax.dot_general(
        dsum, wc[...].astype(F32), (((1,), (1,)), ((), ())), preferred_element_type=F32, precision=PRECISE
    )
    for load in loads:
        load.wait()
    seq, full = cot.shape
    heads = jnp.concatenate([res[b, 0:1, :].astype(F32) for b in range(rows)], axis=0)
    heads = jnp.concatenate([heads, jnp.zeros_like(heads)], axis=0)
    dw_cls[...] = lax.dot_general(dsum, heads, (((0,), (0,)), ((), ())), preferred_element_type=F32, precision=PRECISE)
    row = lax.broadcasted_iota(jnp.int32, (seq, 1), 0)
    for b in range(rows):
        share_b = shares[b:b + 1, 0:1]
        part = share_b * res[b].astype(F32)
        mixed[...] = part if b == 0 else mixed[...] + part
        upstream = share_b * cot[...].astype(F32) + jnp.where(row == 0, extra[b:b + 1], 0.0)
        upstream = upstream.astype(BF).astype(F32)
        normed = nout[b].astype(F32)
        dout = norm_back(upstream, normed, iout[b], wide(vec, VGF))
        add_vec(vecs, VGF, token_sum(upstream * normed))
        add_vec(vecs, VSF, token_sum(upstream))
        add_vec(vecs, VBO, token_sum(dout))
        douter[b] = dout.astype(BF)


def share_out(summ, prod, qv, iout, nout, res, own, theirs):
    rows, seq, full = res.shape
    shape = jax.ShapeDtypeStruct
    return pl.pallas_call(
        shares_kernel,
        out_shape=(
            shape((rows, seq, full), BF), shape((seq, full), F32), shape((2, VROWS, full // 2), F32),
            shape((PROJ, full), F32), shape((1, PROJ), F32),
        ),
        in_specs=vmem_spec(4) + any_spec(22),
        out_specs=tuple(vmem_spec(5)),
        scratch_shapes=[
            pltpu.VMEM((2 * rows, PROJ), F32), pltpu.VMEM((2 * rows, PROJ), F32),
            pltpu.VMEM(nout.shape, BF), pltpu.VMEM(res.shape, BF),
        ] + whole_scratch(own, "cot", "vec", "wc") + [
            pltpu.SemaphoreType.DMA, pltpu.SemaphoreType.DMA, pltpu.SemaphoreType.DMA((2,)),
        ],
        compiler_params=pltpu.CompilerParams(collective_id=1, has_side_effects=True, vmem_limit_bytes=VMEM_LIMIT),
        name="shares",
    )(summ, prod, qv, iout, nout, res, *own, *theirs)


def with_bit(index, position, bit):
    low = 1 << position
    return (index // low) * (2 * low) + bit * low + index % low


def across(bit):
    me = lax.axis_index("dp")
    here = (me // (1 << bit)) % 2
    return here, (me + (1 - 2 * here) * (1 << bit), lax.axis_index("mp"))


class Group:
    def __init__(self, n, bits, bufs, sems, index, near, start=0):
        self.n, self.bits, self.near, self.start = n, bits, near, start
        bufs = list(bufs)
        self.mine = bufs.pop(0)
        self.theirs = bufs.pop(0) if start == 0 else None
        self.out, self.came = [None] * start + bufs[0::2], [None] * start + bufs[1::2]
        self.send_sem, self.recv_sem, self.own_sem, self.index = sems[0], sems[1], sems[2], index
        self.levels = len(bits)

    @staticmethod
    def scratch(n, rows, width, kind, start=0):
        levels = n.bit_length() - 1
        shapes = [(n >> start, rows, width)] * (2 if start == 0 else 1)
        for level in range(start, levels):
            shapes += [(n >> (level + 1), rows, width)] * 2
        return [pltpu.VMEM(s, kind) for s in shapes]

    @staticmethod
    def size(n, start=0):
        return (2 if start == 0 else 1) + 2 * (n.bit_length() - 1 - start)

    def remote(self, level, src, dst, target):
        return pltpu.make_async_remote_copy(
            src_ref=src, dst_ref=dst, send_sem=self.send_sem.at[self.index, level],
            recv_sem=self.recv_sem.at[self.index, level], device_id=target, device_id_type=MESH,
        )

    def first(self, src):
        return self.remote(0, src, self.theirs, self.near["sibling"])

    def load_own(self, src):
        return pltpu.make_async_copy(src, self.mine, self.own_sem.at[self.index])

    def hop(self, level):
        return self.remote(level + 1, self.out[level], self.came[level], self.near[self.bits[level]][1])

    def left(self, level):
        return [bit for bit in range(self.levels) if bit not in self.bits[:level]]

    def places(self, level, t, side=0):
        digit = {bit: self.near[bit][0] for bit in self.bits[self.start:level]}
        if level < self.levels:
            digit[self.bits[level]] = side
        for k, bit in enumerate(self.left(level + 1)):
            digit[bit] = (t >> k) & 1
        held = sum(digit[bit] * (1 << k) for k, bit in enumerate(self.left(self.start)))
        came = sum(digit[bit] * (1 << k) for k, bit in enumerate(self.left(level)))
        return held, came

    def advance(self, level):
        came = self.theirs if level == 0 else self.came[level - 1]
        here = self.near[self.bits[level]][0]
        count = self.n >> (level + 1)
        handed = self.start > 0 and level == self.start
        for t in range(count):
            at, of = self.places(level, t, 1 - here)
            self.out[level][t] = self.mine[at] if handed else self.mine[at] + came[of]
        self.hop(level).start()
        if not handed:
            for t in range(count):
                at, of = self.places(level, t, here)
                self.mine[at] = self.mine[at] + came[of]

    def hand_on(self, level, target):
        for t in range(self.n >> level):
            digit = {bit: self.near[bit][0] for bit in self.bits[:level]}
            for k, bit in enumerate(self.left(level)):
                digit[bit] = (t >> k) & 1
            at = sum(digit[bit] * (1 << bit) for bit in range(self.levels))
            target[t] = self.mine[at] + self.came[level - 1][t]

    def total(self):
        at, _ = self.places(self.levels, 0)
        return self.mine[at].astype(F32) + self.came[-1][0].astype(F32)


def bit_orders(n):
    rest = tuple(range(3, n.bit_length() - 1))
    return (0, 1, 2) + rest, (1, 2, 0) + rest, (2, 0, 1) + rest


def neighbours(n):
    near = {bit: across(bit) for bit in range(n.bit_length() - 1)}
    near["core"] = lax.axis_index("mp")
    near["sibling"] = (lax.axis_index("dp"), 1 - near["core"])
    return near


def bit_partners(n, near):
    return [near["sibling"]] + [near[bit][1] for bit in range(n.bit_length() - 1)]


HANDED = 2


class Reducer:
    @staticmethod
    def plan(mats):
        pieces = []
        for index, mat in enumerate(mats):
            if len(mat.shape) == 4:
                pieces += [(index, g * mat.shape[3], mat.shape[3], HANDED) for g in range(mat.shape[0])]
            else:
                half = mat.shape[2] // 2
                width = half // 3
                pieces += [(index, begin, width, 0) for begin in range(0, half, width)]
        return pieces

    @staticmethod
    def scratch(n, mats):
        shapes = []
        pieces = Reducer.plan(mats)
        for index, _, width, start in pieces:
            shapes += Group.scratch(n, mats[index].shape[-2], width, mats[index].dtype, start)
        dma = pltpu.SemaphoreType.DMA
        levels = n.bit_length()
        return shapes + [dma((len(pieces), levels)), dma((len(pieces), levels)), dma((len(pieces),))]

    def __init__(self, n, mats, outs, refs, near):
        self.mats, self.outs, self.near = mats, outs, near
        self.pieces = Reducer.plan(mats)
        orders = bit_orders(n)
        refs = list(refs)
        self.groups = []
        for index, (_, begin, width, start) in enumerate(self.pieces):
            size = Group.size(n, start)
            order = orders[begin // width % 3]
            self.groups.append(Group(n, order, refs[:size], refs[-3:], index, near, start))
            del refs[:size]

    def source(self, index, side):
        mat, begin, width, start = self.pieces[index]
        if start:
            return self.mats[mat].at[begin // width]
        at = side * (self.mats[mat].shape[2] // 2) + begin
        return self.mats[mat].at[:, :, pl.ds(pl.multiple_of(at, 128), width)]

    def start(self):
        core = self.near["core"]
        for index, group in enumerate(self.groups):
            if not group.start:
                group.first(self.source(index, 1 - core)).start()
            group.load_own(self.source(index, core)).start()

    def move(self, mat, level):
        core = self.near["core"]
        for index, group in enumerate(self.groups):
            at, begin, width, start = self.pieces[index]
            if at != mat:
                continue
            if level == start:
                group.load_own(self.source(index, core)).wait()
                if not start:
                    group.first(self.source(index, 1 - core)).wait()
            else:
                group.hop(level - 1).wait()
            if level < group.levels:
                group.advance(level)
            else:
                self.outs[mat][:, begin:begin + width] = group.total()

    def hand_on(self, target):
        for index, group in enumerate(self.groups):
            group.hop(HANDED - 1).wait()
            group.hand_on(HANDED, target.at[index])


FEED_TIMES = ((4, 0), (11, 1))


def feed_back_kernel(n, summed, douter, slope, nmid, imid, vecs_in, *refs):
    refs = list(refs)

    def take(count):
        taken = refs[:count]
        del refs[:count]
        return taken

    own, theirs = take(10), take(10)
    mats = take(1) if summed else []
    dinner, dattn, vecs = take(3)
    handed = take(1) if summed else []
    acc, vec, wi, wu, sems = take(5)
    if summed:
        near = neighbours(n)
        summer = Reducer(n, mats, [], refs, near)
    b = pl.program_id(0)
    halves = Halves(sems)
    spread_halves(halves, own, theirs, vec=vec, wu=wu, wi=wi)

    def need(*names):
        @pl.when(b == 0)
        def _():
            for name in names:
                halves.wait(name)

    full = acc.shape[1]
    half = full // 2
    hidden = wi.shape[1]

    @pl.when(b == 0)
    def _():
        halves.start()
        vecs[...] = vecs_in[...]
        if summed:
            greet(bit_partners(n, near))
            summer.start()

    need("vec", "wu", "wi")
    acc[...] = douter[0].astype(F32)
    parts = 4
    chunk = hidden // parts
    for j in range(parts):
        for step, level in FEED_TIMES if summed else ():
            if step % parts == j:

                @pl.when(b == step // parts)
                def _(level=level):
                    summer.move(0, level)

        cols = slice(j * chunk, (j + 1) * chunk)
        part = nt(douter[0], wu[cols, :]) * slope[0, :, cols].astype(F32)
        dinner[0, :, cols] = part.astype(BF)
        sums = token_sum(part)
        for i in range(2):
            quarter = 2 * j + i
            vecs[quarter // 4, VIN + quarter % 4:VIN + quarter % 4 + 1, :] += sums[:, i * half:(i + 1) * half]
        acc[...] += nt(dinner[0, :, cols], wi[:, cols])
    upstream = acc[...]
    normed = nmid[0].astype(F32)
    middle = norm_back(upstream, normed, imid[0], wide(vec, VGA))
    add_vec(vecs, VGA, token_sum(upstream * normed))
    add_vec(vecs, VSA, token_sum(upstream))
    add_vec(vecs, VO, token_sum(middle))
    dattn[0] = middle.astype(BF)
    if summed:

        @pl.when(b == pl.num_programs(0) - 1)
        def _():
            summer.hand_on(handed[0])


def feed_back(n, douter, slope, nmid, imid, vecs, own, theirs, mats):
    rows, seq, full = douter.shape
    hidden = slope.shape[2]
    shape = jax.ShapeDtypeStruct
    outs = (shape((rows, seq, hidden), BF), shape((rows, seq, full), BF))
    sums = (shape(vecs.shape, F32),)
    by_row = (douter, slope, nmid, imid)
    scratch = [pltpu.VMEM((seq, full), F32)] + whole_scratch(own, "vec", "wi", "wu")
    params = dict(vmem_limit_bytes=VMEM_LIMIT)
    if mats:
        scratch += Reducer.scratch(n, mats)
        params.update(collective_id=3, has_side_effects=True)
        pieces = Reducer.plan(mats)
        sums += (shape((len(pieces), n >> HANDED, mats[0].shape[1], pieces[0][2]), mats[0].dtype),)
    return pl.pallas_call(
        functools.partial(feed_back_kernel, n, bool(mats)),
        out_shape=outs + sums,
        grid=(rows,),
        in_specs=[row_block(a) for a in by_row] + [whole_block(vecs)] + any_spec(20 + len(mats)),
        out_specs=tuple([row_block(a) for a in outs] + [whole_block(a) for a in sums]),
        scratch_shapes=scratch,
        compiler_params=pltpu.CompilerParams(**params),
        name="feed_back",
    )(*by_row, vecs, *own, *theirs, *mats)


SEND_AT = 2
TAIL_TIMES = (
    (3, 0, 2), (7, 0, 3), (7, 1, 0), (8, 2, 0), (8, 3, 0), (14, 0, 4), (18, 1, 1), (18, 2, 1), (18, 3, 1),
)


def tail_kernel(n, mat_count, slot_row, picks, vecs_in, places, segments, dattn, qkv, lse, mixed_in, xlow, *refs):
    refs = list(refs)

    def take(count):
        taken = refs[:count]
        del refs[:count]
        return taken

    own, theirs, mats = take(10), take(10), take(mat_count)
    gt, arrived, mixed, vec_out = take(4)
    spare = [] if mats else take(2)
    sums_out = take(mat_count)
    small_out = take(4) if mats else []
    bias, grads, dqkv, dstart, gt_v, stage, mix_own, mix_got, vecs, vec_far, vec_rows, vec_got, vec_sums, wqkv, wo, halves_sem = take(16)
    own_sem, sib_send, sib_recv, doc_send, doc_recv, vec_send, vec_recv = take(7)
    x_v = outgoing = None
    small = []
    near = neighbours(n)
    if mats:
        x_v, *outgoing = take(5)
        orders = bit_orders(n)
        count = 4 * Group.size(n) + 3
        small_refs = take(count)
        for index in range(4):
            size = Group.size(n)
            bufs = small_refs[index * size:(index + 1) * size]
            small.append(Group(n, orders[(0, 1, 2, 0)[index]], bufs, small_refs[-3:], index, near))
        summer = Reducer(n, mats, sums_out, refs, near)
    b = pl.program_id(0)
    rows = pl.num_programs(0)
    me = lax.axis_index("dp")
    core = near["core"]
    other = 1 - core
    sibling = near["sibling"]
    levels = n.bit_length() - 1
    row_count, _, half = gt_v.shape
    all_rows = row_count // 2
    seq, full = grads.shape
    gang = GANG
    pair = gang * HEAD_DIM
    pairs = full // pair
    halves = Halves(halves_sem)
    spread_halves(halves, own, theirs, wo=wo)
    for index in range(3):
        halves.add("qkv", own[3 + index], theirs[3 + index], wqkv, 1, index * half, 3 * half)
    here_cols = pl.ds(pl.multiple_of(core * half, half), half)
    there_cols = pl.ds(pl.multiple_of(other * half, half), half)
    first_core = core == 0

    def push(row):
        at = pl.ds(pl.multiple_of(row * seq, seq), seq)
        return pltpu.make_async_remote_copy(
            src_ref=dstart.at[at, there_cols], dst_ref=gt_v.at[2 * row + core],
            send_sem=sib_send.at[row], recv_sem=sib_recv.at[row], device_id=sibling, device_id_type=MESH,
        )

    def document(slot):
        if slot == LOCAL:
            return pltpu.make_async_copy(stage.at[slot], arrived.at[slot], own_sem.at[2])
        return pltpu.make_async_remote_copy(
            src_ref=stage.at[slot], dst_ref=arrived.at[slot], send_sem=doc_send.at[slot], recv_sem=doc_recv.at[slot],
            device_id=(lax.rem(me + OFFSETS[slot] + n, n), core), device_id_type=MESH,
        )

    def pack(slot):
        lowest, highest = max(0, slot - (SLOTS - row_count)), min(row_count - 1, slot)
        value = gt_v[lowest]
        for rank in range(lowest + 1, highest + 1):
            value = jnp.where(slot_row[rank] == slot, gt_v[rank], value)
        stage[slot] = value

    mix_far = pltpu.make_async_remote_copy(
        src_ref=mixed_in.at[:, there_cols], dst_ref=mix_got, send_sem=sib_send.at[all_rows],
        recv_sem=sib_recv.at[all_rows], device_id=sibling, device_id_type=MESH,
    )
    mix_load = pltpu.make_async_copy(mixed_in.at[:, here_cols], mix_own, own_sem.at[0])
    x_loads = []
    if mats:
        for r in range(all_rows):
            x_loads.append(pltpu.make_async_copy(xlow.at[r], x_v.at[pl.ds(r * seq, seq)], own_sem.at[3 + r]))

    @pl.when(b == 0)
    def _():
        halves.start()
        vecs[...] = vecs_in[...]
        everyone = [(lax.rem(me + step, n), core) for step in range(1, n)]
        greet((everyone if mats else ring_partners(me, core, n)) + [sibling])
        if mats:
            summer.start()
        mix_far.start()
        mix_load.start()
        for load in x_loads:
            load.start()
        halves.wait("wo")
        halves.wait("qkv")

    grads[...] = nt(dattn[0], wo[...]).astype(BF)
    turn = rows - 1 - b
    seg_row = segments[pl.ds(picks[row_count + 2 * turn + core], 1), :]
    bias[...] = jnp.where(column(seg_row) == seg_row, 0.0, NEGATIVE)
    masks = head_masks(gang)
    my_rows = pl.ds(pl.multiple_of(turn * seq, seq), seq)

    def heads(p):
        for step, mat, level in TAIL_TIMES if mats else ():
            if step % pairs == p:

                @pl.when(b == step // pairs)
                def _(mat=mat, level=level):
                    summer.move(mat, level)

        if p == SEND_AT:
            for row in range(1, all_rows):

                @pl.when(b == row)
                def _(row=row):
                    push(all_rows - row).wait()
                    for slot in (SLOTS - 2 * row, SLOTS - 2 * row + 1):
                        pack(slot)
                        document(slot).start()

        at = p * pair
        queries = qkv[0, :, pl.ds(at, pair)]
        keys = qkv[0, :, pl.ds(full + at, pair)]
        values = qkv[0, :, pl.ds(2 * full + at, pair)]
        dctx = grads[:, pl.ds(at, pair)]
        lane = lax.broadcasted_iota(jnp.int32, (seq, pair), 1)
        keys_all = jnp.concatenate([keys * m for m in masks], axis=0)
        s = nt(keys_all, queries)
        dw = nt(jnp.concatenate([values * m for m in masks], axis=0), dctx)
        ws, dss = [], []
        for h in range(gang):
            w = jnp.exp(s[h * seq:(h + 1) * seq] + bias[...] - lse[0, gang * p + h:gang * p + h + 1, :])
            prod = w * dw[h * seq:(h + 1) * seq]
            dss.append((prod - w * token_sum(prod)).astype(BF))
            ws.append(w.astype(BF))
        ds = jnp.concatenate(dss, axis=0)
        dv = mm(jnp.concatenate(ws, axis=0), dctx)
        dk = mm(ds, queries)
        dq = tn(ds, keys_all) * HEAD_DIM ** -0.5

        def join(parts):
            joined = parts[0:seq]
            for h in range(1, gang):
                joined = jnp.where(lane < h * HEAD_DIM, joined, parts[h * seq:(h + 1) * seq])
            return joined

        for t, value in enumerate((dq, join(dk), join(dv))):
            for i in range(0, pair, 128):
                column = at + i
                out_at = (column // half) * (3 * half) + column % half + t * half
                dqkv[my_rows, pl.ds(out_at, 128)] = value[:, i:i + 128].astype(BF)

    for p in range(pairs):
        heads(p)
    total = dattn[0].astype(F32) + nt(dqkv[my_rows, :], wqkv[...])
    for h in range(2):
        for t, at in ((0, VQ), (2, VV)):
            source = dqkv[my_rows, (3 * h + t) * half:(3 * h + t + 1) * half]
            vecs[h, at:at + 1, :] += token_sum(source.astype(F32))
    low = total.astype(BF)
    dstart[my_rows, :] = low
    gt_v[2 * turn + core] = jnp.where(first_core, total[:, :half], total[:, half:]).astype(BF)
    push(turn).start()

    @pl.when(b == rows - 1)
    def _():
        vec_copy = pltpu.make_async_remote_copy(
            src_ref=vecs.at[other], dst_ref=vec_far, send_sem=vec_send.at[0],
            recv_sem=vec_recv.at[0], device_id=sibling, device_id_type=MESH,
        )
        vec_copy.start()

        def vec_hop(again, step):
            to = lax.rem(me + step, n)
            src, dst = (vec_sums.at[me], vec_sums.at[me]) if again else (vec_rows.at[to], vec_got.at[me])
            return pltpu.make_async_remote_copy(
                src_ref=src, dst_ref=dst, send_sem=vec_send.at[again * n + step], recv_sem=vec_recv.at[again * n + step],
                device_id=(to, core), device_id_type=MESH,
            )

        def vec_out_rows():
            vec_copy.wait()
            held = vecs[core] + vec_far[...]
            depth = held.shape[0] // n
            for i in range(n):
                vec_rows[i] = held[i * depth:(i + 1) * depth]
            for step in range(1, n):
                vec_hop(0, step).start()

        def vec_sum_rows():
            for step in range(1, n):
                vec_hop(0, step).wait()
            total = vec_rows[me]
            for step in range(1, n):
                total = total + vec_got[lax.rem(me + step, n)]
            vec_sums[me] = total
            for step in range(1, n):
                vec_hop(1, step).start()

        def vec_finish():
            for step in range(1, n):
                vec_hop(1, step).wait()
            vec_out[...] = jnp.concatenate([vec_sums[i] for i in range(n)], axis=0)

        if mats:
            vec_out_rows()
        push(0).wait()
        tok_out = pltpu.make_async_copy(gt_v, gt, own_sem.at[1])
        tok_out.start()
        for slot in reversed(range(SLOTS - 2 * all_rows + 2)):
            pack(slot)
        for slot in reversed(range(SLOTS - 2 * all_rows + 2)):
            document(slot).start()

        if not mats:
            vec_copy.wait()
            vec_out[...] = vecs[core] + vec_far[...]
            for source, target in ((dqkv, spare[0]), (dstart, spare[1])):
                copy = pltpu.make_async_copy(source, target, own_sem.at[3])
                copy.start()
                copy.wait()
        else:
            for load in x_loads:
                load.wait()
            table = small_out[3].shape[0] * n
            one_hots = []
            for r in range(all_rows):
                place = places[pl.ds(picks[row_count + 2 * r + core], 1), :]
                here = place == lax.broadcasted_iota(jnp.int32, (table, seq), 0)
                one_hots.append(here.astype(F32).astype(BF))

            def product(index, side, target):
                if index < 3:
                    at = pl.ds(pl.multiple_of(side * 3 * half + index * half, half), half)
                    value = tn(x_v[...], dqkv[:, at])
                else:
                    at = pl.ds(pl.multiple_of(side * half, half), half)
                    value = sum(mm(one_hots[r], dstart[r * seq:(r + 1) * seq, at]) for r in range(all_rows))
                depth = target.shape[1]
                for i in range(n):
                    target[i] = value[i * depth:(i + 1) * depth].astype(target.dtype)

            firsts = []

            def begin(index):
                product(index, other, outgoing[index])
                copy = small[index].first(outgoing[index])
                copy.start()
                firsts.append(copy)
                product(index, core, small[index].mine)

            def step(index, level):
                if level == 0:
                    firsts[index].wait()
                else:
                    small[index].hop(level - 1).wait()
                if level < levels:
                    small[index].advance(level)
                else:
                    small_out[index][...] = small[index].total()

            taken = {}
            for _, mat, level in TAIL_TIMES:
                taken[mat] = max(taken.get(mat, -1), level)
            left = [(mat, level) for level in range(levels + 1) for mat in range(mat_count) if level > taken.get(mat, -1)]

            def some(mat):
                for at, (m, level) in enumerate(left):
                    if m == mat:
                        del left[at]
                        summer.move(mat, level)
                        return

            begin(0)
            begin(1)
            step(0, 0)
            begin(2)
            step(1, 0)
            begin(3)
            step(2, 0)
            step(3, 0)
            vec_sum_rows()
            while left:
                some(left[0][0])
            for level in range(1, levels + 1):
                for index in range(4):
                    step(index, level)
            vec_finish()
        mix_load.wait()
        mix_far.wait()
        mixed[...] = (mix_own[...] + mix_got[...]).astype(BF)
        tok_out.wait()
        for slot in range(SLOTS):
            document(slot).wait()


def tail(n, table, slot_of, picks, vecs, places, segments, dattn, qkv, lse, mixed, xlow, own, theirs, mats):
    rows, seq, full = dattn.shape
    half = full // 2
    tokens = rows * seq
    levels = n.bit_length() - 1
    shape = jax.ShapeDtypeStruct
    outs = [shape((2 * rows, seq, half), BF), shape((SLOTS, seq, half), BF), shape((seq, half), BF), shape(vecs.shape[1:], F32)]
    if not mats:
        outs += [shape((tokens, 3 * full), BF), shape((tokens, full), BF)]
    out_specs = any_spec(2) + [whole_block(o) for o in outs[2:4]] + any_spec(len(outs) - 4)
    by_row = (dattn, qkv, lse)
    dma = pltpu.SemaphoreType.DMA
    scratch = [
        pltpu.VMEM((seq, seq), F32), pltpu.VMEM((seq, full), BF), pltpu.VMEM((tokens, 3 * full), BF),
        pltpu.VMEM((tokens, full), BF), pltpu.VMEM((2 * rows, seq, half), BF), pltpu.VMEM((SLOTS, seq, half), BF),
        pltpu.VMEM((seq, half), F32), pltpu.VMEM((seq, half), F32), pltpu.VMEM(vecs.shape, F32),
        pltpu.VMEM(vecs.shape[1:], F32),
    ] + [pltpu.VMEM((n, max(1, vecs.shape[1] // n), half), F32)] * 3 + whole_scratch(own, "wqkv", "wo") + [
        dma((3 + rows,)), dma((rows + 1,)), dma((rows + 1,)), dma((SLOTS,)), dma((SLOTS,)), dma((2 * n,)), dma((2 * n,)),
    ]
    if mats:
        depths = [full // n] * 3 + [table // n]
        scratch += [pltpu.VMEM((tokens, full), BF)] + [pltpu.VMEM((n, depth, half), BF) for depth in depths]
        for depth in depths:
            scratch += Group.scratch(n, depth, half, BF)
        scratch += [dma((4, levels + 1)), dma((4, levels + 1)), dma((4,))]
        scratch += Reducer.scratch(n, mats)
        sums = [shape((m.shape[-2], m.shape[0] * m.shape[3] if len(m.shape) == 4 else m.shape[2] // 2), F32) for m in mats] + [shape((depth, half), F32) for depth in depths]
        outs += sums
        out_specs += [whole_block(o) for o in sums]
    return pl.pallas_call(
        functools.partial(tail_kernel, n, len(mats)),
        out_shape=tuple(outs),
        grid=(rows,),
        in_specs=[pl.BlockSpec(memory_space=pltpu.SMEM)] * 2 + [whole_block(a) for a in (vecs, places, segments)]
        + [row_back(a) for a in by_row] + any_spec(22 + len(mats)),
        out_specs=tuple(out_specs),
        scratch_shapes=scratch,
        compiler_params=pltpu.CompilerParams(
            collective_id=2, has_side_effects=True, vmem_limit_bytes=VMEM_LIMIT
        ),
        name="tail",
    )(slot_of, picks, vecs, places, segments, *by_row, mixed, xlow, *own, *theirs, *mats)


FINISHED = ("mixed", "pos", "wq", "wk", "wv", "wo", "inner", "outer", "cls", "gq")


def finish_kernel(names, want, rank, arrived, gt, vec_sum, *refs):
    refs = list(refs)

    def take(count):
        taken = refs[:count]
        del refs[:count]
        return taken

    ins, (docs_out, tokens_out) = take(len(names)), take(2)
    outs, vectors = take(len(names)), take(9)
    got, total, tok, sems = refs
    docs = docs_out.shape[0]
    row_count, _, half = tokens_out.shape
    loads = [pltpu.make_async_copy(arrived.at[slot], got.at[slot], sems.at[slot]) for slot in range(SLOTS)]
    tok_loads = [pltpu.make_async_copy(gt.at[jnp.minimum(rank[k], row_count - 1)], tok.at[k], sems.at[SLOTS + 1 + k]) for k in range(row_count)]
    for load in tok_loads + loads:
        load.start()

    def clear(d, carry):
        total[d] = jnp.zeros(total.shape[1:], F32)
        return carry

    lax.fori_loop(0, docs, clear, 0)
    for load in tok_loads:
        load.wait()
    tok_done = pltpu.make_async_copy(tok, tokens_out, sems.at[SLOTS + 1])
    tok_done.start()
    for slot in range(SLOTS):
        loads[slot].wait()
        at = jnp.where(want[slot] < 0, docs, jnp.minimum(want[slot], docs))
        total[at] += got[slot].astype(F32)
    done = pltpu.make_async_copy(total.at[pl.ds(0, docs)], docs_out, sems.at[SLOTS])
    done.start()
    for name, source, target in zip(names, ins, outs):
        if name == "mixed":
            target[0] = source[...]
        else:
            target[...] = source[...]
    for index, vector in enumerate(vectors):
        for i in range(vector.shape[0] // half):
            vector[i * half:(i + 1) * half] = vec_sum[index + i]
    tok_done.wait()
    done.wait()


def finish(docs, want, rank, arrived, gt, vec_sum, named):
    _, seq, half = arrived.shape
    shape = jax.ShapeDtypeStruct
    names = tuple(named)
    outs = [shape((docs, seq, half), F32), shape(gt.shape, BF)]
    for name, value in named.items():
        outs.append(shape(((1,) if name == "mixed" else ()) + value.shape, value.dtype))
    outs += [shape((half * (4 if index == VIN else 1),), F32) for index in range(9)]
    smem = pl.BlockSpec(memory_space=pltpu.SMEM)
    grad_docs, grad_tokens, *rest = pl.pallas_call(
        functools.partial(finish_kernel, names),
        out_shape=tuple(outs),
        in_specs=[smem, smem] + any_spec(2) + vmem_spec(1 + len(names)),
        out_specs=tuple(any_spec(2) + vmem_spec(len(outs) - 2)),
        scratch_shapes=[
            pltpu.VMEM(arrived.shape, BF), pltpu.VMEM((docs + 1, seq, half), F32), pltpu.VMEM(gt.shape, BF),
            pltpu.SemaphoreType.DMA((SLOTS + 1 + gt.shape[0],)),
        ],
        compiler_params=pltpu.CompilerParams(vmem_limit_bytes=VMEM_LIMIT),
        name="finish",
    )(want, rank, arrived, gt, vec_sum, *named.values())
    return grad_docs, grad_tokens, dict(zip(names, rest)), rest[len(names):]


def body(
    tokens, segment_ids, positions, query_vectors, doc_owner, doc_slot, doc_store, pos_table,
    w_query, w_key, w_value, b_query, b_value, w_out, b_out, gain_attn, shift_attn,
    w_inner, b_inner, w_outer, b_outer, gain_ffn, shift_ffn, w_cls, cotangent,
):
    n = lax.axis_size("dp")
    core = lax.axis_index("mp")
    row_count, _, half = tokens.shape
    full = 2 * half
    weights = (w_query, w_key, w_value, w_out, w_inner, w_outer, w_cls)
    vectors = (b_query, b_value, b_out, gain_attn, shift_attn, b_outer, gain_ffn, shift_ffn, b_inner)
    theirs, vec_own, (want, rank, slot_of, picks), acts = forward(
        n, doc_owner, doc_slot, positions, segment_ids, vectors, doc_store, tokens, cotangent[0], pos_table, weights
    )
    own = (cotangent[0], pos_table, vec_own) + weights
    xlow, qkv, lse, ctx, nmid, imid, mlow, act, slope, nout, iout, res, summ, prod = acts

    douter, mixed, vecs, dw_cls, grad_query = share_out(summ, prod, query_vectors, iout, nout, res, own, theirs)

    def cross(left, right):
        left = left.reshape(-1, left.shape[-1])
        right = right.reshape(-1, right.shape[-1])
        return tn(left, right)

    def cut(part, kind):
        return part.astype(kind).reshape(n, part.shape[0] // n, part.shape[1])

    summed = full // n % 16 == 0
    table = pos_table.shape[0]
    dw_outer = cross(douter, act)
    dinner, dattn, vecs, *handed = feed_back(
        n, douter, slope, nmid, imid, vecs, own, theirs, [cut(dw_outer, BF)] if summed else []
    )
    dw_inner, dw_out = cross(mlow, dinner), cross(dattn, ctx)
    mats = handed + [cut(dw_inner, BF), cut(dw_out, BF), cut(dw_cls, F32)] if summed else []
    grad_tokens, arrived, mixed_out, vec_sum, *sums = tail(
        n, table, slot_of, picks, vecs, positions, segment_ids, dattn, qkv, lse, mixed, xlow, own, theirs, mats
    )
    if summed:
        g_outer, g_inner, g_wo, g_cls, g_q, g_k, g_v, g_pos = sums
    else:
        vec_sum = lax.psum(vec_sum, "dp")
        dqkv, dstart = sums
        place = jnp.take(positions, picks[row_count:].reshape(-1, 2)[:, core], axis=0, mode="clip")
        one_hot = (place.reshape(-1)[:, None] == jnp.arange(table, dtype=jnp.int32)[None, :]).astype(BF)

        def scatter(part):
            part = lax.psum_scatter(part.astype(F32), "mp", scatter_dimension=1, tiled=True)
            return lax.psum_scatter(part, "dp", scatter_dimension=0, tiled=True)

        g_outer, g_inner, g_wo, g_qkv, g_cls, g_pos = [
            scatter(p) for p in (dw_outer, dw_inner, dw_out, cross(xlow, dqkv), dw_cls, cross(one_hot, dstart))
        ]
        g_q, g_k, g_v = g_qkv[:, :half], g_qkv[:, half:2 * half], g_qkv[:, 2 * half:]
    named = dict(zip(FINISHED, (mixed_out, g_pos, g_q, g_k, g_v, g_wo, g_inner, g_outer, g_cls, grad_query)))
    grad_docs, grad_tokens, out, vec = finish(doc_store.shape[0], want, rank, arrived, grad_tokens, vec_sum, named)
    return (
        out["mixed"], grad_tokens, out["gq"], grad_docs, out["pos"], out["wq"], out["wk"], out["wv"], vec[VQ], vec[VV],
        out["wo"].T, vec[VO], vec[VGA], vec[VSA], out["inner"], vec[VIN], out["outer"].T, vec[VBO], vec[VGF], vec[VSF],
        out["cls"].T,
    )


def solution(mesh):
    rows = P("dp", None, "mp")
    ids = P("dp", None)
    cols = P(None, "mp")
    vec = P("mp")
    deep = P("mp", None)
    in_specs = (
        rows, ids, ids, ids, ids, ids, rows, cols, cols, cols, cols, vec, vec, deep, vec, vec, vec,
        cols, vec, deep, vec, vec, vec, deep, rows,
    )
    near = P("dp", "mp")
    turned = P("mp", "dp")
    out_specs = (
        rows, rows, ids, rows, near, near, near, near, vec, vec, turned, vec, vec, vec, near, vec,
        turned, vec, vec, vec, turned,
    )
    return jax.shard_map(body, mesh=mesh, in_specs=in_specs, out_specs=out_specs, check_vma=False)
```

```python
import functools

import jax
import jax.numpy as jnp
from jax import lax
from jax.experimental import pallas as pl
from jax.experimental.pallas import tpu as pltpu
from jax.sharding import PartitionSpec as P

HEAD_DIM = 64
PROJ = 128
REACH = 6
SLOTS = 2 * REACH
OFFSETS = (0, 1, -1, 2, -2, -4, -3, 4, 3, -5, 5, -6)
LOCAL = 0
REMOTE = tuple(range(1, SLOTS))
EPSILON = 1e-05
NEGATIVE = -1e30
PRECISE = lax.Precision.HIGHEST
MESH = pl.DeviceIdType.MESH
BF = jnp.bfloat16
F32 = jnp.float32
VMEM_LIMIT = 60 * 1024 * 1024
VQ, VV, VO, VGA, VSA, VBO, VGF, VSF, VIN = range(9)
VROWS = 16
GANG = 2


def any_spec(count):
    return [pl.BlockSpec(memory_space=pl.ANY)] * count


def vmem_spec(count):
    return [pl.BlockSpec(memory_space=pltpu.VMEM)] * count


def row_block(array):
    dims = array.shape[1:]
    return pl.BlockSpec((1,) + dims, lambda b: (b,) + (0,) * len(dims))


def row_back(array):
    dims = array.shape[1:]
    last = array.shape[0] - 1
    return pl.BlockSpec((1,) + dims, lambda b: (last - b,) + (0,) * len(dims))


def whole_block(array):
    dims = array.shape
    return pl.BlockSpec(dims, lambda b: (0,) * len(dims), pipeline_mode=pl.Buffered(1))


def nt(left, right):
    return lax.dot_general(left, right, (((1,), (1,)), ((), ())), preferred_element_type=F32)


def tn(left, right):
    return lax.dot_general(left, right, (((0,), (0,)), ((), ())), preferred_element_type=F32)


def mm(left, right):
    return jnp.dot(left, right, preferred_element_type=F32)


def greet(targets):
    barrier = pltpu.get_barrier_semaphore()
    for target in targets:
        pl.semaphore_signal(barrier, inc=1, device_id=target, device_id_type=MESH)
    pl.semaphore_wait(barrier, len(targets))


def ring_partners(me, core, n):
    return [(lax.rem(me + step + n, n), core) for step in range(-REACH, REACH + 1) if step != 0]


class Halves:
    def __init__(self, sems):
        self.sems, self.copies, self.names = sems, [], {}

    def add(self, name, own, theirs, whole, axis, offset=0, stride=None):
        core = lax.axis_index("mp")
        size = own.shape[axis] if axis is not None else 1
        for source, side in ((own, core), (theirs, 1 - core)):
            if axis is None:
                target = whole.at[side]
            else:
                begin = offset + side * (stride or size)
                at = pl.ds(pl.multiple_of(begin, 128), size)
                target = whole.at[at] if axis == 0 else whole.at[:, at]
            copy = pltpu.make_async_copy(source, target, self.sems.at[len(self.copies)])
            self.copies.append(copy)
            self.names.setdefault(name, []).append(copy)

    def add_chunks(self, name, own, theirs, whole, axis):
        core = lax.axis_index("mp")
        size = whole.shape[1] // 2
        for j in range(whole.shape[0]):
            for source, side in ((own, core), (theirs, 1 - core)):
                to = pl.ds(pl.multiple_of(side * size, 128), size)
                part = pl.ds(j * size, size)
                source_part, target = (source.at[part], whole.at[j, to]) if axis == 0 else (source.at[:, part], whole.at[j, :, to])
                copy = pltpu.make_async_copy(source_part, target, self.sems.at[len(self.copies)])
                self.copies.append(copy)
                self.names.setdefault(name, []).append(copy)

    def start(self):
        self.start_own()
        self.start_theirs()

    def start_own(self):
        for copy in self.copies[0::2]:
            copy.start()

    def start_theirs(self):
        for copy in self.copies[1::2]:
            copy.start()

    def wait(self, name):
        for copy in self.names[name]:
            copy.wait()


def wide(vec, row):
    return jnp.concatenate([vec[0, row:row + 1, :], vec[1, row:row + 1, :]], axis=1)


def normalize(hidden):
    average = jnp.mean(hidden, axis=-1, keepdims=True)
    centered = hidden - average
    spread = jnp.mean(centered * centered, axis=-1, keepdims=True)
    inverse = lax.rsqrt(spread + EPSILON)
    return centered * inverse, inverse


def column(row):
    size = row.shape[1]
    here = lax.broadcasted_iota(jnp.int32, (size, size), 0) == lax.broadcasted_iota(jnp.int32, (size, size), 1)
    return jnp.sum(jnp.where(here, row, 0), axis=1, keepdims=True)


def head_masks(count):
    lane = lax.broadcasted_iota(jnp.int32, (1, count * HEAD_DIM), 1) // HEAD_DIM
    return [(lane == h).astype(F32).astype(BF) for h in range(count)]


def spread_halves(halves, own, theirs, **whole):
    places = {"cot": (0, 1), "pos": (1, 1), "vec": (2, None), "wo": (6, 0), "wi": (7, 1), "wu": (8, 0), "wc": (9, 0)}
    for name, ref in whole.items():
        if name == "wqkv":
            for index in range(3):
                halves.add("qkv", own[3 + index], theirs[3 + index], ref, 1, index * ref.shape[0])
        elif name in ("wi", "wu"):
            at, axis = places[name]
            halves.add_chunks(name, own[at], theirs[at], ref, axis)
        else:
            at, axis = places[name]
            halves.add(name, own[at], theirs[at], ref, axis)


def whole_scratch(own, *names):
    cot, pos, vec, wq, _, _, wo, wi, wu, wc = own
    full = wq.shape[0]
    shapes = {
        "cot": ((cot.shape[0], full), BF), "pos": ((pos.shape[0], full), BF), "vec": ((2,) + vec.shape, F32),
        "wqkv": ((full, 3 * full), BF), "wo": ((full, full), BF), "wi": ((2 * wi.shape[1] // full, full, full), BF),
        "wu": ((2 * wu.shape[0] // full, full, full), BF), "wc": ((full, wc.shape[1]), BF),
    }
    return [pltpu.VMEM(*shapes[name]) for name in names] + [pltpu.SemaphoreType.DMA((40,))]


LATE_START = 4
LATE_AT = 2
LATE_FIRST = 4


def forward_kernel(n, owner, doc_slot, places, segments, *refs):
    refs = list(refs)

    def take(count):
        taken = refs[:count]
        del refs[:count]
        return taken

    vectors = take(9)
    docs_in, tok_in, cot_in, pos_in = take(4)
    weights_in = take(7)
    theirs = take(10)
    vec_own, want, rank_out, slot_of, picks = take(5)
    xlow, qkv, lse, ctx, nmid, imid, mlow, act, slope, nout, iout, res, summ, prod = take(14)
    bias, stats, acc, cot, pos, vec, wqkv, wo, wi, wu, wc, sems = take(12)
    doc_buf, stage, docs, docs_sib, tok, tok_sib, req, got, got_s = take(9)
    req_send, req_recv, doc_send, doc_recv, fwd_send, fwd_recv, sib_send, sib_recv, misc_sem = take(9)
    own = [cot_in, pos_in, vec_own] + weights_in
    b = pl.program_id(0)
    rows = pl.num_programs(0)
    me = lax.axis_index("dp")
    core = lax.axis_index("mp")
    sibling = (me, 1 - core)
    seq, full = acc.shape
    row_count, _, half = tok_in.shape
    all_rows = row_count // 2
    early = SLOTS - row_count + 2
    halves = Halves(sems)
    spread_halves(halves, own, theirs, pos=pos, vec=vec, wqkv=wqkv, wo=wo, wi=wi, wu=wu, wc=wc, cot=cot)
    fresh = b == 0

    def request(slot):
        return pltpu.make_async_remote_copy(
            src_ref=req.at[slot], dst_ref=got.at[slot], send_sem=req_send.at[slot], recv_sem=req_recv.at[slot],
            device_id=(lax.rem(me + OFFSETS[slot] + n, n), core), device_id_type=MESH,
        )

    def document(slot):
        return pltpu.make_async_remote_copy(
            src_ref=stage.at[slot], dst_ref=docs.at[slot], send_sem=doc_send.at[slot], recv_sem=doc_recv.at[slot],
            device_id=(lax.rem(me - OFFSETS[slot] + n, n), core), device_id_type=MESH,
        )

    def pass_on(slot):
        return pltpu.make_async_remote_copy(
            src_ref=docs.at[slot], dst_ref=docs_sib.at[slot], send_sem=fwd_send.at[slot], recv_sem=fwd_recv.at[slot],
            device_id=sibling, device_id_type=MESH,
        )

    sources = [tok_in, pos_in, vec_own] + weights_in + [cot_in]
    targets = [tok_sib] + theirs[1:] + [theirs[0]]

    def share(index):
        return pltpu.make_async_remote_copy(
            src_ref=sources[index], dst_ref=targets[index], send_sem=sib_send.at[index], recv_sem=sib_recv.at[index],
            device_id=sibling, device_id_type=MESH,
        )

    doc_load = pltpu.make_async_copy(docs_in, doc_buf, misc_sem.at[0])
    tok_load = pltpu.make_async_copy(tok_in, tok, misc_sem.at[1])
    to_scalar = pltpu.make_async_copy(got, got_s, misc_sem.at[2])

    @pl.when(fresh)
    def _():
        doc_load.start()
        one = jnp.int32(1)
        zero = jnp.int32(0)
        offsets = [lax.rem(owner[0, k] - me + REACH + n, n) - REACH for k in range(row_count)]
        slots = [sum(jnp.where(o == OFFSETS[slot], slot * one, zero) for slot in range(SLOTS)) for o in offsets]
        ranks = []
        for k in range(row_count):
            ranks.append(sum(jnp.where(slots[j] < slots[k], one, zero) for j in range(row_count) if j != k))
            rank_out[k] = ranks[k]
        for slot in range(SLOTS):
            asked_for = sum(jnp.where(slots[k] == slot, doc_slot[0, k] + 1, zero) for k in range(row_count)) - 1
            req[slot] = jnp.full(req.shape[1:], asked_for, jnp.int32)
        vec_own[...] = jnp.zeros_like(vec_own)
        for index, vector in enumerate(vectors):
            for i in range(vector.shape[0] // half):
                vec_own[index + i] = vector[i * half:(i + 1) * half]
        greet(ring_partners(me, core, n) + [sibling])
        for slot in REMOTE:
            request(slot).start()
        for index in range(len(sources)):
            share(index).start()
        tok_load.start()
        halves.start_own()
        for rank in range(row_count):
            slot = sum(jnp.where(ranks[k] == rank, slots[k], zero) for k in range(row_count))
            row = sum(jnp.where(ranks[k] == rank, k * one, zero) for k in range(row_count))
            slot_of[rank] = slot
            picks[rank] = slot
            picks[row_count + rank] = jnp.minimum(row, row_count - 1)
        got[LOCAL] = req[LOCAL]
        for slot in REMOTE:
            request(slot).wait()
        to_scalar.start()
        doc_load.wait()
        to_scalar.wait()
        for slot in range(SLOTS):
            want[slot] = got_s[slot, 0, 0]
        for slot in REMOTE[:early - 1]:
            stage[slot] = doc_buf[jnp.clip(got_s[slot, 0, 0], 0, doc_buf.shape[0] - 1)]
            document(slot).start()
        docs[LOCAL] = doc_buf[jnp.clip(got_s[LOCAL, 0, 0], 0, doc_buf.shape[0] - 1)]
        pass_on(LOCAL).start()
        for slot in range(early, SLOTS):
            stage[slot] = doc_buf[jnp.clip(got_s[slot, 0, 0], 0, doc_buf.shape[0] - 1)]
        for index in range(len(sources)):
            share(index).wait()
        halves.start_theirs()
        tok_load.wait()
        for slot in REMOTE[:early - 1]:
            document(slot).wait_recv()
            pass_on(slot).start()
            if slot == LATE_START:
                for late in range(early, early + LATE_FIRST):
                    document(late).start()
        for slot in range(early):
            pass_on(slot).wait_recv()

    for step in range(1, all_rows):

        @pl.when(b == step)
        def _(step=step):
            for slot in range(early + 2 * step - 2, early + 2 * step):
                pass_on(slot).wait_recv()

    def take_late(step):
        for slot in range(early + 2 * step, early + 2 * step + 2):
            document(slot).wait_recv()
            pass_on(slot).start()
        for slot in range(early + LATE_FIRST + 2 * step, min(SLOTS, early + LATE_FIRST + 2 * step + 2)):
            document(slot).start()

    def need(*names):
        @pl.when(fresh)
        def _():
            for name in names:
                halves.wait(name)

    first = core == 0
    my_rank = 2 * b + core

    def join(a, b):
        a, b = a.astype(F32), b.astype(F32)
        return jnp.concatenate([jnp.where(first, a, b), jnp.where(first, b, a)], axis=1)

    def chosen(held):
        value = held[my_rank]
        for i in range(1, SLOTS - row_count + 1):
            value = jnp.where(picks[my_rank] == my_rank + i, held[my_rank + i], value)
        return value

    need("pos", "vec")
    table = pos.shape[0]
    row = picks[row_count + my_rank]
    seg_row = segments[pl.ds(row, 1), :]
    one_hot = (column(places[pl.ds(row, 1), :]) == lax.broadcasted_iota(jnp.int32, (seq, table), 1)).astype(F32).astype(BF)
    embedded = join(tok[row], tok_sib[row]) + mm(one_hot, pos[...]) + join(chosen(docs), chosen(docs_sib))
    low = embedded.astype(BF)
    xlow[0] = low
    acc[...] = embedded
    need("qkv")
    q = (mm(low, wqkv[:, 0:full]) + wide(vec, VQ)).astype(BF)
    qkv[0, :, 0:full] = q * jnp.asarray(HEAD_DIM ** -0.5, BF)
    qkv[0, :, full:2 * full] = mm(low, wqkv[:, full:2 * full]).astype(BF)
    qkv[0, :, 2 * full:] = (mm(low, wqkv[:, 2 * full:]) + wide(vec, VV)).astype(BF)
    bias[...] = jnp.where(column(seg_row) == seg_row, 0.0, NEGATIVE)
    stats[...] = jnp.zeros_like(stats)
    masks = head_masks(GANG)
    wide_gang = GANG * HEAD_DIM

    def heads(p, carry):
        at = pl.multiple_of(p * wide_gang, wide_gang)
        queries = qkv[0, :, pl.ds(at, wide_gang)]
        keys = qkv[0, :, pl.ds(full + at, wide_gang)]
        values = qkv[0, :, pl.ds(2 * full + at, wide_gang)]
        lane = lax.broadcasted_iota(jnp.int32, (seq, wide_gang), 1)
        small_lane = lax.broadcasted_iota(jnp.int32, (seq, 128), 1)
        s = nt(jnp.concatenate([queries * m for m in masks], axis=0), keys)
        es, totals = [], []
        for h in range(GANG):
            sh = s[h * seq:(h + 1) * seq] + bias[...]
            top = jnp.max(sh, axis=1, keepdims=True)
            e = jnp.exp(sh - top)
            total = jnp.sum(e, axis=1, keepdims=True)
            es.append(e.astype(BF))
            totals.append(1.0 / total)
            stats[0:seq, :] = jnp.where(small_lane == GANG * p + h, top + jnp.log(total), stats[0:seq, :])
        out = mm(jnp.concatenate(es, axis=0), values)
        joined = out[0:seq] * totals[0]
        for h in range(1, GANG):
            joined = jnp.where(lane < h * HEAD_DIM, joined, out[h * seq:(h + 1) * seq] * totals[h])
        ctx[0, :, pl.ds(at, wide_gang)] = joined.astype(BF)
        return carry

    lax.fori_loop(0, full // wide_gang, heads, 0, unroll=3)
    lse[0] = jnp.transpose(stats[...])[0:lse.shape[1], 0:seq]
    need("wo")
    normed, inverse = normalize(acc[...] + mm(ctx[0], wo[...]) + wide(vec, VO))
    middle = normed * wide(vec, VGA) + wide(vec, VSA)
    nmid[0] = normed.astype(BF)
    imid[0] = inverse
    acc[...] = middle + wide(vec, VBO)
    mlow[0] = middle.astype(BF)
    need("wi", "wu", "wc", "cot")
    for j in range(wi.shape[0]):
        if j == LATE_AT:
            for step in range(all_rows - 1):

                @pl.when(b == step)
                def _(step=step):
                    take_late(step)

        pre = mm(mlow[0], wi[j]) + wide(vec, VIN + j)
        phi = 0.5 + 0.5 * lax.erf(pre * (0.5 ** 0.5))
        act[0, j] = (pre * phi).astype(BF)
        slope[0, j] = (phi + pre * (jnp.exp(-0.5 * pre * pre) * 0.3989422804014327)).astype(BF)
        acc[...] += mm(act[0, j], wu[j])
    normed, inverse = normalize(acc[...])
    nout[0] = normed.astype(BF)
    iout[0] = inverse
    result = (normed * wide(vec, VGF) + wide(vec, VSF)).astype(BF)
    res[0] = result
    summ[0] = mm(res[0, 0:16, :], wc[...])[0:8]
    product = jnp.sum(cot[...].astype(F32) * result.astype(F32))
    prod[0] = jnp.full(prod.shape[1:], product, F32)

    @pl.when(b == rows - 1)
    def _():
        for slot in REMOTE:
            document(slot).wait_send()
        for slot in range(SLOTS):
            pass_on(slot).wait_send()


def forward(n, owner, doc_slot, places, segments, vectors, doc_store, tokens, cot, pos, weights):
    all_rows, seq, half = tokens.shape
    rows = all_rows // 2
    full = 2 * half
    hidden = 2 * weights[4].shape[1]
    shape = jax.ShapeDtypeStruct
    heads = full // HEAD_DIM
    lse_rows = (heads + 7) // 8 * 8
    vec = shape((VROWS, half), F32)
    own = (cot, pos, vec) + weights
    acts = [
        ((seq, full), BF), ((seq, 3 * full), BF), ((lse_rows, seq), F32), ((seq, full), BF),
        ((seq, full), BF), ((seq, 1), F32), ((seq, full), BF), ((hidden // full, seq, full), BF), ((hidden // full, seq, full), BF),
        ((seq, full), BF), ((seq, 1), F32), ((seq, full), BF), ((8, PROJ), F32), ((8, PROJ), F32),
    ]
    acts = [shape((rows,) + dims, kind) for dims, kind in acts]
    smem = pl.BlockSpec(memory_space=pltpu.SMEM)
    dma = pltpu.SemaphoreType.DMA
    outs = [shape(o.shape, o.dtype) for o in own] + [vec]
    outs += [shape((count,), jnp.int32) for count in (SLOTS, all_rows, all_rows, 2 * all_rows)]
    result = pl.pallas_call(
        functools.partial(forward_kernel, n),
        out_shape=tuple(outs + acts),
        grid=(rows,),
        in_specs=[smem, smem] + [whole_block(a) for a in (places, segments) + tuple(vectors)] + any_spec(11),
        out_specs=tuple(any_spec(10) + [whole_block(vec)] + [smem] * 4 + [row_block(a) for a in acts]),
        scratch_shapes=[
            pltpu.VMEM((seq, seq), F32), pltpu.VMEM((384, 128), F32), pltpu.VMEM((seq, full), F32),
        ] + whole_scratch(own, "cot", "pos", "vec", "wqkv", "wo", "wi", "wu", "wc") + [
            pltpu.VMEM(doc_store.shape, BF), pltpu.VMEM((SLOTS, seq, half), BF),
            pltpu.VMEM((SLOTS, seq, half), BF), pltpu.VMEM((SLOTS, seq, half), BF),
            pltpu.VMEM(tokens.shape, BF), pltpu.VMEM(tokens.shape, BF),
            pltpu.VMEM((SLOTS, 8, 128), jnp.int32), pltpu.VMEM((SLOTS, 8, 128), jnp.int32),
            pltpu.SMEM((SLOTS, 8, 128), jnp.int32),
            dma((SLOTS,)), dma((SLOTS,)), dma((SLOTS,)), dma((SLOTS,)), dma((SLOTS,)), dma((SLOTS,)),
            dma((11,)), dma((11,)), dma((3,)),
        ],
        compiler_params=pltpu.CompilerParams(
            collective_id=0, has_side_effects=True, vmem_limit_bytes=VMEM_LIMIT
        ),
        name="forward",
    )(owner, doc_slot, places, segments, *vectors, doc_store, tokens, cot, pos, *weights)
    return result[:10], result[10], result[11:15], result[15:]


def norm_back(upstream, normed, inverse, gain):
    scaled = upstream * gain
    first = jnp.mean(scaled, axis=-1, keepdims=True)
    second = jnp.mean(scaled * normed, axis=-1, keepdims=True)
    return inverse * (scaled - first - normed * second)


def add_vec(vecs, row, value):
    half = value.shape[1] // 2
    vecs[0, row:row + 1, :] += value[:, :half]
    vecs[1, row:row + 1, :] += value[:, half:]


def token_sum(values):
    return jnp.sum(values, axis=0, keepdims=True)


def spread(value, target):
    _, n, depth, width = target.shape
    for side in range(2):
        for i in range(n):
            target[side, i] = value[i * depth:(i + 1) * depth, side * width:(side + 1) * width].astype(target.dtype)


def shares_kernel(summ, prod, qv, iout, nout_in, res_in, *refs):
    own, theirs = refs[:10], refs[10:20]
    douter, mixed, vecs, dw_cls, gq = refs[20:25]
    mine, got, nout, res, cot, vec, wc, halves_sem, send_sem, recv_sem, load_sem = refs[25:]
    me = lax.axis_index("dp")
    core = lax.axis_index("mp")
    sibling = (me, 1 - core)
    rows = summ.shape[0]
    halves = Halves(halves_sem)
    spread_halves(halves, own, theirs, vec=vec, cot=cot, wc=wc)
    halves.start()
    loads = [
        pltpu.make_async_copy(res_in, res, load_sem.at[0]),
        pltpu.make_async_copy(nout_in, nout, load_sem.at[1]),
    ]
    for load in loads:
        load.start()
    greet([sibling])
    mine[...] = jnp.concatenate([summ[b, 0:1, :] for b in range(rows)] + [prod[b, 0:1, :] for b in range(rows)], axis=0)
    copy = pltpu.make_async_remote_copy(
        src_ref=mine, dst_ref=got, send_sem=send_sem, recv_sem=recv_sem,
        device_id=sibling, device_id_type=MESH,
    )
    copy.start()
    vecs[...] = jnp.zeros_like(vecs)
    copy.wait()
    first = core == 0
    low = jnp.where(first, mine[...], got[...])
    high = jnp.where(first, got[...], mine[...])
    summary = jnp.concatenate([low[:rows], high[:rows]], axis=0)
    product = jnp.concatenate([low[rows:], high[rows:]], axis=0)
    inv_root = PROJ ** (-0.5)
    logits = jnp.sum(summary * qv[...], axis=1, keepdims=True) * inv_root
    e = jnp.exp(logits - jnp.max(logits, axis=0, keepdims=True))
    share = e / jnp.sum(e, axis=0, keepdims=True)
    dlogits = share * (product - jnp.sum(share * product, axis=0, keepdims=True))
    gq[...] = jnp.sum(dlogits * summary, axis=0, keepdims=True) * inv_root
    ds = dlogits * qv[...] * inv_root
    wide_share = share + jnp.zeros_like(ds)
    shares = jnp.where(first, wide_share, jnp.concatenate([wide_share[rows:], wide_share[:rows]], axis=0))
    dsum = jnp.where(first, ds, jnp.concatenate([ds[rows:], ds[:rows]], axis=0))
    halves.wait("vec")
    halves.wait("cot")
    halves.wait("wc")
    extra = lax.dot_general(
        dsum, wc[...].astype(F32), (((1,), (1,)), ((), ())), preferred_element_type=F32, precision=PRECISE
    )
    for load in loads:
        load.wait()
    seq, full = cot.shape
    heads = jnp.concatenate([res[b, 0:1, :].astype(F32) for b in range(rows)], axis=0)
    heads = jnp.concatenate([heads, jnp.zeros_like(heads)], axis=0)
    product = lax.dot_general(dsum, heads, (((0,), (0,)), ((), ())), preferred_element_type=F32, precision=PRECISE)
    spread(product, dw_cls)
    row = lax.broadcasted_iota(jnp.int32, (seq, 1), 0)
    for b in range(rows):
        share_b = shares[b:b + 1, 0:1]
        part = share_b * res[b].astype(F32)
        mixed[...] = part if b == 0 else mixed[...] + part
        upstream = share_b * cot[...].astype(F32) + jnp.where(row == 0, extra[b:b + 1], 0.0)
        upstream = upstream.astype(BF).astype(F32)
        normed = nout[b].astype(F32)
        dout = norm_back(upstream, normed, iout[b], wide(vec, VGF))
        add_vec(vecs, VGF, token_sum(upstream * normed))
        add_vec(vecs, VSF, token_sum(upstream))
        add_vec(vecs, VBO, token_sum(dout))
        douter[b] = dout.astype(BF)


def share_out(n, summ, prod, qv, iout, nout, res, own, theirs):
    rows, seq, full = res.shape
    shape = jax.ShapeDtypeStruct
    return pl.pallas_call(
        shares_kernel,
        out_shape=(
            shape((rows, seq, full), BF), shape((seq, full), F32), shape((2, VROWS, full // 2), F32),
            shape((2, n, PROJ // n, full // 2), F32), shape((1, PROJ), F32),
        ),
        in_specs=vmem_spec(4) + any_spec(22),
        out_specs=tuple(vmem_spec(5)),
        scratch_shapes=[
            pltpu.VMEM((2 * rows, PROJ), F32), pltpu.VMEM((2 * rows, PROJ), F32),
            pltpu.VMEM(nout.shape, BF), pltpu.VMEM(res.shape, BF),
        ] + whole_scratch(own, "cot", "vec", "wc") + [
            pltpu.SemaphoreType.DMA, pltpu.SemaphoreType.DMA, pltpu.SemaphoreType.DMA((2,)),
        ],
        compiler_params=pltpu.CompilerParams(collective_id=1, has_side_effects=True, vmem_limit_bytes=VMEM_LIMIT),
        name="shares",
    )(summ, prod, qv, iout, nout, res, *own, *theirs)


def with_bit(index, position, bit):
    low = 1 << position
    return (index // low) * (2 * low) + bit * low + index % low


def across(bit):
    me = lax.axis_index("dp")
    here = (me // (1 << bit)) % 2
    return here, (me + (1 - 2 * here) * (1 << bit), lax.axis_index("mp"))


HANDED = 2


class Group:
    def __init__(self, n, bits, bufs, sems, index, near, start=0):
        self.n, self.bits, self.near, self.start = n, bits, near, start
        bufs = list(bufs)
        self.mine = bufs.pop(0)
        self.theirs = bufs.pop(0) if start == 0 else None
        self.out, self.came = [None] * start + bufs[0::2], [None] * start + bufs[1::2]
        self.send_sem, self.recv_sem, self.own_sem, self.index = sems[0], sems[1], sems[2], index
        self.levels = len(bits)

    @staticmethod
    def scratch(n, rows, width, kind, start=0):
        levels = n.bit_length() - 1
        shapes = [(n >> start, rows, width)] * (2 if start == 0 else 1)
        for level in range(start, levels):
            shapes += [(n >> (level + 1), rows, width)] * 2
        return [pltpu.VMEM(s, kind) for s in shapes]

    @staticmethod
    def size(n, start=0):
        return (2 if start == 0 else 1) + 2 * (n.bit_length() - 1 - start)

    def remote(self, level, src, dst, target):
        return pltpu.make_async_remote_copy(
            src_ref=src, dst_ref=dst, send_sem=self.send_sem.at[self.index, level],
            recv_sem=self.recv_sem.at[self.index, level], device_id=target, device_id_type=MESH,
        )

    @staticmethod
    def handing_scratch(n, rows, width, kind):
        shapes = [(2, n, rows, width), (n, rows, width)]
        for level in range(HANDED):
            shapes += [(n >> (level + 1), rows, width)] * 2
        return [pltpu.VMEM(s, kind) for s in shapes]

    def first(self, src):
        return self.remote(0, src, self.theirs, self.near["sibling"])

    def load_own(self, src):
        return pltpu.make_async_copy(src, self.mine, self.own_sem.at[self.index])

    def hop(self, level):
        return self.remote(level + 1, self.out[level], self.came[level], self.near[self.bits[level]][1])

    def left(self, level):
        return [bit for bit in range(self.levels) if bit not in self.bits[:level]]

    def places(self, level, t, side=0):
        digit = {bit: self.near[bit][0] for bit in self.bits[self.start:level]}
        if level < self.levels:
            digit[self.bits[level]] = side
        for k, bit in enumerate(self.left(level + 1)):
            digit[bit] = (t >> k) & 1
        held = sum(digit[bit] * (1 << k) for k, bit in enumerate(self.left(self.start)))
        came = sum(digit[bit] * (1 << k) for k, bit in enumerate(self.left(level)))
        return held, came

    def advance(self, level):
        came = self.theirs if level == 0 else self.came[level - 1]
        here = self.near[self.bits[level]][0]
        count = self.n >> (level + 1)
        handed = self.start > 0 and level == self.start
        for t in range(count):
            at, of = self.places(level, t, 1 - here)
            self.out[level][t] = self.mine[at] if handed else self.mine[at] + came[of]
        self.hop(level).start()
        if not handed:
            for t in range(count):
                at, of = self.places(level, t, here)
                self.mine[at] = self.mine[at] + came[of]

    def hand_on(self, level, target):
        for t in range(self.n >> level):
            digit = {bit: self.near[bit][0] for bit in self.bits[:level]}
            for k, bit in enumerate(self.left(level)):
                digit[bit] = (t >> k) & 1
            at = sum(digit[bit] * (1 << bit) for bit in range(self.levels))
            target[t] = self.mine[at] + self.came[level - 1][t]

    def total(self):
        at, _ = self.places(self.levels, 0)
        return self.mine[at].astype(F32) + self.came[-1][0].astype(F32)


def bit_orders(n):
    rest = tuple(range(3, n.bit_length() - 1))
    return (0, 1, 2) + rest, (1, 2, 0) + rest, (2, 0, 1) + rest


def neighbours(n):
    near = {bit: across(bit) for bit in range(n.bit_length() - 1)}
    near["core"] = lax.axis_index("mp")
    near["sibling"] = (lax.axis_index("dp"), 1 - near["core"])
    return near


def bit_partners(n, near):
    return [near["sibling"]] + [near[bit][1] for bit in range(n.bit_length() - 1)]


class Reducer:
    @staticmethod
    def plan(n, mats):
        pieces = []
        for index, mat in enumerate(mats):
            if mat.shape[1] == n:
                pieces.append((index, 0, mat.shape[3], 0, index % 3))
            else:
                pieces += [(index, g * mat.shape[3], mat.shape[3], HANDED, g % 3) for g in range(mat.shape[0])]
        return pieces

    @staticmethod
    def scratch(n, mats):
        shapes = []
        pieces = Reducer.plan(n, mats)
        for index, _, width, start, _ in pieces:
            shapes += Group.scratch(n, mats[index].shape[-2], width, mats[index].dtype, start)
        dma = pltpu.SemaphoreType.DMA
        levels = n.bit_length()
        return shapes + [dma((len(pieces), levels)), dma((len(pieces), levels)), dma((len(pieces),))]

    def __init__(self, n, mats, outs, refs, near):
        self.mats, self.outs, self.near = mats, outs, near
        self.pieces = Reducer.plan(n, mats)
        orders = bit_orders(n)
        refs = list(refs)
        self.groups = []
        for index, (_, begin, width, start, order) in enumerate(self.pieces):
            size = Group.size(n, start)
            self.groups.append(Group(n, orders[order], refs[:size], refs[-3:], index, near, start))
            del refs[:size]

    def source(self, index, side):
        mat, begin, width, start, _ = self.pieces[index]
        return self.mats[mat].at[begin // width if start else side]

    def start(self):
        core = self.near["core"]
        for index, group in enumerate(self.groups):
            if not group.start:
                group.first(self.source(index, 1 - core)).start()
            group.load_own(self.source(index, core)).start()

    def move(self, mat, level):
        core = self.near["core"]
        for index, group in enumerate(self.groups):
            at, begin, width, start, _ = self.pieces[index]
            if at != mat:
                continue
            if level == start:
                group.load_own(self.source(index, core)).wait()
                if not start:
                    group.first(self.source(index, 1 - core)).wait()
            else:
                group.hop(level - 1).wait()
            if level < group.levels:
                group.advance(level)
            else:
                self.outs[mat][:, begin:begin + width] = group.total()


def middle_kernel(n, handed_count, summed, vecs_in, imid, *refs):
    refs = list(refs)

    def take(count):
        taken = refs[:count]
        del refs[:count]
        return taken

    own, theirs = take(10), take(10)
    douter_in, act_in, slope_in, mlow_in, nmid_in, ctx_in = take(6)
    dattn_out, vecs = take(2)
    handed, late_inner, late_last, dw_out = take(4) if summed else (None,) * 4
    dinner_out = None if summed else take(1)[0]
    douter, dinner, mlow, nmid, ctx, dattn, acts, slopes, acc, vec, wi, wu, halves_sem, load_sem = take(14)
    rows, seq, full = acc.shape
    half = full // 2
    chunks = wi.shape[0]
    near = neighbours(n)
    core = near["core"]
    halves = Halves(halves_sem)
    spread_halves(halves, own, theirs, vec=vec, wu=wu, wi=wi)

    def chunk_load(source, target, j, base):
        return pltpu.make_async_copy(source.at[:, j], target.at[j % 2], load_sem.at[base + j])

    def act_load(j):
        return chunk_load(act_in, acts, j, 8)

    def slope_load(j):
        return chunk_load(slope_in, slopes, j, 8 + chunks)

    pairs = ((douter_in, douter), (mlow_in, mlow), (nmid_in, nmid), (ctx_in, ctx))
    plain = [pltpu.make_async_copy(src, dst, load_sem.at[index]) for index, (src, dst) in enumerate(pairs)]
    plain[0].start()
    if summed:
        act_load(0).start()
        act_load(1).start()
    slope_load(0).start()
    halves.start()
    slope_load(1).start()
    for load in plain[1:]:
        load.start()
    vecs[...] = vecs_in[...]
    groups = []
    if summed:
        orders = bit_orders(n)
        size = 2 + 2 * HANDED
        sems = refs[-2:] + [None]
        pair_of = []
        for index in range(handed_count):
            pair, *bufs = take(size)
            pair_of.append(pair)
            groups.append(Group(n, orders[index % 3], [pair.at[core]] + bufs, sems, index, near))
        greet(bit_partners(n, near))
    plain[0].wait()

    def flat(ref):
        return ref[...].reshape(rows * seq, full)

    def begin(index, left, right):
        spread(tn(left, right), pair_of[index])
        groups[index].first(pair_of[index].at[1 - core]).start()

    def move(index, level):
        if level == 0:
            groups[index].first(pair_of[index].at[1 - core]).wait()
        else:
            groups[index].hop(level - 1).wait()
        groups[index].advance(level)

    if summed:
        for j in range(chunks):
            act_load(j).wait()
            if j >= 2:
                move(j - 2, 0)
            begin(j, flat(douter), acts[j % 2].reshape(rows * seq, full))
            if j + 2 < chunks:
                act_load(j + 2).start()
    moves = {
        (0, 0): ((2, 0),), (0, 1): ((3, 0),), (0, 2): ((0, 1),), (1, 1): ((1, 1), (4, 0)), (1, 2): ((2, 1),),
        (2, 1): ((3, 1), (5, 0)), (2, 2): ((4, 1),), (3, 2): ((5, 1),),
    }

    def moved(j, point):
        for index, level in moves.get((j, point), ()) if summed else ():
            move(index, level)

    acc[...] = douter[...].astype(F32)
    halves.wait("vec")
    halves.wait("wu")
    halves.wait("wi")
    plain[1].wait()
    for j in range(chunks):
        slope_load(j).wait()
        for m in range(0, rows, 2):
            moved(j, m // 2)
            part = nt(douter[m:m + 2].reshape(2 * seq, full), wu[j])
            part = part * slopes[j % 2, m:m + 2].reshape(2 * seq, full).astype(F32)
            low = part.astype(BF)
            dinner[m:m + 2] = low.reshape(2, seq, full)
            sums = token_sum(part)
            for side in range(2):
                vecs[side, VIN + j:VIN + j + 1, :] += sums[:, side * half:(side + 1) * half]
            acc[m:m + 2] += nt(low, wi[j]).reshape(2, seq, full)
        if j + 2 < chunks:
            slope_load(j + 2).start()
        moved(j, 2)
        if not summed:
            copy = pltpu.make_async_copy(dinner, dinner_out.at[j], load_sem.at[4])
            copy.start()
            copy.wait()
        elif chunks + j < handed_count:
            begin(chunks + j, flat(mlow), flat(dinner))
        else:
            spread(tn(flat(mlow), flat(dinner)), (late_inner, late_last)[chunks + j - handed_count])
    plain[2].wait()
    for r in range(rows):
        upstream = acc[r]
        normed = nmid[r].astype(F32)
        middle = norm_back(upstream, normed, imid[r], wide(vec, VGA))
        add_vec(vecs, VGA, token_sum(upstream * normed))
        add_vec(vecs, VSA, token_sum(upstream))
        add_vec(vecs, VO, token_sum(middle))
        dattn[r] = middle.astype(BF)
    done = pltpu.make_async_copy(dattn, dattn_out, load_sem.at[5])
    done.start()
    plain[3].wait()
    if summed:
        spread(tn(flat(dattn), flat(ctx)), dw_out)
        for index, group in enumerate(groups):
            group.hop(HANDED - 1).wait()
            group.hand_on(HANDED, handed.at[index])
    done.wait()


def middle(n, summed, douter, act, slope, mlow, nmid, imid, ctx, vecs, own, theirs):
    rows, seq, full = douter.shape
    half = full // 2
    chunks = act.shape[1]
    shape = jax.ShapeDtypeStruct
    dma = pltpu.SemaphoreType.DMA
    outs = [shape((rows, seq, full), BF), shape(vecs.shape, F32)]
    specs = any_spec(1) + vmem_spec(1)
    handed_count = chunks + 2
    depth = full // n
    scratch = [pltpu.VMEM((rows, seq, full), BF)] * 6 + [pltpu.VMEM((2, rows, seq, full), BF)] * 2
    scratch += [pltpu.VMEM((rows, seq, full), F32)] + whole_scratch(own, "vec", "wi", "wu") + [dma((8 + 2 * chunks,))]
    params = dict(vmem_limit_bytes=VMEM_LIMIT)
    if summed:
        outs.append(shape((handed_count, n >> HANDED, depth, half), BF))
        outs += [shape((2, n, depth, half), BF)] * 3
        specs += vmem_spec(4)
        for _ in range(handed_count):
            scratch += Group.handing_scratch(n, depth, half, BF)
        scratch += [dma((handed_count, HANDED + 1))] * 2
        params.update(collective_id=3, has_side_effects=True)
    else:
        outs.append(shape((chunks, rows, seq, full), BF))
        specs += any_spec(1)
    return pl.pallas_call(
        functools.partial(middle_kernel, n, handed_count, summed),
        out_shape=tuple(outs),
        in_specs=vmem_spec(2) + any_spec(26),
        out_specs=tuple(specs),
        scratch_shapes=scratch,
        compiler_params=pltpu.CompilerParams(**params),
        name="middle",
    )(vecs, imid, *own, *theirs, douter, act, slope, mlow, nmid, ctx)


SEND_AT = 2
VEC_AT = 1
TAIL_TIMES = (
    (3, 0, 2), (7, 0, 3), (7, 1, 0), (8, 2, 0), (8, 3, 0), (8, 4, 0), (14, 0, 4),
    (17, 1, 1), (17, 2, 1), (17, 3, 1), (17, 4, 1),
)


def tail_kernel(n, mat_count, slot_row, picks, vecs_in, places, segments, dattn, qkv, lse, mixed_in, xlow, *refs):
    refs = list(refs)

    def take(count):
        taken = refs[:count]
        del refs[:count]
        return taken

    own, theirs, mats = take(10), take(10), take(mat_count)
    gt, arrived, mixed, vec_out = take(4)
    spare = [] if mats else take(2)
    sums_out = take(mat_count)
    small_out = take(4) if mats else []
    bias, grads, dqkv, dstart, gt_v, stage, mix_own, mix_got, late, late_far, late_all, vec_far, vec_rows, vec_got, vec_sums, wqkv, wo, halves_sem = take(18)
    own_sem, sib_send, sib_recv, doc_send, doc_recv, vec_send, vec_recv, late_send, late_recv = take(9)
    x_v = outgoing = None
    small = []
    near = neighbours(n)
    if mats:
        x_v, *outgoing = take(5)
        orders = bit_orders(n)
        count = 4 * Group.size(n) + 3
        small_refs = take(count)
        for index in range(4):
            size = Group.size(n)
            bufs = small_refs[index * size:(index + 1) * size]
            small.append(Group(n, orders[(0, 1, 2, 0)[index]], bufs, small_refs[-3:], index, near))
        summer = Reducer(n, mats, sums_out, refs, near)
    b = pl.program_id(0)
    rows = pl.num_programs(0)
    me = lax.axis_index("dp")
    core = near["core"]
    other = 1 - core
    sibling = near["sibling"]
    levels = n.bit_length() - 1
    row_count, _, half = gt_v.shape
    all_rows = row_count // 2
    seq, full = grads.shape
    gang = GANG
    pair = gang * HEAD_DIM
    pairs = full // pair
    halves = Halves(halves_sem)
    spread_halves(halves, own, theirs, wo=wo)
    for index in range(3):
        halves.add("qkv", own[3 + index], theirs[3 + index], wqkv, 1, index * half, 3 * half)
    here_cols = pl.ds(pl.multiple_of(core * half, half), half)
    there_cols = pl.ds(pl.multiple_of(other * half, half), half)
    first_core = core == 0

    def push(row):
        at = pl.ds(pl.multiple_of(row * seq, seq), seq)
        return pltpu.make_async_remote_copy(
            src_ref=dstart.at[at, there_cols], dst_ref=gt_v.at[2 * row + core],
            send_sem=sib_send.at[row], recv_sem=sib_recv.at[row], device_id=sibling, device_id_type=MESH,
        )

    def document(slot):
        if slot == LOCAL:
            return pltpu.make_async_copy(stage.at[slot], arrived.at[slot], own_sem.at[2])
        return pltpu.make_async_remote_copy(
            src_ref=stage.at[slot], dst_ref=arrived.at[slot], send_sem=doc_send.at[slot], recv_sem=doc_recv.at[slot],
            device_id=(lax.rem(me + OFFSETS[slot] + n, n), core), device_id_type=MESH,
        )

    def pack(slot):
        lowest, highest = max(0, slot - (SLOTS - row_count)), min(row_count - 1, slot)
        value = gt_v[lowest]
        for rank in range(lowest + 1, highest + 1):
            value = jnp.where(slot_row[rank] == slot, gt_v[rank], value)
        stage[slot] = value

    mix_far = pltpu.make_async_remote_copy(
        src_ref=mixed_in.at[:, there_cols], dst_ref=mix_got, send_sem=sib_send.at[all_rows],
        recv_sem=sib_recv.at[all_rows], device_id=sibling, device_id_type=MESH,
    )
    mix_load = pltpu.make_async_copy(mixed_in.at[:, here_cols], mix_own, own_sem.at[0])
    vec_copy = pltpu.make_async_remote_copy(
        src_ref=vecs_in.at[other], dst_ref=vec_far, send_sem=vec_send.at[0], recv_sem=vec_recv.at[0],
        device_id=sibling, device_id_type=MESH,
    )

    def vec_hop(again, step):
        to = lax.rem(me + step, n)
        src, dst = (vec_sums.at[me], vec_sums.at[me]) if again else (vec_rows.at[to], vec_got.at[me])
        return pltpu.make_async_remote_copy(
            src_ref=src, dst_ref=dst, send_sem=vec_send.at[again * n + step], recv_sem=vec_recv.at[again * n + step],
            device_id=(to, core), device_id_type=MESH,
        )

    def vec_out_rows():
        vec_copy.wait()
        held = vecs_in[core] + vec_far[...]
        depth = held.shape[0] // n
        for i in range(n):
            vec_rows[i] = held[i * depth:(i + 1) * depth]
        for step in range(1, n):
            vec_hop(0, step).start()

    def vec_sum_rows():
        for step in range(1, n):
            vec_hop(0, step).wait()
        total = vec_rows[me]
        for step in range(1, n):
            total = total + vec_got[lax.rem(me + step, n)]
        vec_sums[me] = total
        for step in range(1, n):
            vec_hop(1, step).start()

    late_copy = pltpu.make_async_remote_copy(
        src_ref=late.at[other], dst_ref=late_far, send_sem=late_send.at[0], recv_sem=late_recv.at[0],
        device_id=sibling, device_id_type=MESH,
    )

    def late_hop(step):
        return pltpu.make_async_remote_copy(
            src_ref=late_all.at[me], dst_ref=late_all.at[me], send_sem=late_send.at[step], recv_sem=late_recv.at[step],
            device_id=(lax.rem(me + step, n), core), device_id_type=MESH,
        )

    x_loads = []
    if mats:
        for r in range(all_rows):
            x_loads.append(pltpu.make_async_copy(xlow.at[r], x_v.at[pl.ds(r * seq, seq)], own_sem.at[3 + r]))

    @pl.when(b == 0)
    def _():
        halves.start()
        late[...] = jnp.zeros_like(late)
        everyone = [(lax.rem(me + step, n), core) for step in range(1, n)]
        greet((everyone if mats else ring_partners(me, core, n)) + [sibling])
        if mats:
            summer.start()
        vec_copy.start()
        mix_far.start()
        mix_load.start()
        for load in x_loads:
            load.start()
        halves.wait("wo")
        halves.wait("qkv")

    grads[...] = nt(dattn[0], wo[...]).astype(BF)
    turn = rows - 1 - b
    seg_row = segments[pl.ds(picks[row_count + 2 * turn + core], 1), :]
    bias[...] = jnp.where(column(seg_row) == seg_row, 0.0, NEGATIVE)
    masks = head_masks(gang)
    my_rows = pl.ds(pl.multiple_of(turn * seq, seq), seq)

    def heads(p):
        for step, mat, level in TAIL_TIMES if mats else ():
            if step % pairs == p:

                @pl.when(b == step // pairs)
                def _(mat=mat, level=level):
                    summer.move(mat, level)

        if p == SEND_AT and mats:

            @pl.when(b == 0)
            def _():
                vec_out_rows()

        if p == VEC_AT and mats:

            @pl.when(b == 1)
            def _():
                vec_sum_rows()

        if p == SEND_AT:
            for row in range(1, all_rows):

                @pl.when(b == row)
                def _(row=row):
                    push(all_rows - row).wait()
                    for slot in (SLOTS - 2 * row, SLOTS - 2 * row + 1):
                        pack(slot)
                        document(slot).start()

        at = p * pair
        queries = qkv[0, :, pl.ds(at, pair)]
        keys = qkv[0, :, pl.ds(full + at, pair)]
        values = qkv[0, :, pl.ds(2 * full + at, pair)]
        dctx = grads[:, pl.ds(at, pair)]
        lane = lax.broadcasted_iota(jnp.int32, (seq, pair), 1)
        keys_all = jnp.concatenate([keys * m for m in masks], axis=0)
        s = nt(keys_all, queries)
        dw = nt(jnp.concatenate([values * m for m in masks], axis=0), dctx)
        ws, dss = [], []
        for h in range(gang):
            w = jnp.exp(s[h * seq:(h + 1) * seq] + bias[...] - lse[0, gang * p + h:gang * p + h + 1, :])
            prod = w * dw[h * seq:(h + 1) * seq]
            dss.append((prod - w * token_sum(prod)).astype(BF))
            ws.append(w.astype(BF))
        ds = jnp.concatenate(dss, axis=0)
        dv = mm(jnp.concatenate(ws, axis=0), dctx)
        dk = mm(ds, queries)
        dq = tn(ds, keys_all) * HEAD_DIM ** -0.5

        def join(parts):
            joined = parts[0:seq]
            for h in range(1, gang):
                joined = jnp.where(lane < h * HEAD_DIM, joined, parts[h * seq:(h + 1) * seq])
            return joined

        for t, value in enumerate((dq, join(dk), join(dv))):
            for i in range(0, pair, 128):
                column = at + i
                out_at = (column // half) * (3 * half) + column % half + t * half
                dqkv[my_rows, pl.ds(out_at, 128)] = value[:, i:i + 128].astype(BF)

    for p in range(pairs):
        heads(p)
    total = dattn[0].astype(F32) + nt(dqkv[my_rows, :], wqkv[...])
    for h in range(2):
        for t in (0, 2):
            source = dqkv[my_rows, (3 * h + t) * half:(3 * h + t + 1) * half]
            late[h, t // 2:t // 2 + 1, :] += token_sum(source.astype(F32))
    low = total.astype(BF)
    dstart[my_rows, :] = low
    gt_v[2 * turn + core] = jnp.where(first_core, total[:, :half], total[:, half:]).astype(BF)
    push(turn).start()

    @pl.when(b == rows - 1)
    def _():
        late_copy.start()
        late_copy.wait()
        late_all[me] = late[core] + late_far[...]
        if mats:
            for step in range(1, n):
                late_hop(step).start()
        push(0).wait()
        tok_out = pltpu.make_async_copy(gt_v, gt, own_sem.at[1])
        tok_out.start()
        for slot in reversed(range(SLOTS - 2 * all_rows + 2)):
            pack(slot)
        for slot in reversed(range(SLOTS - 2 * all_rows + 2)):
            document(slot).start()

        if not mats:
            vec_copy.wait()
            vec_out[...] = vecs_in[core] + vec_far[...]
            vec_out[VQ:VV + 1] = late_all[me]
            for source, target in ((dqkv, spare[0]), (dstart, spare[1])):
                copy = pltpu.make_async_copy(source, target, own_sem.at[3])
                copy.start()
                copy.wait()
        else:
            for load in x_loads:
                load.wait()
            table = small_out[3].shape[0] * n
            one_hots = []
            for r in range(all_rows):
                place = places[pl.ds(picks[row_count + 2 * r + core], 1), :]
                here = place == lax.broadcasted_iota(jnp.int32, (table, seq), 0)
                one_hots.append(here.astype(F32).astype(BF))

            def product(index, side, target):
                if index < 3:
                    at = pl.ds(pl.multiple_of(side * 3 * half + index * half, half), half)
                    value = tn(x_v[...], dqkv[:, at])
                else:
                    at = pl.ds(pl.multiple_of(side * half, half), half)
                    value = sum(mm(one_hots[r], dstart[r * seq:(r + 1) * seq, at]) for r in range(all_rows))
                depth = target.shape[1]
                for i in range(n):
                    target[i] = value[i * depth:(i + 1) * depth].astype(target.dtype)

            firsts = []

            def begin(index):
                product(index, other, outgoing[index])
                copy = small[index].first(outgoing[index])
                copy.start()
                firsts.append(copy)
                product(index, core, small[index].mine)

            def step(index, level):
                if level == 0:
                    firsts[index].wait()
                else:
                    small[index].hop(level - 1).wait()
                if level < levels:
                    small[index].advance(level)
                else:
                    small_out[index][...] = small[index].total()

            taken = {}
            for _, mat, level in TAIL_TIMES:
                taken[mat] = max(taken.get(mat, -1), level)
            left = [(mat, level) for level in range(levels + 1) for mat in range(mat_count) if level > taken.get(mat, -1)]

            def some(mat):
                for at, (m, level) in enumerate(left):
                    if m == mat:
                        del left[at]
                        summer.move(mat, level)
                        return

            begin(0)
            begin(1)
            step(0, 0)
            begin(2)
            step(1, 0)
            begin(3)
            step(2, 0)
            step(3, 0)
            while left:
                some(left[0][0])
            for level in range(1, levels + 1):
                for index in range(4):
                    step(index, level)
            for step_to in range(1, n):
                vec_hop(1, step_to).wait()
                late_hop(step_to).wait()
            vec_out[...] = jnp.concatenate([vec_sums[i] for i in range(n)], axis=0)
            total = late_all[0]
            for i in range(1, n):
                total = total + late_all[i]
            vec_out[VQ:VV + 1] = total
        mix_load.wait()
        mix_far.wait()
        mixed[...] = (mix_own[...] + mix_got[...]).astype(BF)
        tok_out.wait()
        for slot in range(SLOTS):
            document(slot).wait()


def tail(n, table, slot_of, picks, vecs, places, segments, dattn, qkv, lse, mixed, xlow, own, theirs, mats):
    rows, seq, full = dattn.shape
    half = full // 2
    tokens = rows * seq
    levels = n.bit_length() - 1
    shape = jax.ShapeDtypeStruct
    outs = [shape((2 * rows, seq, half), BF), shape((SLOTS, seq, half), BF), shape((seq, half), BF), shape(vecs.shape[1:], F32)]
    if not mats:
        outs += [shape((tokens, 3 * full), BF), shape((tokens, full), BF)]
    out_specs = any_spec(2) + [whole_block(o) for o in outs[2:4]] + any_spec(len(outs) - 4)
    by_row = (dattn, qkv, lse)
    dma = pltpu.SemaphoreType.DMA
    scratch = [
        pltpu.VMEM((seq, seq), F32), pltpu.VMEM((seq, full), BF), pltpu.VMEM((tokens, 3 * full), BF),
        pltpu.VMEM((tokens, full), BF), pltpu.VMEM((2 * rows, seq, half), BF), pltpu.VMEM((SLOTS, seq, half), BF),
        pltpu.VMEM((seq, half), F32), pltpu.VMEM((seq, half), F32), pltpu.VMEM((2, 2, half), F32),
        pltpu.VMEM((2, half), F32), pltpu.VMEM((n, 2, half), F32), pltpu.VMEM(vecs.shape[1:], F32),
    ] + [pltpu.VMEM((n, max(1, vecs.shape[1] // n), half), F32)] * 3 + whole_scratch(own, "wqkv", "wo") + [
        dma((3 + rows,)), dma((rows + 1,)), dma((rows + 1,)), dma((SLOTS,)), dma((SLOTS,)), dma((2 * n,)), dma((2 * n,)), dma((n,)), dma((n,)),
    ]
    if mats:
        depths = [full // n] * 3 + [table // n]
        scratch += [pltpu.VMEM((tokens, full), BF)] + [pltpu.VMEM((n, depth, half), BF) for depth in depths]
        for depth in depths:
            scratch += Group.scratch(n, depth, half, BF)
        scratch += [dma((4, levels + 1)), dma((4, levels + 1)), dma((4,))]
        scratch += Reducer.scratch(n, mats)
        sums = [shape((m.shape[2], m.shape[3] * (1 if m.shape[1] == n else m.shape[0])), F32) for m in mats] + [shape((depth, half), F32) for depth in depths]
        outs += sums
        out_specs += [whole_block(o) for o in sums]
    return pl.pallas_call(
        functools.partial(tail_kernel, n, len(mats)),
        out_shape=tuple(outs),
        grid=(rows,),
        in_specs=[pl.BlockSpec(memory_space=pltpu.SMEM)] * 2 + [whole_block(a) for a in (vecs, places, segments)]
        + [row_back(a) for a in by_row] + any_spec(22 + len(mats)),
        out_specs=tuple(out_specs),
        scratch_shapes=scratch,
        compiler_params=pltpu.CompilerParams(
            collective_id=2, has_side_effects=True, vmem_limit_bytes=VMEM_LIMIT
        ),
        name="tail",
    )(slot_of, picks, vecs, places, segments, *by_row, mixed, xlow, *own, *theirs, *mats)


FINISHED = ("mixed", "pos", "wq", "wk", "wv", "wo", "cls", "gq")


def finish_kernel(names, want, rank, arrived, gt, vec_sum, *refs):
    refs = list(refs)

    def take(count):
        taken = refs[:count]
        del refs[:count]
        return taken

    ins, handed, lates, (docs_out, tokens_out) = take(len(names)), take(1)[0], take(2), take(2)
    outs, (outer, inner), vectors = take(len(names)), take(2), take(9)
    got, total, tok, sems = refs
    docs = docs_out.shape[0]
    row_count, _, half = tokens_out.shape
    loads = [pltpu.make_async_copy(arrived.at[slot], got.at[slot], sems.at[slot]) for slot in range(SLOTS)]
    tok_loads = [pltpu.make_async_copy(gt.at[jnp.minimum(rank[k], row_count - 1)], tok.at[k], sems.at[SLOTS + 1 + k]) for k in range(row_count)]
    for load in tok_loads + loads:
        load.start()

    def clear(d, carry):
        total[d] = jnp.zeros(total.shape[1:], F32)
        return carry

    lax.fori_loop(0, docs, clear, 0)
    for load in tok_loads:
        load.wait()
    tok_done = pltpu.make_async_copy(tok, tokens_out, sems.at[SLOTS + 1])
    tok_done.start()
    for slot in range(SLOTS):
        loads[slot].wait()
        at = jnp.where(want[slot] < 0, docs, jnp.minimum(want[slot], docs))
        total[at] += got[slot].astype(F32)
    done = pltpu.make_async_copy(total.at[pl.ds(0, docs)], docs_out, sems.at[SLOTS])
    done.start()
    for name, source, target in zip(names, ins, outs):
        if name == "mixed":
            target[0] = source[...]
        else:
            target[...] = source[...]
    hidden = outer.shape[1]
    first_inner = handed.shape[1] - hidden
    outer[...] = handed[:, :hidden]
    inner[:, :first_inner] = handed[:, hidden:]
    for index, late in enumerate(lates):
        inner[:, first_inner + index * half:first_inner + (index + 1) * half] = late[...]
    for index, vector in enumerate(vectors):
        for i in range(vector.shape[0] // half):
            vector[i * half:(i + 1) * half] = vec_sum[index + i]
    tok_done.wait()
    done.wait()


def finish(docs, want, rank, arrived, gt, vec_sum, named, handed, lates):
    _, seq, half = arrived.shape
    shape = jax.ShapeDtypeStruct
    names = tuple(named)
    outs = [shape((docs, seq, half), F32), shape(gt.shape, BF)]
    for name, value in named.items():
        outs.append(shape(((1,) if name == "mixed" else ()) + value.shape, value.dtype))
    hidden = (handed.shape[1] + 2 * half) // 2
    outs += [shape((handed.shape[0], hidden), F32)] * 2
    outs += [shape((half * (hidden // half if index == VIN else 1),), F32) for index in range(9)]
    smem = pl.BlockSpec(memory_space=pltpu.SMEM)
    grad_docs, grad_tokens, *rest = pl.pallas_call(
        functools.partial(finish_kernel, names),
        out_shape=tuple(outs),
        in_specs=[smem, smem] + any_spec(2) + vmem_spec(4 + len(names)),
        out_specs=tuple(any_spec(2) + vmem_spec(len(outs) - 2)),
        scratch_shapes=[
            pltpu.VMEM(arrived.shape, BF), pltpu.VMEM((docs + 1, seq, half), F32), pltpu.VMEM(gt.shape, BF),
            pltpu.SemaphoreType.DMA((SLOTS + 1 + gt.shape[0],)),
        ],
        compiler_params=pltpu.CompilerParams(vmem_limit_bytes=VMEM_LIMIT),
        name="finish",
    )(want, rank, arrived, gt, vec_sum, *named.values(), handed, *lates)
    return grad_docs, grad_tokens, dict(zip(names + ("outer", "inner"), rest)), rest[len(names) + 2:]


def body(
    tokens, segment_ids, positions, query_vectors, doc_owner, doc_slot, doc_store, pos_table,
    w_query, w_key, w_value, b_query, b_value, w_out, b_out, gain_attn, shift_attn,
    w_inner, b_inner, w_outer, b_outer, gain_ffn, shift_ffn, w_cls, cotangent,
):
    n = lax.axis_size("dp")
    core = lax.axis_index("mp")
    row_count, _, half = tokens.shape
    full = 2 * half
    weights = (w_query, w_key, w_value, w_out, w_inner, w_outer, w_cls)
    vectors = (b_query, b_value, b_out, gain_attn, shift_attn, b_outer, gain_ffn, shift_ffn, b_inner)
    theirs, vec_own, (want, rank, slot_of, picks), acts = forward(
        n, doc_owner, doc_slot, positions, segment_ids, vectors, doc_store, tokens, cotangent[0], pos_table, weights
    )
    own = (cotangent[0], pos_table, vec_own) + weights
    xlow, qkv, lse, ctx, nmid, imid, mlow, act, slope, nout, iout, res, summ, prod = acts

    douter, mixed, vecs, dw_cls, grad_query = share_out(n, summ, prod, query_vectors, iout, nout, res, own, theirs)

    def cross(left, right):
        left = left.reshape(-1, left.shape[-1])
        right = right.reshape(-1, right.shape[-1])
        return tn(left, right)

    summed = full // n % 16 == 0
    table = pos_table.shape[0]
    dattn, vecs, *parts = middle(n, summed, douter, act, slope, mlow, nmid, imid, ctx, vecs, own, theirs)
    mats = parts + [dw_cls] if summed else []
    grad_tokens, arrived, mixed_out, vec_sum, *sums = tail(
        n, table, slot_of, picks, vecs, positions, segment_ids, dattn, qkv, lse, mixed, xlow, own, theirs, mats
    )
    if summed:
        handed, late_inner, late_last, g_wo, g_cls, g_q, g_k, g_v, g_pos = sums
    else:
        vec_sum = lax.psum(vec_sum, "dp")
        dqkv, dstart = sums
        place = jnp.take(positions, picks[row_count:].reshape(-1, 2)[:, core], axis=0, mode="clip")
        one_hot = (place.reshape(-1)[:, None] == jnp.arange(table, dtype=jnp.int32)[None, :]).astype(BF)

        def scatter(part):
            part = lax.psum_scatter(part.astype(F32), "mp", scatter_dimension=1, tiled=True)
            return lax.psum_scatter(part, "dp", scatter_dimension=0, tiled=True)

        def in_order(part):
            return part.reshape(full, -1, 2, half).swapaxes(1, 2).reshape(full, -1)

        dinner = parts[0].transpose(1, 2, 0, 3)
        dw_outer = in_order(cross(douter, act.transpose(0, 2, 1, 3).reshape(-1, act.shape[1] * full)))
        dw_inner = in_order(cross(mlow, dinner.reshape(-1, act.shape[1] * full)))
        dw_cls = dw_cls.transpose(1, 2, 0, 3).reshape(PROJ, full)
        g_outer, g_inner, g_wo, g_qkv, g_cls, g_pos = [
            scatter(p) for p in (dw_outer, dw_inner, cross(dattn, ctx), cross(xlow, dqkv), dw_cls, cross(one_hot, dstart))
        ]
        g_q, g_k, g_v = g_qkv[:, :half], g_qkv[:, half:2 * half], g_qkv[:, 2 * half:]
        handed = jnp.concatenate([g_outer, g_inner[:, :-2 * half]], axis=1)
        late_inner, late_last = g_inner[:, -2 * half:-half], g_inner[:, -half:]
    named = dict(zip(FINISHED, (mixed_out, g_pos, g_q, g_k, g_v, g_wo, g_cls, grad_query)))
    grad_docs, grad_tokens, out, vec = finish(
        doc_store.shape[0], want, rank, arrived, grad_tokens, vec_sum, named, handed, (late_inner, late_last)
    )
    return (
        out["mixed"], grad_tokens, out["gq"], grad_docs, out["pos"], out["wq"], out["wk"], out["wv"], vec[VQ], vec[VV],
        out["wo"].T, vec[VO], vec[VGA], vec[VSA], out["inner"], vec[VIN], out["outer"].T, vec[VBO], vec[VGF], vec[VSF],
        out["cls"].T,
    )


def solution(mesh):
    rows = P("dp", None, "mp")
    ids = P("dp", None)
    cols = P(None, "mp")
    vec = P("mp")
    deep = P("mp", None)
    in_specs = (
        rows, ids, ids, ids, ids, ids, rows, cols, cols, cols, cols, vec, vec, deep, vec, vec, vec,
        cols, vec, deep, vec, vec, vec, deep, rows,
    )
    near = P("dp", "mp")
    turned = P("mp", "dp")
    out_specs = (
        rows, rows, ids, rows, near, near, near, near, vec, vec, turned, vec, vec, vec, near, vec,
        turned, vec, vec, vec, turned,
    )
    return jax.shard_map(body, mesh=mesh, in_specs=in_specs, out_specs=out_specs, check_vma=False)
```

```python
import functools

import jax
import jax.numpy as jnp
from jax import lax
from jax.experimental import pallas as pl
from jax.experimental.pallas import tpu as pltpu
from jax.sharding import PartitionSpec as P

HEAD_DIM = 64
PROJ = 128
REACH = 6
SLOTS = 2 * REACH
OFFSETS = (0, 1, -1, 2, -2, -4, -3, 4, 3, -5, 5, -6)
LOCAL = 0
REMOTE = tuple(range(1, SLOTS))
EPSILON = 1e-05
NEGATIVE = -1e30
PRECISE = lax.Precision.HIGHEST
MESH = pl.DeviceIdType.MESH
BF = jnp.bfloat16
F32 = jnp.float32
VMEM_LIMIT = 60 * 1024 * 1024
VQ, VV, VO, VGA, VSA, VBO, VGF, VSF, VIN = range(9)
VROWS = 16
GANG = 2


def any_spec(count):
    return [pl.BlockSpec(memory_space=pl.ANY)] * count


def vmem_spec(count):
    return [pl.BlockSpec(memory_space=pltpu.VMEM)] * count


def row_block(array):
    dims = array.shape[1:]
    return pl.BlockSpec((1,) + dims, lambda b: (b,) + (0,) * len(dims))


def row_back(array):
    dims = array.shape[1:]
    last = array.shape[0] - 1
    return pl.BlockSpec((1,) + dims, lambda b: (last - b,) + (0,) * len(dims))


def whole_block(array):
    dims = array.shape
    return pl.BlockSpec(dims, lambda b: (0,) * len(dims), pipeline_mode=pl.Buffered(1))


def nt(left, right):
    return lax.dot_general(left, right, (((1,), (1,)), ((), ())), preferred_element_type=F32)


def tn(left, right):
    return lax.dot_general(left, right, (((0,), (0,)), ((), ())), preferred_element_type=F32)


def mm(left, right):
    return jnp.dot(left, right, preferred_element_type=F32)


def greet(targets):
    barrier = pltpu.get_barrier_semaphore()
    for target in targets:
        pl.semaphore_signal(barrier, inc=1, device_id=target, device_id_type=MESH)
    pl.semaphore_wait(barrier, len(targets))


def ring_partners(me, core, n):
    return [(lax.rem(me + step + n, n), core) for step in range(-REACH, REACH + 1) if step != 0]


class Halves:
    def __init__(self, sems):
        self.sems, self.copies, self.names = sems, [], {}

    def add(self, name, own, theirs, whole, axis, offset=0, stride=None):
        core = lax.axis_index("mp")
        size = own.shape[axis] if axis is not None else 1
        for source, side in ((own, core), (theirs, 1 - core)):
            if axis is None:
                target = whole.at[side]
            else:
                begin = offset + side * (stride or size)
                at = pl.ds(pl.multiple_of(begin, 128), size)
                target = whole.at[at] if axis == 0 else whole.at[:, at]
            copy = pltpu.make_async_copy(source, target, self.sems.at[len(self.copies)])
            self.copies.append(copy)
            self.names.setdefault(name, []).append(copy)

    def add_chunks(self, name, own, theirs, whole, axis):
        core = lax.axis_index("mp")
        size = whole.shape[1] // 2
        for j in range(whole.shape[0]):
            for source, side in ((own, core), (theirs, 1 - core)):
                to = pl.ds(pl.multiple_of(side * size, 128), size)
                part = pl.ds(j * size, size)
                source_part, target = (source.at[part], whole.at[j, to]) if axis == 0 else (source.at[:, part], whole.at[j, :, to])
                copy = pltpu.make_async_copy(source_part, target, self.sems.at[len(self.copies)])
                self.copies.append(copy)
                self.names.setdefault(name, []).append(copy)

    def start(self):
        self.start_own()
        self.start_theirs()

    def start_own(self):
        for copy in self.copies[0::2]:
            copy.start()

    def start_theirs(self):
        for copy in self.copies[1::2]:
            copy.start()

    def wait(self, name):
        for copy in self.names[name]:
            copy.wait()


def wide(vec, row):
    return jnp.concatenate([vec[0, row:row + 1, :], vec[1, row:row + 1, :]], axis=1)


def normalize(hidden):
    average = jnp.mean(hidden, axis=-1, keepdims=True)
    centered = hidden - average
    spread = jnp.mean(centered * centered, axis=-1, keepdims=True)
    inverse = lax.rsqrt(spread + EPSILON)
    return centered * inverse, inverse


def column(row):
    size = row.shape[1]
    here = lax.broadcasted_iota(jnp.int32, (size, size), 0) == lax.broadcasted_iota(jnp.int32, (size, size), 1)
    return jnp.sum(jnp.where(here, row, 0), axis=1, keepdims=True)


def head_masks(count):
    lane = lax.broadcasted_iota(jnp.int32, (1, count * HEAD_DIM), 1) // HEAD_DIM
    return [(lane == h).astype(F32).astype(BF) for h in range(count)]


def spread_halves(halves, own, theirs, **whole):
    places = {"cot": (0, 1), "pos": (1, 1), "vec": (2, None), "wo": (6, 0), "wi": (7, 1), "wu": (8, 0), "wc": (9, 0)}
    for name, ref in whole.items():
        if name == "wqkv":
            for index in range(3):
                halves.add("qkv", own[3 + index], theirs[3 + index], ref, 1, index * ref.shape[0])
        elif name in ("wi", "wu"):
            at, axis = places[name]
            halves.add_chunks(name, own[at], theirs[at], ref, axis)
        else:
            at, axis = places[name]
            halves.add(name, own[at], theirs[at], ref, axis)


def whole_scratch(own, *names):
    cot, pos, vec, wq, _, _, wo, wi, wu, wc = own
    full = wq.shape[0]
    shapes = {
        "cot": ((cot.shape[0], full), BF), "pos": ((pos.shape[0], full), BF), "vec": ((2,) + vec.shape, F32),
        "wqkv": ((full, 3 * full), BF), "wo": ((full, full), BF), "wi": ((2 * wi.shape[1] // full, full, full), BF),
        "wu": ((2 * wu.shape[0] // full, full, full), BF), "wc": ((full, wc.shape[1]), BF),
    }
    return [pltpu.VMEM(*shapes[name]) for name in names] + [pltpu.SemaphoreType.DMA((40,))]


LATE_START = 4
LATE_AT = 2
LATE_FIRST = 4


def forward_kernel(n, owner, doc_slot, places, segments, *refs):
    refs = list(refs)

    def take(count):
        taken = refs[:count]
        del refs[:count]
        return taken

    vectors = take(9)
    docs_in, tok_in, cot_in, pos_in = take(4)
    weights_in = take(7)
    theirs = take(10)
    vec_own, want, rank_out, slot_of, picks = take(5)
    xlow, qkv, lse, ctx, nmid, imid, mlow, act, slope, nout, iout, res, summ, prod = take(14)
    bias, stats, acc, cot, pos, vec, wqkv, wo, wi, wu, wc, sems = take(12)
    doc_buf, stage, docs, docs_sib, tok, tok_sib, req, got, got_s = take(9)
    req_send, req_recv, doc_send, doc_recv, fwd_send, fwd_recv, sib_send, sib_recv, misc_sem = take(9)
    own = [cot_in, pos_in, vec_own] + weights_in
    b = pl.program_id(0)
    rows = pl.num_programs(0)
    me = lax.axis_index("dp")
    core = lax.axis_index("mp")
    sibling = (me, 1 - core)
    seq, full = acc.shape
    row_count, _, half = tok_in.shape
    all_rows = row_count // 2
    early = SLOTS - row_count + 2
    halves = Halves(sems)
    spread_halves(halves, own, theirs, pos=pos, vec=vec, wqkv=wqkv, wo=wo, wi=wi, wu=wu, wc=wc, cot=cot)
    fresh = b == 0

    def request(slot):
        return pltpu.make_async_remote_copy(
            src_ref=req.at[slot], dst_ref=got.at[slot], send_sem=req_send.at[slot], recv_sem=req_recv.at[slot],
            device_id=(lax.rem(me + OFFSETS[slot] + n, n), core), device_id_type=MESH,
        )

    def document(slot):
        return pltpu.make_async_remote_copy(
            src_ref=stage.at[slot], dst_ref=docs.at[slot], send_sem=doc_send.at[slot], recv_sem=doc_recv.at[slot],
            device_id=(lax.rem(me - OFFSETS[slot] + n, n), core), device_id_type=MESH,
        )

    def pass_on(slot):
        return pltpu.make_async_remote_copy(
            src_ref=docs.at[slot], dst_ref=docs_sib.at[slot], send_sem=fwd_send.at[slot], recv_sem=fwd_recv.at[slot],
            device_id=sibling, device_id_type=MESH,
        )

    sources = [tok_in, pos_in, vec_own] + weights_in + [cot_in]
    targets = [tok_sib] + theirs[1:] + [theirs[0]]

    def share(index):
        return pltpu.make_async_remote_copy(
            src_ref=sources[index], dst_ref=targets[index], send_sem=sib_send.at[index], recv_sem=sib_recv.at[index],
            device_id=sibling, device_id_type=MESH,
        )

    doc_load = pltpu.make_async_copy(docs_in, doc_buf, misc_sem.at[0])
    tok_load = pltpu.make_async_copy(tok_in, tok, misc_sem.at[1])
    to_scalar = pltpu.make_async_copy(got, got_s, misc_sem.at[2])

    @pl.when(fresh)
    def _():
        doc_load.start()
        one = jnp.int32(1)
        zero = jnp.int32(0)
        offsets = [lax.rem(owner[0, k] - me + REACH + n, n) - REACH for k in range(row_count)]
        slots = [sum(jnp.where(o == OFFSETS[slot], slot * one, zero) for slot in range(SLOTS)) for o in offsets]
        ranks = []
        for k in range(row_count):
            ranks.append(sum(jnp.where(slots[j] < slots[k], one, zero) for j in range(row_count) if j != k))
            rank_out[k] = ranks[k]
        for slot in range(SLOTS):
            asked_for = sum(jnp.where(slots[k] == slot, doc_slot[0, k] + 1, zero) for k in range(row_count)) - 1
            req[slot] = jnp.full(req.shape[1:], asked_for, jnp.int32)
        vec_own[...] = jnp.zeros_like(vec_own)
        for index, vector in enumerate(vectors):
            for i in range(vector.shape[0] // half):
                vec_own[index + i] = vector[i * half:(i + 1) * half]
        greet(ring_partners(me, core, n) + [sibling])
        for slot in REMOTE:
            request(slot).start()
        for index in range(len(sources)):
            share(index).start()
        tok_load.start()
        halves.start_own()
        for rank in range(row_count):
            slot = sum(jnp.where(ranks[k] == rank, slots[k], zero) for k in range(row_count))
            row = sum(jnp.where(ranks[k] == rank, k * one, zero) for k in range(row_count))
            slot_of[rank] = slot
            picks[rank] = slot
            picks[row_count + rank] = jnp.minimum(row, row_count - 1)
        got[LOCAL] = req[LOCAL]
        for slot in REMOTE:
            request(slot).wait()
        to_scalar.start()
        doc_load.wait()
        to_scalar.wait()
        for slot in range(SLOTS):
            want[slot] = got_s[slot, 0, 0]
        for slot in REMOTE[:early - 1]:
            stage[slot] = doc_buf[jnp.clip(got_s[slot, 0, 0], 0, doc_buf.shape[0] - 1)]
            document(slot).start()
        docs[LOCAL] = doc_buf[jnp.clip(got_s[LOCAL, 0, 0], 0, doc_buf.shape[0] - 1)]
        pass_on(LOCAL).start()
        for slot in range(early, SLOTS):
            stage[slot] = doc_buf[jnp.clip(got_s[slot, 0, 0], 0, doc_buf.shape[0] - 1)]
        for index in range(len(sources)):
            share(index).wait()
        halves.start_theirs()
        tok_load.wait()
        for slot in REMOTE[:early - 1]:
            document(slot).wait_recv()
            pass_on(slot).start()
            if slot == LATE_START:
                for late in range(early, early + LATE_FIRST):
                    document(late).start()
        for slot in range(early):
            pass_on(slot).wait_recv()

    for step in range(1, all_rows):

        @pl.when(b == step)
        def _(step=step):
            for slot in range(early + 2 * step - 2, early + 2 * step):
                pass_on(slot).wait_recv()

    def take_late(step):
        for slot in range(early + 2 * step, early + 2 * step + 2):
            document(slot).wait_recv()
            pass_on(slot).start()
        for slot in range(early + LATE_FIRST + 2 * step, min(SLOTS, early + LATE_FIRST + 2 * step + 2)):
            document(slot).start()

    def need(*names):
        @pl.when(fresh)
        def _():
            for name in names:
                halves.wait(name)

    first = core == 0
    my_rank = 2 * b + core

    def join(a, b):
        a, b = a.astype(F32), b.astype(F32)
        return jnp.concatenate([jnp.where(first, a, b), jnp.where(first, b, a)], axis=1)

    def chosen(held):
        value = held[my_rank]
        for i in range(1, SLOTS - row_count + 1):
            value = jnp.where(picks[my_rank] == my_rank + i, held[my_rank + i], value)
        return value

    need("pos", "vec")
    table = pos.shape[0]
    row = picks[row_count + my_rank]
    seg_row = segments[pl.ds(row, 1), :]
    one_hot = (column(places[pl.ds(row, 1), :]) == lax.broadcasted_iota(jnp.int32, (seq, table), 1)).astype(F32).astype(BF)
    embedded = join(tok[row], tok_sib[row]) + mm(one_hot, pos[...]) + join(chosen(docs), chosen(docs_sib))
    low = embedded.astype(BF)
    xlow[0] = low
    acc[...] = embedded
    need("qkv")
    q = (mm(low, wqkv[:, 0:full]) + wide(vec, VQ)).astype(BF)
    qkv[0, :, 0:full] = q * jnp.asarray(HEAD_DIM ** -0.5, BF)
    qkv[0, :, full:2 * full] = mm(low, wqkv[:, full:2 * full]).astype(BF)
    qkv[0, :, 2 * full:] = (mm(low, wqkv[:, 2 * full:]) + wide(vec, VV)).astype(BF)
    bias[...] = jnp.where(column(seg_row) == seg_row, 0.0, NEGATIVE)
    stats[...] = jnp.zeros_like(stats)
    masks = head_masks(GANG)
    wide_gang = GANG * HEAD_DIM

    def heads(p):
        at = p * wide_gang
        queries = qkv[0, :, pl.ds(at, wide_gang)]
        keys = qkv[0, :, pl.ds(full + at, wide_gang)]
        values = qkv[0, :, pl.ds(2 * full + at, wide_gang)]
        lane = lax.broadcasted_iota(jnp.int32, (seq, wide_gang), 1)
        small_lane = lax.broadcasted_iota(jnp.int32, (seq, 128), 1)
        s = nt(jnp.concatenate([queries * m for m in masks], axis=0), keys)
        es, totals = [], []
        for h in range(GANG):
            sh = s[h * seq:(h + 1) * seq] + bias[...]
            top = jnp.max(sh, axis=1, keepdims=True)
            e = jnp.exp(sh - top)
            total = jnp.sum(e, axis=1, keepdims=True)
            es.append(e.astype(BF))
            totals.append(1.0 / total)
            stats[0:seq, :] = jnp.where(small_lane == GANG * p + h, top + jnp.log(total), stats[0:seq, :])
        out = mm(jnp.concatenate(es, axis=0), values)
        joined = out[0:seq] * totals[0]
        for h in range(1, GANG):
            joined = jnp.where(lane < h * HEAD_DIM, joined, out[h * seq:(h + 1) * seq] * totals[h])
        ctx[0, :, pl.ds(at, wide_gang)] = joined.astype(BF)

    for p in range(full // wide_gang):
        heads(p)
    lse[0] = jnp.transpose(stats[...])[0:lse.shape[1], 0:seq]
    need("wo")
    normed, inverse = normalize(acc[...] + mm(ctx[0], wo[...]) + wide(vec, VO))
    middle = normed * wide(vec, VGA) + wide(vec, VSA)
    nmid[0] = normed.astype(BF)
    imid[0] = inverse
    acc[...] = middle + wide(vec, VBO)
    mlow[0] = middle.astype(BF)
    need("wi", "wu", "wc", "cot")
    for j in range(wi.shape[0]):
        if j == LATE_AT:
            for step in range(all_rows - 1):

                @pl.when(b == step)
                def _(step=step):
                    take_late(step)

        pre = mm(mlow[0], wi[j]) + wide(vec, VIN + j)
        phi = 0.5 + 0.5 * lax.erf(pre * (0.5 ** 0.5))
        act[0, j] = (pre * phi).astype(BF)
        slope[0, j] = (phi + pre * (jnp.exp(-0.5 * pre * pre) * 0.3989422804014327)).astype(BF)
        acc[...] += mm(act[0, j], wu[j])
    normed, inverse = normalize(acc[...])
    nout[0] = normed.astype(BF)
    iout[0] = inverse
    result = (normed * wide(vec, VGF) + wide(vec, VSF)).astype(BF)
    res[0] = result
    summ[0] = mm(res[0, 0:16, :], wc[...])[0:8]
    product = jnp.sum(cot[...].astype(F32) * result.astype(F32))
    prod[0] = jnp.full(prod.shape[1:], product, F32)

    @pl.when(b == rows - 1)
    def _():
        for slot in REMOTE:
            document(slot).wait_send()
        for slot in range(SLOTS):
            pass_on(slot).wait_send()


def forward(n, owner, doc_slot, places, segments, vectors, doc_store, tokens, cot, pos, weights):
    all_rows, seq, half = tokens.shape
    rows = all_rows // 2
    full = 2 * half
    hidden = 2 * weights[4].shape[1]
    shape = jax.ShapeDtypeStruct
    heads = full // HEAD_DIM
    lse_rows = (heads + 7) // 8 * 8
    vec = shape((VROWS, half), F32)
    own = (cot, pos, vec) + weights
    acts = [
        ((seq, full), BF), ((seq, 3 * full), BF), ((lse_rows, seq), F32), ((seq, full), BF),
        ((seq, full), BF), ((seq, 1), F32), ((seq, full), BF), ((hidden // full, seq, full), BF), ((hidden // full, seq, full), BF),
        ((seq, full), BF), ((seq, 1), F32), ((seq, full), BF), ((8, PROJ), F32), ((8, PROJ), F32),
    ]
    acts = [shape((rows,) + dims, kind) for dims, kind in acts]
    smem = pl.BlockSpec(memory_space=pltpu.SMEM)
    dma = pltpu.SemaphoreType.DMA
    outs = [shape(o.shape, o.dtype) for o in own] + [vec]
    outs += [shape((count,), jnp.int32) for count in (SLOTS, all_rows, all_rows, 2 * all_rows)]
    result = pl.pallas_call(
        functools.partial(forward_kernel, n),
        out_shape=tuple(outs + acts),
        grid=(rows,),
        in_specs=[smem, smem] + [whole_block(a) for a in (places, segments) + tuple(vectors)] + any_spec(11),
        out_specs=tuple(any_spec(10) + [whole_block(vec)] + [smem] * 4 + [row_block(a) for a in acts]),
        scratch_shapes=[
            pltpu.VMEM((seq, seq), F32), pltpu.VMEM((384, 128), F32), pltpu.VMEM((seq, full), F32),
        ] + whole_scratch(own, "cot", "pos", "vec", "wqkv", "wo", "wi", "wu", "wc") + [
            pltpu.VMEM(doc_store.shape, BF), pltpu.VMEM((SLOTS, seq, half), BF),
            pltpu.VMEM((SLOTS, seq, half), BF), pltpu.VMEM((SLOTS, seq, half), BF),
            pltpu.VMEM(tokens.shape, BF), pltpu.VMEM(tokens.shape, BF),
            pltpu.VMEM((SLOTS, 8, 128), jnp.int32), pltpu.VMEM((SLOTS, 8, 128), jnp.int32),
            pltpu.SMEM((SLOTS, 8, 128), jnp.int32),
            dma((SLOTS,)), dma((SLOTS,)), dma((SLOTS,)), dma((SLOTS,)), dma((SLOTS,)), dma((SLOTS,)),
            dma((11,)), dma((11,)), dma((3,)),
        ],
        compiler_params=pltpu.CompilerParams(
            collective_id=0, has_side_effects=True, vmem_limit_bytes=VMEM_LIMIT
        ),
        name="forward",
    )(owner, doc_slot, places, segments, *vectors, doc_store, tokens, cot, pos, *weights)
    return result[:10], result[10], result[11:15], result[15:]


def norm_back(upstream, normed, inverse, gain):
    scaled = upstream * gain
    first = jnp.mean(scaled, axis=-1, keepdims=True)
    second = jnp.mean(scaled * normed, axis=-1, keepdims=True)
    return inverse * (scaled - first - normed * second)


def add_vec(vecs, row, value):
    half = value.shape[1] // 2
    vecs[0, row:row + 1, :] += value[:, :half]
    vecs[1, row:row + 1, :] += value[:, half:]


def token_sum(values):
    return jnp.sum(values, axis=0, keepdims=True)


def spread(value, target):
    _, n, depth, width = target.shape
    for side in range(2):
        for i in range(n):
            target[side, i] = value[i * depth:(i + 1) * depth, side * width:(side + 1) * width].astype(target.dtype)


def shares_kernel(summ, prod, qv, iout, nout_in, res_in, *refs):
    own, theirs = refs[:10], refs[10:20]
    douter, mixed, vecs, dw_cls, gq = refs[20:25]
    mine, got, nout, res, cot, vec, wc, halves_sem, send_sem, recv_sem, load_sem = refs[25:]
    me = lax.axis_index("dp")
    core = lax.axis_index("mp")
    sibling = (me, 1 - core)
    rows = summ.shape[0]
    halves = Halves(halves_sem)
    spread_halves(halves, own, theirs, vec=vec, cot=cot, wc=wc)
    halves.start()
    loads = [
        pltpu.make_async_copy(res_in, res, load_sem.at[0]),
        pltpu.make_async_copy(nout_in, nout, load_sem.at[1]),
    ]
    for load in loads:
        load.start()
    greet([sibling])
    mine[...] = jnp.concatenate([summ[b, 0:1, :] for b in range(rows)] + [prod[b, 0:1, :] for b in range(rows)], axis=0)
    copy = pltpu.make_async_remote_copy(
        src_ref=mine, dst_ref=got, send_sem=send_sem, recv_sem=recv_sem,
        device_id=sibling, device_id_type=MESH,
    )
    copy.start()
    vecs[...] = jnp.zeros_like(vecs)
    copy.wait()
    first = core == 0
    low = jnp.where(first, mine[...], got[...])
    high = jnp.where(first, got[...], mine[...])
    summary = jnp.concatenate([low[:rows], high[:rows]], axis=0)
    product = jnp.concatenate([low[rows:], high[rows:]], axis=0)
    inv_root = PROJ ** (-0.5)
    logits = jnp.sum(summary * qv[...], axis=1, keepdims=True) * inv_root
    e = jnp.exp(logits - jnp.max(logits, axis=0, keepdims=True))
    share = e / jnp.sum(e, axis=0, keepdims=True)
    dlogits = share * (product - jnp.sum(share * product, axis=0, keepdims=True))
    gq[...] = jnp.sum(dlogits * summary, axis=0, keepdims=True) * inv_root
    ds = dlogits * qv[...] * inv_root
    wide_share = share + jnp.zeros_like(ds)
    shares = jnp.where(first, wide_share, jnp.concatenate([wide_share[rows:], wide_share[:rows]], axis=0))
    dsum = jnp.where(first, ds, jnp.concatenate([ds[rows:], ds[:rows]], axis=0))
    halves.wait("vec")
    halves.wait("cot")
    halves.wait("wc")
    extra = lax.dot_general(
        dsum, wc[...].astype(F32), (((1,), (1,)), ((), ())), preferred_element_type=F32, precision=PRECISE
    )
    for load in loads:
        load.wait()
    seq, full = cot.shape
    heads = jnp.concatenate([res[b, 0:1, :].astype(F32) for b in range(rows)], axis=0)
    heads = jnp.concatenate([heads, jnp.zeros_like(heads)], axis=0)
    product = lax.dot_general(dsum, heads, (((0,), (0,)), ((), ())), preferred_element_type=F32, precision=PRECISE)
    spread(product, dw_cls)
    row = lax.broadcasted_iota(jnp.int32, (seq, 1), 0)
    for b in range(rows):
        share_b = shares[b:b + 1, 0:1]
        part = share_b * res[b].astype(F32)
        mixed[...] = part if b == 0 else mixed[...] + part
        upstream = share_b * cot[...].astype(F32) + jnp.where(row == 0, extra[b:b + 1], 0.0)
        upstream = upstream.astype(BF).astype(F32)
        normed = nout[b].astype(F32)
        dout = norm_back(upstream, normed, iout[b], wide(vec, VGF))
        add_vec(vecs, VGF, token_sum(upstream * normed))
        add_vec(vecs, VSF, token_sum(upstream))
        add_vec(vecs, VBO, token_sum(dout))
        douter[b] = dout.astype(BF)


def share_out(n, summ, prod, qv, iout, nout, res, own, theirs):
    rows, seq, full = res.shape
    shape = jax.ShapeDtypeStruct
    return pl.pallas_call(
        shares_kernel,
        out_shape=(
            shape((rows, seq, full), BF), shape((seq, full), F32), shape((2, VROWS, full // 2), F32),
            shape((2, n, PROJ // n, full // 2), F32), shape((1, PROJ), F32),
        ),
        in_specs=vmem_spec(4) + any_spec(22),
        out_specs=tuple(vmem_spec(5)),
        scratch_shapes=[
            pltpu.VMEM((2 * rows, PROJ), F32), pltpu.VMEM((2 * rows, PROJ), F32),
            pltpu.VMEM(nout.shape, BF), pltpu.VMEM(res.shape, BF),
        ] + whole_scratch(own, "cot", "vec", "wc") + [
            pltpu.SemaphoreType.DMA, pltpu.SemaphoreType.DMA, pltpu.SemaphoreType.DMA((2,)),
        ],
        compiler_params=pltpu.CompilerParams(collective_id=1, has_side_effects=True, vmem_limit_bytes=VMEM_LIMIT),
        name="shares",
    )(summ, prod, qv, iout, nout, res, *own, *theirs)


def with_bit(index, position, bit):
    low = 1 << position
    return (index // low) * (2 * low) + bit * low + index % low


def across(bit):
    me = lax.axis_index("dp")
    here = (me // (1 << bit)) % 2
    return here, (me + (1 - 2 * here) * (1 << bit), lax.axis_index("mp"))


HANDED = 2


class Group:
    def __init__(self, n, bits, bufs, sems, index, near, start=0):
        self.n, self.bits, self.near, self.start = n, bits, near, start
        bufs = list(bufs)
        self.mine = bufs.pop(0)
        self.theirs = bufs.pop(0) if start == 0 else None
        self.out, self.came = [None] * start + bufs[0::2], [None] * start + bufs[1::2]
        self.send_sem, self.recv_sem, self.own_sem, self.index = sems[0], sems[1], sems[2], index
        self.levels = len(bits)

    @staticmethod
    def scratch(n, rows, width, kind, start=0):
        levels = n.bit_length() - 1
        shapes = [(n >> start, rows, width)] * (2 if start == 0 else 1)
        for level in range(start, levels):
            shapes += [(n >> (level + 1), rows, width)] * 2
        return [pltpu.VMEM(s, kind) for s in shapes]

    @staticmethod
    def size(n, start=0):
        return (2 if start == 0 else 1) + 2 * (n.bit_length() - 1 - start)

    def remote(self, level, src, dst, target):
        return pltpu.make_async_remote_copy(
            src_ref=src, dst_ref=dst, send_sem=self.send_sem.at[self.index, level],
            recv_sem=self.recv_sem.at[self.index, level], device_id=target, device_id_type=MESH,
        )

    @staticmethod
    def handing_scratch(n, rows, width, kind):
        shapes = [(2, n, rows, width), (n, rows, width)]
        for level in range(HANDED):
            shapes += [(n >> (level + 1), rows, width)] * 2
        return [pltpu.VMEM(s, kind) for s in shapes]

    def first(self, src):
        return self.remote(0, src, self.theirs, self.near["sibling"])

    def load_own(self, src):
        return pltpu.make_async_copy(src, self.mine, self.own_sem.at[self.index])

    def hop(self, level):
        return self.remote(level + 1, self.out[level], self.came[level], self.near[self.bits[level]][1])

    def left(self, level):
        return [bit for bit in range(self.levels) if bit not in self.bits[:level]]

    def places(self, level, t, side=0):
        digit = {bit: self.near[bit][0] for bit in self.bits[self.start:level]}
        if level < self.levels:
            digit[self.bits[level]] = side
        for k, bit in enumerate(self.left(level + 1)):
            digit[bit] = (t >> k) & 1
        held = sum(digit[bit] * (1 << k) for k, bit in enumerate(self.left(self.start)))
        came = sum(digit[bit] * (1 << k) for k, bit in enumerate(self.left(level)))
        return held, came

    def advance(self, level):
        came = self.theirs if level == 0 else self.came[level - 1]
        here = self.near[self.bits[level]][0]
        count = self.n >> (level + 1)
        handed = self.start > 0 and level == self.start
        for t in range(count):
            at, of = self.places(level, t, 1 - here)
            self.out[level][t] = self.mine[at] if handed else self.mine[at] + came[of]
        self.hop(level).start()
        if not handed:
            for t in range(count):
                at, of = self.places(level, t, here)
                self.mine[at] = self.mine[at] + came[of]

    def hand_on(self, level, target):
        for t in range(self.n >> level):
            digit = {bit: self.near[bit][0] for bit in self.bits[:level]}
            for k, bit in enumerate(self.left(level)):
                digit[bit] = (t >> k) & 1
            at = sum(digit[bit] * (1 << bit) for bit in range(self.levels))
            target[t] = self.mine[at] + self.came[level - 1][t]

    def total(self):
        at, _ = self.places(self.levels, 0)
        return self.mine[at].astype(F32) + self.came[-1][0].astype(F32)


def bit_orders(n):
    rest = tuple(range(3, n.bit_length() - 1))
    return (0, 1, 2) + rest, (1, 2, 0) + rest, (2, 0, 1) + rest


def neighbours(n):
    near = {bit: across(bit) for bit in range(n.bit_length() - 1)}
    near["core"] = lax.axis_index("mp")
    near["sibling"] = (lax.axis_index("dp"), 1 - near["core"])
    return near


def bit_partners(n, near):
    return [near["sibling"]] + [near[bit][1] for bit in range(n.bit_length() - 1)]


class Reducer:
    @staticmethod
    def plan(n, mats):
        pieces = []
        for index, mat in enumerate(mats):
            if mat.shape[1] == n:
                pieces.append((index, 0, mat.shape[3], 0, index % 3))
            else:
                pieces += [(index, g * mat.shape[3], mat.shape[3], HANDED, g % 3) for g in range(mat.shape[0])]
        return pieces

    @staticmethod
    def scratch(n, mats):
        shapes = []
        pieces = Reducer.plan(n, mats)
        for index, _, width, start, _ in pieces:
            shapes += Group.scratch(n, mats[index].shape[-2], width, mats[index].dtype, start)
        dma = pltpu.SemaphoreType.DMA
        levels = n.bit_length()
        return shapes + [dma((len(pieces), levels)), dma((len(pieces), levels)), dma((len(pieces),))]

    def __init__(self, n, mats, outs, refs, near):
        self.mats, self.outs, self.near = mats, outs, near
        self.pieces = Reducer.plan(n, mats)
        orders = bit_orders(n)
        refs = list(refs)
        self.groups = []
        for index, (_, begin, width, start, order) in enumerate(self.pieces):
            size = Group.size(n, start)
            self.groups.append(Group(n, orders[order], refs[:size], refs[-3:], index, near, start))
            del refs[:size]

    def source(self, index, side):
        mat, begin, width, start, _ = self.pieces[index]
        return self.mats[mat].at[begin // width if start else side]

    def start(self):
        core = self.near["core"]
        for index, group in enumerate(self.groups):
            if not group.start:
                group.first(self.source(index, 1 - core)).start()
            group.load_own(self.source(index, core)).start()

    def move(self, mat, level):
        core = self.near["core"]
        for index, group in enumerate(self.groups):
            at, begin, width, start, _ = self.pieces[index]
            if at != mat:
                continue
            if level == start:
                group.load_own(self.source(index, core)).wait()
                if not start:
                    group.first(self.source(index, 1 - core)).wait()
            else:
                group.hop(level - 1).wait()
            if level < group.levels:
                group.advance(level)
            else:
                self.outs[mat][:, begin:begin + width] = group.total()


def middle_kernel(n, handed_count, summed, vecs_in, imid, *refs):
    refs = list(refs)

    def take(count):
        taken = refs[:count]
        del refs[:count]
        return taken

    own, theirs = take(10), take(10)
    douter_in, act_in, slope_in, mlow_in, nmid_in, ctx_in = take(6)
    dattn_out, vecs = take(2)
    handed, late_inner, late_last, dw_out = take(4) if summed else (None,) * 4
    dinner_out = None if summed else take(1)[0]
    douter, dinner, mlow, nmid, ctx, dattn, acts, slopes, acc, vec, wi, wu, halves_sem, load_sem = take(14)
    rows, seq, full = acc.shape
    half = full // 2
    chunks = wi.shape[0]
    near = neighbours(n)
    core = near["core"]
    halves = Halves(halves_sem)
    spread_halves(halves, own, theirs, vec=vec, wu=wu, wi=wi)

    def chunk_load(source, target, j, base):
        return pltpu.make_async_copy(source.at[:, j], target.at[j % 2], load_sem.at[base + j])

    def act_load(j):
        return chunk_load(act_in, acts, j, 8)

    def slope_load(j):
        return chunk_load(slope_in, slopes, j, 8 + chunks)

    pairs = ((douter_in, douter), (mlow_in, mlow), (nmid_in, nmid), (ctx_in, ctx))
    plain = [pltpu.make_async_copy(src, dst, load_sem.at[index]) for index, (src, dst) in enumerate(pairs)]
    plain[0].start()
    if summed:
        act_load(0).start()
        act_load(1).start()
    slope_load(0).start()
    halves.start()
    slope_load(1).start()
    for load in plain[1:]:
        load.start()
    vecs[...] = vecs_in[...]
    groups = []
    if summed:
        orders = bit_orders(n)
        size = 2 + 2 * HANDED
        sems = refs[-2:] + [None]
        pair_of = []
        for index in range(handed_count):
            pair, *bufs = take(size)
            pair_of.append(pair)
            groups.append(Group(n, orders[index % 3], [pair.at[core]] + bufs, sems, index, near))
        greet(bit_partners(n, near))
    plain[0].wait()

    def flat(ref):
        return ref[...].reshape(rows * seq, full)

    def begin(index, left, right):
        spread(tn(left, right), pair_of[index])
        groups[index].first(pair_of[index].at[1 - core]).start()

    def move(index, level):
        if level == 0:
            groups[index].first(pair_of[index].at[1 - core]).wait()
        else:
            groups[index].hop(level - 1).wait()
        groups[index].advance(level)

    if summed:
        for j in range(chunks):
            act_load(j).wait()
            if j >= 2:
                move(j - 2, 0)
            begin(j, flat(douter), acts[j % 2].reshape(rows * seq, full))
            if j + 2 < chunks:
                act_load(j + 2).start()
    moves = {
        (0, 0): ((2, 0),), (0, 1): ((3, 0),), (0, 2): ((0, 1),), (1, 1): ((1, 1), (4, 0)), (1, 2): ((2, 1),),
        (2, 1): ((3, 1), (5, 0)), (2, 2): ((4, 1),), (3, 2): ((5, 1),),
    }

    def moved(j, point):
        for index, level in moves.get((j, point), ()) if summed else ():
            move(index, level)

    acc[...] = douter[...].astype(F32)
    halves.wait("vec")
    halves.wait("wu")
    halves.wait("wi")
    plain[1].wait()
    for j in range(chunks):
        slope_load(j).wait()
        for m in range(0, rows, 2):
            moved(j, m // 2)
            part = nt(douter[m:m + 2].reshape(2 * seq, full), wu[j])
            part = part * slopes[j % 2, m:m + 2].reshape(2 * seq, full).astype(F32)
            low = part.astype(BF)
            dinner[m:m + 2] = low.reshape(2, seq, full)
            sums = token_sum(part)
            for side in range(2):
                vecs[side, VIN + j:VIN + j + 1, :] += sums[:, side * half:(side + 1) * half]
            acc[m:m + 2] += nt(low, wi[j]).reshape(2, seq, full)
        if j + 2 < chunks:
            slope_load(j + 2).start()
        moved(j, 2)
        if not summed:
            copy = pltpu.make_async_copy(dinner, dinner_out.at[j], load_sem.at[4])
            copy.start()
            copy.wait()
        elif chunks + j < handed_count:
            begin(chunks + j, flat(mlow), flat(dinner))
        else:
            spread(tn(flat(mlow), flat(dinner)), (late_inner, late_last)[chunks + j - handed_count])
    plain[2].wait()
    for r in range(rows):
        upstream = acc[r]
        normed = nmid[r].astype(F32)
        middle = norm_back(upstream, normed, imid[r], wide(vec, VGA))
        add_vec(vecs, VGA, token_sum(upstream * normed))
        add_vec(vecs, VSA, token_sum(upstream))
        add_vec(vecs, VO, token_sum(middle))
        dattn[r] = middle.astype(BF)
    done = pltpu.make_async_copy(dattn, dattn_out, load_sem.at[5])
    done.start()
    plain[3].wait()
    if summed:
        spread(tn(flat(dattn), flat(ctx)), dw_out)
        for index, group in enumerate(groups):
            group.hop(HANDED - 1).wait()
            group.hand_on(HANDED, handed.at[index])
    done.wait()


def middle(n, summed, douter, act, slope, mlow, nmid, imid, ctx, vecs, own, theirs):
    rows, seq, full = douter.shape
    half = full // 2
    chunks = act.shape[1]
    shape = jax.ShapeDtypeStruct
    dma = pltpu.SemaphoreType.DMA
    outs = [shape((rows, seq, full), BF), shape(vecs.shape, F32)]
    specs = any_spec(1) + vmem_spec(1)
    handed_count = chunks + 2
    depth = full // n
    scratch = [pltpu.VMEM((rows, seq, full), BF)] * 6 + [pltpu.VMEM((2, rows, seq, full), BF)] * 2
    scratch += [pltpu.VMEM((rows, seq, full), F32)] + whole_scratch(own, "vec", "wi", "wu") + [dma((8 + 2 * chunks,))]
    params = dict(vmem_limit_bytes=VMEM_LIMIT)
    if summed:
        outs.append(shape((handed_count, n >> HANDED, depth, half), BF))
        outs += [shape((2, n, depth, half), BF)] * 3
        specs += vmem_spec(4)
        for _ in range(handed_count):
            scratch += Group.handing_scratch(n, depth, half, BF)
        scratch += [dma((handed_count, HANDED + 1))] * 2
        params.update(collective_id=3, has_side_effects=True)
    else:
        outs.append(shape((chunks, rows, seq, full), BF))
        specs += any_spec(1)
    return pl.pallas_call(
        functools.partial(middle_kernel, n, handed_count, summed),
        out_shape=tuple(outs),
        in_specs=vmem_spec(2) + any_spec(26),
        out_specs=tuple(specs),
        scratch_shapes=scratch,
        compiler_params=pltpu.CompilerParams(**params),
        name="middle",
    )(vecs, imid, *own, *theirs, douter, act, slope, mlow, nmid, ctx)


SEND_AT = 2
VEC_AT = 1
TAIL_TIMES = (
    (3, 0, 2), (7, 0, 3), (7, 1, 0), (8, 2, 0), (8, 3, 0), (8, 4, 0), (14, 0, 4),
    (15, 1, 1), (15, 2, 1), (15, 3, 1), (15, 4, 1), (22, 1, 2), (22, 2, 2), (22, 3, 2), (22, 4, 2),
)


def tail_kernel(n, mat_count, slot_row, picks, vecs_in, places, segments, dattn, qkv, lse, mixed_in, xlow, *refs):
    refs = list(refs)

    def take(count):
        taken = refs[:count]
        del refs[:count]
        return taken

    own, theirs, mats = take(10), take(10), take(mat_count)
    gt, arrived, mixed, vec_out = take(4)
    spare = [] if mats else take(2)
    sums_out = take(mat_count)
    small_out = take(4) if mats else []
    bias, grads, dqkv, dstart, gt_v, stage, mix_own, mix_got, late, late_far, late_all, vec_far, vec_rows, vec_got, vec_sums, wqkv, wo, halves_sem = take(18)
    own_sem, sib_send, sib_recv, doc_send, doc_recv, vec_send, vec_recv, late_send, late_recv = take(9)
    x_v = outgoing = None
    small = []
    near = neighbours(n)
    if mats:
        x_v, *outgoing = take(5)
        orders = bit_orders(n)
        count = 4 * Group.size(n) + 3
        small_refs = take(count)
        for index in range(4):
            size = Group.size(n)
            bufs = small_refs[index * size:(index + 1) * size]
            small.append(Group(n, orders[(0, 1, 2, 0)[index]], bufs, small_refs[-3:], index, near))
        summer = Reducer(n, mats, sums_out, refs, near)
    b = pl.program_id(0)
    rows = pl.num_programs(0)
    me = lax.axis_index("dp")
    core = near["core"]
    other = 1 - core
    sibling = near["sibling"]
    levels = n.bit_length() - 1
    row_count, _, half = gt_v.shape
    all_rows = row_count // 2
    seq, full = grads.shape
    gang = GANG
    pair = gang * HEAD_DIM
    pairs = full // pair
    halves = Halves(halves_sem)
    spread_halves(halves, own, theirs, wo=wo)
    for index in range(3):
        halves.add("qkv", own[3 + index], theirs[3 + index], wqkv, 1, index * half, 3 * half)
    here_cols = pl.ds(pl.multiple_of(core * half, half), half)
    there_cols = pl.ds(pl.multiple_of(other * half, half), half)
    first_core = core == 0

    def push(row):
        at = pl.ds(pl.multiple_of(row * seq, seq), seq)
        return pltpu.make_async_remote_copy(
            src_ref=dstart.at[at, there_cols], dst_ref=gt_v.at[2 * row + core],
            send_sem=sib_send.at[row], recv_sem=sib_recv.at[row], device_id=sibling, device_id_type=MESH,
        )

    def document(slot):
        if slot == LOCAL:
            return pltpu.make_async_copy(stage.at[slot], arrived.at[slot], own_sem.at[2])
        return pltpu.make_async_remote_copy(
            src_ref=stage.at[slot], dst_ref=arrived.at[slot], send_sem=doc_send.at[slot], recv_sem=doc_recv.at[slot],
            device_id=(lax.rem(me + OFFSETS[slot] + n, n), core), device_id_type=MESH,
        )

    def pack(slot):
        lowest, highest = max(0, slot - (SLOTS - row_count)), min(row_count - 1, slot)
        value = gt_v[lowest]
        for rank in range(lowest + 1, highest + 1):
            value = jnp.where(slot_row[rank] == slot, gt_v[rank], value)
        stage[slot] = value

    mix_far = pltpu.make_async_remote_copy(
        src_ref=mixed_in.at[:, there_cols], dst_ref=mix_got, send_sem=sib_send.at[all_rows],
        recv_sem=sib_recv.at[all_rows], device_id=sibling, device_id_type=MESH,
    )
    mix_load = pltpu.make_async_copy(mixed_in.at[:, here_cols], mix_own, own_sem.at[0])
    vec_copy = pltpu.make_async_remote_copy(
        src_ref=vecs_in.at[other], dst_ref=vec_far, send_sem=vec_send.at[0], recv_sem=vec_recv.at[0],
        device_id=sibling, device_id_type=MESH,
    )

    def vec_hop(again, step):
        to = lax.rem(me + step, n)
        src, dst = (vec_sums.at[me], vec_sums.at[me]) if again else (vec_rows.at[to], vec_got.at[me])
        return pltpu.make_async_remote_copy(
            src_ref=src, dst_ref=dst, send_sem=vec_send.at[again * n + step], recv_sem=vec_recv.at[again * n + step],
            device_id=(to, core), device_id_type=MESH,
        )

    def vec_out_rows():
        vec_copy.wait()
        held = vecs_in[core] + vec_far[...]
        depth = held.shape[0] // n
        for i in range(n):
            vec_rows[i] = held[i * depth:(i + 1) * depth]
        for step in range(1, n):
            vec_hop(0, step).start()

    def vec_sum_rows():
        for step in range(1, n):
            vec_hop(0, step).wait()
        total = vec_rows[me]
        for step in range(1, n):
            total = total + vec_got[lax.rem(me + step, n)]
        vec_sums[me] = total
        for step in range(1, n):
            vec_hop(1, step).start()

    late_copy = pltpu.make_async_remote_copy(
        src_ref=late.at[other], dst_ref=late_far, send_sem=late_send.at[0], recv_sem=late_recv.at[0],
        device_id=sibling, device_id_type=MESH,
    )

    def late_hop(step):
        return pltpu.make_async_remote_copy(
            src_ref=late_all.at[me], dst_ref=late_all.at[me], send_sem=late_send.at[step], recv_sem=late_recv.at[step],
            device_id=(lax.rem(me + step, n), core), device_id_type=MESH,
        )

    x_loads = []
    if mats:
        for r in range(all_rows):
            x_loads.append(pltpu.make_async_copy(xlow.at[r], x_v.at[pl.ds(r * seq, seq)], own_sem.at[3 + r]))

    @pl.when(b == 0)
    def _():
        halves.start()
        late[...] = jnp.zeros_like(late)
        everyone = [(lax.rem(me + step, n), core) for step in range(1, n)]
        greet((everyone if mats else ring_partners(me, core, n)) + [sibling])
        if mats:
            summer.start()
        vec_copy.start()
        mix_far.start()
        mix_load.start()
        for load in x_loads:
            load.start()
        halves.wait("wo")
        halves.wait("qkv")

    grads[...] = nt(dattn[0], wo[...]).astype(BF)
    turn = rows - 1 - b
    seg_row = segments[pl.ds(picks[row_count + 2 * turn + core], 1), :]
    bias[...] = jnp.where(column(seg_row) == seg_row, 0.0, NEGATIVE)
    masks = head_masks(gang)
    my_rows = pl.ds(pl.multiple_of(turn * seq, seq), seq)

    def heads(p):
        for step, mat, level in TAIL_TIMES if mats else ():
            if step % pairs == p:

                @pl.when(b == step // pairs)
                def _(mat=mat, level=level):
                    summer.move(mat, level)

        if p == SEND_AT and mats:

            @pl.when(b == 0)
            def _():
                vec_out_rows()

        if p == VEC_AT and mats:

            @pl.when(b == 1)
            def _():
                vec_sum_rows()

        if p == SEND_AT:
            for row in range(1, all_rows):

                @pl.when(b == row)
                def _(row=row):
                    push(all_rows - row).wait()
                    for slot in (SLOTS - 2 * row, SLOTS - 2 * row + 1):
                        pack(slot)
                        document(slot).start()

        at = p * pair
        queries = qkv[0, :, pl.ds(at, pair)]
        keys = qkv[0, :, pl.ds(full + at, pair)]
        values = qkv[0, :, pl.ds(2 * full + at, pair)]
        dctx = grads[:, pl.ds(at, pair)]
        lane = lax.broadcasted_iota(jnp.int32, (seq, pair), 1)
        keys_all = jnp.concatenate([keys * m for m in masks], axis=0)
        s = nt(keys_all, queries)
        dw = nt(jnp.concatenate([values * m for m in masks], axis=0), dctx)
        ws, dss = [], []
        for h in range(gang):
            w = jnp.exp(s[h * seq:(h + 1) * seq] + bias[...] - lse[0, gang * p + h:gang * p + h + 1, :])
            prod = w * dw[h * seq:(h + 1) * seq]
            dss.append((prod - w * token_sum(prod)).astype(BF))
            ws.append(w.astype(BF))
        ds = jnp.concatenate(dss, axis=0)
        dv = mm(jnp.concatenate(ws, axis=0), dctx)
        dk = mm(ds, queries)
        dq = tn(ds, keys_all) * HEAD_DIM ** -0.5

        def join(parts):
            joined = parts[0:seq]
            for h in range(1, gang):
                joined = jnp.where(lane < h * HEAD_DIM, joined, parts[h * seq:(h + 1) * seq])
            return joined

        for t, value in enumerate((dq, join(dk), join(dv))):
            for i in range(0, pair, 128):
                column = at + i
                out_at = (column // half) * (3 * half) + column % half + t * half
                dqkv[my_rows, pl.ds(out_at, 128)] = value[:, i:i + 128].astype(BF)

    for p in range(pairs):
        heads(p)
    total = dattn[0].astype(F32) + nt(dqkv[my_rows, :], wqkv[...])
    for h in range(2):
        for t in (0, 2):
            source = dqkv[my_rows, (3 * h + t) * half:(3 * h + t + 1) * half]
            late[h, t // 2:t // 2 + 1, :] += token_sum(source.astype(F32))
    low = total.astype(BF)
    dstart[my_rows, :] = low
    gt_v[2 * turn + core] = jnp.where(first_core, total[:, :half], total[:, half:]).astype(BF)
    push(turn).start()

    @pl.when(b == rows - 1)
    def _():
        late_copy.start()
        late_copy.wait()
        late_all[me] = late[core] + late_far[...]
        if mats:
            for step in range(1, n):
                late_hop(step).start()
        push(0).wait()
        tok_out = pltpu.make_async_copy(gt_v, gt, own_sem.at[1])
        tok_out.start()
        for slot in reversed(range(SLOTS - 2 * all_rows + 2)):
            pack(slot)
        for slot in reversed(range(SLOTS - 2 * all_rows + 2)):
            document(slot).start()

        if not mats:
            vec_copy.wait()
            vec_out[...] = vecs_in[core] + vec_far[...]
            vec_out[VQ:VV + 1] = late_all[me]
            for source, target in ((dqkv, spare[0]), (dstart, spare[1])):
                copy = pltpu.make_async_copy(source, target, own_sem.at[3])
                copy.start()
                copy.wait()
        else:
            for load in x_loads:
                load.wait()
            table = small_out[3].shape[0] * n
            one_hots = []
            for r in range(all_rows):
                place = places[pl.ds(picks[row_count + 2 * r + core], 1), :]
                here = place == lax.broadcasted_iota(jnp.int32, (table, seq), 0)
                one_hots.append(here.astype(F32).astype(BF))

            def product(index, side, target):
                if index < 3:
                    at = pl.ds(pl.multiple_of(side * 3 * half + index * half, half), half)
                    value = tn(x_v[...], dqkv[:, at])
                else:
                    at = pl.ds(pl.multiple_of(side * half, half), half)
                    value = sum(mm(one_hots[r], dstart[r * seq:(r + 1) * seq, at]) for r in range(all_rows))
                depth = target.shape[1]
                for i in range(n):
                    target[i] = value[i * depth:(i + 1) * depth].astype(target.dtype)

            firsts = []

            def begin(index):
                product(index, other, outgoing[index])
                copy = small[index].first(outgoing[index])
                copy.start()
                firsts.append(copy)
                product(index, core, small[index].mine)

            def step(index, level):
                if level == 0:
                    firsts[index].wait()
                else:
                    small[index].hop(level - 1).wait()
                if level < levels:
                    small[index].advance(level)
                else:
                    small_out[index][...] = small[index].total()

            taken = {}
            for _, mat, level in TAIL_TIMES:
                taken[mat] = max(taken.get(mat, -1), level)
            left = [(mat, level) for level in range(levels + 1) for mat in range(mat_count) if level > taken.get(mat, -1)]

            def some(mat):
                for at, (m, level) in enumerate(left):
                    if m == mat:
                        del left[at]
                        summer.move(mat, level)
                        return

            for index in range(4):
                begin(index)
                step(index, 0)
                if index == 1:
                    for mat in range(1, mat_count):
                        some(mat)
            while left:
                some(left[0][0])
            for level in range(1, levels + 1):
                for index in range(4):
                    step(index, level)
            for step_to in range(1, n):
                vec_hop(1, step_to).wait()
                late_hop(step_to).wait()
            vec_out[...] = jnp.concatenate([vec_sums[i] for i in range(n)], axis=0)
            total = late_all[0]
            for i in range(1, n):
                total = total + late_all[i]
            vec_out[VQ:VV + 1] = total
        mix_load.wait()
        mix_far.wait()
        mixed[...] = (mix_own[...] + mix_got[...]).astype(BF)
        tok_out.wait()
        for slot in range(SLOTS):
            document(slot).wait()


def tail(n, table, slot_of, picks, vecs, places, segments, dattn, qkv, lse, mixed, xlow, own, theirs, mats):
    rows, seq, full = dattn.shape
    half = full // 2
    tokens = rows * seq
    levels = n.bit_length() - 1
    shape = jax.ShapeDtypeStruct
    outs = [shape((2 * rows, seq, half), BF), shape((SLOTS, seq, half), BF), shape((seq, half), BF), shape(vecs.shape[1:], F32)]
    if not mats:
        outs += [shape((tokens, 3 * full), BF), shape((tokens, full), BF)]
    out_specs = any_spec(2) + [whole_block(o) for o in outs[2:4]] + any_spec(len(outs) - 4)
    by_row = (dattn, qkv, lse)
    dma = pltpu.SemaphoreType.DMA
    scratch = [
        pltpu.VMEM((seq, seq), F32), pltpu.VMEM((seq, full), BF), pltpu.VMEM((tokens, 3 * full), BF),
        pltpu.VMEM((tokens, full), BF), pltpu.VMEM((2 * rows, seq, half), BF), pltpu.VMEM((SLOTS, seq, half), BF),
        pltpu.VMEM((seq, half), F32), pltpu.VMEM((seq, half), F32), pltpu.VMEM((2, 2, half), F32),
        pltpu.VMEM((2, half), F32), pltpu.VMEM((n, 2, half), F32), pltpu.VMEM(vecs.shape[1:], F32),
    ] + [pltpu.VMEM((n, max(1, vecs.shape[1] // n), half), F32)] * 3 + whole_scratch(own, "wqkv", "wo") + [
        dma((3 + rows,)), dma((rows + 1,)), dma((rows + 1,)), dma((SLOTS,)), dma((SLOTS,)), dma((2 * n,)), dma((2 * n,)), dma((n,)), dma((n,)),
    ]
    if mats:
        depths = [full // n] * 3 + [table // n]
        scratch += [pltpu.VMEM((tokens, full), BF)] + [pltpu.VMEM((n, depth, half), BF) for depth in depths]
        for depth in depths:
            scratch += Group.scratch(n, depth, half, BF)
        scratch += [dma((4, levels + 1)), dma((4, levels + 1)), dma((4,))]
        scratch += Reducer.scratch(n, mats)
        sums = [shape((m.shape[2], m.shape[3] * (1 if m.shape[1] == n else m.shape[0])), F32) for m in mats] + [shape((depth, half), F32) for depth in depths]
        outs += sums
        out_specs += [whole_block(o) for o in sums]
    return pl.pallas_call(
        functools.partial(tail_kernel, n, len(mats)),
        out_shape=tuple(outs),
        grid=(rows,),
        in_specs=[pl.BlockSpec(memory_space=pltpu.SMEM)] * 2 + [whole_block(a) for a in (vecs, places, segments)]
        + [row_back(a) for a in by_row] + any_spec(22 + len(mats)),
        out_specs=tuple(out_specs),
        scratch_shapes=scratch,
        compiler_params=pltpu.CompilerParams(
            collective_id=2, has_side_effects=True, vmem_limit_bytes=VMEM_LIMIT
        ),
        name="tail",
    )(slot_of, picks, vecs, places, segments, *by_row, mixed, xlow, *own, *theirs, *mats)


PIECES = 3
FINISHED = ("mixed", "pos", "wq", "wk", "wv", "wo", "cls", "gq")


def finish_kernel(names, want, rank, arrived, gt, vec_sum, *refs):
    refs = list(refs)

    def take(count):
        taken = refs[:count]
        del refs[:count]
        return taken

    ins, handed, lates, (docs_out, tokens_out) = take(len(names)), take(1)[0], take(2), take(2)
    outs, (outer, inner), vectors = take(len(names)), take(2), take(9)
    got, total, tok, sems = refs
    docs = docs_out.shape[0]
    row_count, _, half = tokens_out.shape
    loads = [pltpu.make_async_copy(arrived.at[slot], got.at[slot], sems.at[slot]) for slot in range(SLOTS)]
    tok_loads = [pltpu.make_async_copy(gt.at[jnp.minimum(rank[k], row_count - 1)], tok.at[k], sems.at[SLOTS + PIECES + k]) for k in range(row_count)]
    for load in tok_loads + loads:
        load.start()

    for name, source, target in zip(names, ins, outs):
        if name == "mixed":
            target[0] = source[...]
        else:
            target[...] = source[...]
    hidden = outer.shape[1]
    first_inner = handed.shape[1] - hidden
    outer[...] = handed[:, :hidden]
    inner[:, :first_inner] = handed[:, hidden:]
    for index, late in enumerate(lates):
        inner[:, first_inner + index * half:first_inner + (index + 1) * half] = late[...]
    for index, vector in enumerate(vectors):
        for i in range(vector.shape[0] // half):
            vector[i * half:(i + 1) * half] = vec_sum[index + i]
    for load in tok_loads:
        load.wait()
    tok_done = pltpu.make_async_copy(tok, tokens_out, sems.at[SLOTS + PIECES])
    tok_done.start()
    for load in loads:
        load.wait()
    size = got.shape[1] // PIECES
    done = []
    for piece in range(PIECES):
        rows = pl.ds(piece * size, size)

        def clear(d, carry, rows=rows):
            total[d, rows] = jnp.zeros((size, half), F32)
            return carry

        lax.fori_loop(0, docs, clear, 0)
        for slot in range(SLOTS):
            at = jnp.where(want[slot] < 0, docs, jnp.minimum(want[slot], docs))
            total[at, rows] += got[slot, rows].astype(F32)
        copy = pltpu.make_async_copy(total.at[pl.ds(0, docs), rows], docs_out.at[:, rows], sems.at[SLOTS + piece])
        copy.start()
        done.append(copy)
    tok_done.wait()
    for copy in done:
        copy.wait()


def finish(docs, want, rank, arrived, gt, vec_sum, named, handed, lates):
    _, seq, half = arrived.shape
    shape = jax.ShapeDtypeStruct
    names = tuple(named)
    outs = [shape((docs, seq, half), F32), shape(gt.shape, BF)]
    for name, value in named.items():
        outs.append(shape(((1,) if name == "mixed" else ()) + value.shape, value.dtype))
    hidden = (handed.shape[1] + 2 * half) // 2
    outs += [shape((handed.shape[0], hidden), F32)] * 2
    outs += [shape((half * (hidden // half if index == VIN else 1),), F32) for index in range(9)]
    smem = pl.BlockSpec(memory_space=pltpu.SMEM)
    grad_docs, grad_tokens, *rest = pl.pallas_call(
        functools.partial(finish_kernel, names),
        out_shape=tuple(outs),
        in_specs=[smem, smem] + any_spec(2) + vmem_spec(4 + len(names)),
        out_specs=tuple(any_spec(2) + vmem_spec(len(outs) - 2)),
        scratch_shapes=[
            pltpu.VMEM(arrived.shape, BF), pltpu.VMEM((docs + 1, seq, half), F32), pltpu.VMEM(gt.shape, BF),
            pltpu.SemaphoreType.DMA((SLOTS + PIECES + gt.shape[0],)),
        ],
        compiler_params=pltpu.CompilerParams(vmem_limit_bytes=VMEM_LIMIT),
        name="finish",
    )(want, rank, arrived, gt, vec_sum, *named.values(), handed, *lates)
    return grad_docs, grad_tokens, dict(zip(names + ("outer", "inner"), rest)), rest[len(names) + 2:]


def body(
    tokens, segment_ids, positions, query_vectors, doc_owner, doc_slot, doc_store, pos_table,
    w_query, w_key, w_value, b_query, b_value, w_out, b_out, gain_attn, shift_attn,
    w_inner, b_inner, w_outer, b_outer, gain_ffn, shift_ffn, w_cls, cotangent,
):
    n = lax.axis_size("dp")
    core = lax.axis_index("mp")
    row_count, _, half = tokens.shape
    full = 2 * half
    weights = (w_query, w_key, w_value, w_out, w_inner, w_outer, w_cls)
    vectors = (b_query, b_value, b_out, gain_attn, shift_attn, b_outer, gain_ffn, shift_ffn, b_inner)
    theirs, vec_own, (want, rank, slot_of, picks), acts = forward(
        n, doc_owner, doc_slot, positions, segment_ids, vectors, doc_store, tokens, cotangent[0], pos_table, weights
    )
    own = (cotangent[0], pos_table, vec_own) + weights
    xlow, qkv, lse, ctx, nmid, imid, mlow, act, slope, nout, iout, res, summ, prod = acts

    douter, mixed, vecs, dw_cls, grad_query = share_out(n, summ, prod, query_vectors, iout, nout, res, own, theirs)

    def cross(left, right):
        left = left.reshape(-1, left.shape[-1])
        right = right.reshape(-1, right.shape[-1])
        return tn(left, right)

    summed = full // n % 16 == 0
    table = pos_table.shape[0]
    dattn, vecs, *parts = middle(n, summed, douter, act, slope, mlow, nmid, imid, ctx, vecs, own, theirs)
    mats = parts + [dw_cls] if summed else []
    grad_tokens, arrived, mixed_out, vec_sum, *sums = tail(
        n, table, slot_of, picks, vecs, positions, segment_ids, dattn, qkv, lse, mixed, xlow, own, theirs, mats
    )
    if summed:
        handed, late_inner, late_last, g_wo, g_cls, g_q, g_k, g_v, g_pos = sums
    else:
        vec_sum = lax.psum(vec_sum, "dp")
        dqkv, dstart = sums
        place = jnp.take(positions, picks[row_count:].reshape(-1, 2)[:, core], axis=0, mode="clip")
        one_hot = (place.reshape(-1)[:, None] == jnp.arange(table, dtype=jnp.int32)[None, :]).astype(BF)

        def scatter(part):
            part = lax.psum_scatter(part.astype(F32), "mp", scatter_dimension=1, tiled=True)
            return lax.psum_scatter(part, "dp", scatter_dimension=0, tiled=True)

        def in_order(part):
            return part.reshape(full, -1, 2, half).swapaxes(1, 2).reshape(full, -1)

        dinner = parts[0].transpose(1, 2, 0, 3)
        dw_outer = in_order(cross(douter, act.transpose(0, 2, 1, 3).reshape(-1, act.shape[1] * full)))
        dw_inner = in_order(cross(mlow, dinner.reshape(-1, act.shape[1] * full)))
        dw_cls = dw_cls.transpose(1, 2, 0, 3).reshape(PROJ, full)
        g_outer, g_inner, g_wo, g_qkv, g_cls, g_pos = [
            scatter(p) for p in (dw_outer, dw_inner, cross(dattn, ctx), cross(xlow, dqkv), dw_cls, cross(one_hot, dstart))
        ]
        g_q, g_k, g_v = g_qkv[:, :half], g_qkv[:, half:2 * half], g_qkv[:, 2 * half:]
        handed = jnp.concatenate([g_outer, g_inner[:, :-2 * half]], axis=1)
        late_inner, late_last = g_inner[:, -2 * half:-half], g_inner[:, -half:]
    named = dict(zip(FINISHED, (mixed_out, g_pos, g_q, g_k, g_v, g_wo, g_cls, grad_query)))
    grad_docs, grad_tokens, out, vec = finish(
        doc_store.shape[0], want, rank, arrived, grad_tokens, vec_sum, named, handed, (late_inner, late_last)
    )
    return (
        out["mixed"], grad_tokens, out["gq"], grad_docs, out["pos"], out["wq"], out["wk"], out["wv"], vec[VQ], vec[VV],
        out["wo"].T, vec[VO], vec[VGA], vec[VSA], out["inner"], vec[VIN], out["outer"].T, vec[VBO], vec[VGF], vec[VSF],
        out["cls"].T,
    )


def solution(mesh):
    rows = P("dp", None, "mp")
    ids = P("dp", None)
    cols = P(None, "mp")
    vec = P("mp")
    deep = P("mp", None)
    in_specs = (
        rows, ids, ids, ids, ids, ids, rows, cols, cols, cols, cols, vec, vec, deep, vec, vec, vec,
        cols, vec, deep, vec, vec, vec, deep, rows,
    )
    near = P("dp", "mp")
    turned = P("mp", "dp")
    out_specs = (
        rows, rows, ids, rows, near, near, near, near, vec, vec, turned, vec, vec, vec, near, vec,
        turned, vec, vec, vec, turned,
    )
    return jax.shard_map(body, mesh=mesh, in_specs=in_specs, out_specs=out_specs, check_vma=False)
```

```python
import functools

import jax
import jax.numpy as jnp
from jax import lax
from jax.experimental import pallas as pl
from jax.experimental.pallas import tpu as pltpu
from jax.sharding import PartitionSpec as P

HEAD_DIM = 64
PROJ = 128
REACH = 6
SLOTS = 2 * REACH
OFFSETS = (0, 1, -1, 2, -2, -4, -3, 4, 3, -5, 5, -6)
LOCAL = 0
REMOTE = tuple(range(1, SLOTS))
EPSILON = 1e-05
NEGATIVE = -1e30
PRECISE = lax.Precision.HIGHEST
MESH = pl.DeviceIdType.MESH
BF = jnp.bfloat16
F32 = jnp.float32
VMEM_LIMIT = 60 * 1024 * 1024
VQ, VV, VO, VGA, VSA, VBO, VGF, VSF, VIN = range(9)
VROWS = 16
GANG = 2


def any_spec(count):
    return [pl.BlockSpec(memory_space=pl.ANY)] * count


def vmem_spec(count):
    return [pl.BlockSpec(memory_space=pltpu.VMEM)] * count


def row_block(array):
    dims = array.shape[1:]
    return pl.BlockSpec((1,) + dims, lambda b: (b,) + (0,) * len(dims))


def row_back(array):
    dims = array.shape[1:]
    last = array.shape[0] - 1
    return pl.BlockSpec((1,) + dims, lambda b: (last - b,) + (0,) * len(dims))


def whole_block(array):
    dims = array.shape
    return pl.BlockSpec(dims, lambda b: (0,) * len(dims), pipeline_mode=pl.Buffered(1))


def nt(left, right):
    return lax.dot_general(left, right, (((1,), (1,)), ((), ())), preferred_element_type=F32)


def tn(left, right):
    return lax.dot_general(left, right, (((0,), (0,)), ((), ())), preferred_element_type=F32)


def mm(left, right):
    return jnp.dot(left, right, preferred_element_type=F32)


def greet(targets):
    barrier = pltpu.get_barrier_semaphore()
    for target in targets:
        pl.semaphore_signal(barrier, inc=1, device_id=target, device_id_type=MESH)
    pl.semaphore_wait(barrier, len(targets))


def ring_partners(me, core, n):
    return [(lax.rem(me + step + n, n), core) for step in range(-REACH, REACH + 1) if step != 0]


class Halves:
    def __init__(self, sems):
        self.sems, self.copies, self.names = sems, [], {}

    def add(self, name, own, theirs, whole, axis, offset=0, stride=None):
        core = lax.axis_index("mp")
        size = own.shape[axis] if axis is not None else 1
        for source, side in ((own, core), (theirs, 1 - core)):
            if axis is None:
                target = whole.at[side]
            else:
                begin = offset + side * (stride or size)
                at = pl.ds(pl.multiple_of(begin, 128), size)
                target = whole.at[at] if axis == 0 else whole.at[:, at]
            copy = pltpu.make_async_copy(source, target, self.sems.at[len(self.copies)])
            self.copies.append(copy)
            self.names.setdefault(name, []).append(copy)

    def add_chunks(self, name, own, theirs, whole, axis):
        core = lax.axis_index("mp")
        size = whole.shape[1] // 2
        for j in range(whole.shape[0]):
            for source, side in ((own, core), (theirs, 1 - core)):
                to = pl.ds(pl.multiple_of(side * size, 128), size)
                part = pl.ds(j * size, size)
                source_part, target = (source.at[part], whole.at[j, to]) if axis == 0 else (source.at[:, part], whole.at[j, :, to])
                copy = pltpu.make_async_copy(source_part, target, self.sems.at[len(self.copies)])
                self.copies.append(copy)
                self.names.setdefault(name, []).append(copy)

    def start(self):
        self.start_own()
        self.start_theirs()

    def start_own(self):
        for copy in self.copies[0::2]:
            copy.start()

    def start_theirs(self):
        for copy in self.copies[1::2]:
            copy.start()

    def wait(self, name):
        for copy in self.names[name]:
            copy.wait()


def wide(vec, row):
    return jnp.concatenate([vec[0, row:row + 1, :], vec[1, row:row + 1, :]], axis=1)


def normalize(hidden):
    average = jnp.mean(hidden, axis=-1, keepdims=True)
    centered = hidden - average
    spread = jnp.mean(centered * centered, axis=-1, keepdims=True)
    inverse = lax.rsqrt(spread + EPSILON)
    return centered * inverse, inverse


def column(row):
    size = row.shape[1]
    here = lax.broadcasted_iota(jnp.int32, (size, size), 0) == lax.broadcasted_iota(jnp.int32, (size, size), 1)
    return jnp.sum(jnp.where(here, row, 0), axis=1, keepdims=True)


def head_masks(count):
    lane = lax.broadcasted_iota(jnp.int32, (1, count * HEAD_DIM), 1) // HEAD_DIM
    return [(lane == h).astype(F32).astype(BF) for h in range(count)]


def spread_halves(halves, own, theirs, **whole):
    places = {"cot": (0, 1), "pos": (1, 1), "vec": (2, None), "wo": (6, 0), "wi": (7, 1), "wu": (8, 0), "wc": (9, 0)}
    for name, ref in whole.items():
        if name == "wqkv":
            for index in range(3):
                halves.add("qkv", own[3 + index], theirs[3 + index], ref, 1, index * ref.shape[0])
        elif name in ("wi", "wu"):
            at, axis = places[name]
            halves.add_chunks(name, own[at], theirs[at], ref, axis)
        else:
            at, axis = places[name]
            halves.add(name, own[at], theirs[at], ref, axis)


def whole_scratch(own, *names):
    cot, pos, vec, wq, _, _, wo, wi, wu, wc = own
    full = wq.shape[0]
    shapes = {
        "cot": ((cot.shape[0], full), BF), "pos": ((pos.shape[0], full), BF), "vec": ((2,) + vec.shape, F32),
        "wqkv": ((full, 3 * full), BF), "wo": ((full, full), BF), "wi": ((2 * wi.shape[1] // full, full, full), BF),
        "wu": ((2 * wu.shape[0] // full, full, full), BF), "wc": ((full, wc.shape[1]), BF),
    }
    return [pltpu.VMEM(*shapes[name]) for name in names] + [pltpu.SemaphoreType.DMA((40,))]


LATE_START = 4
LATE_AT = 2
LATE_FIRST = 4


def forward_kernel(n, owner, doc_slot, places, segments, *refs):
    refs = list(refs)

    def take(count):
        taken = refs[:count]
        del refs[:count]
        return taken

    vectors = take(9)
    docs_in, tok_in, cot_in, pos_in = take(4)
    weights_in = take(7)
    theirs = take(10)
    vec_own, want, rank_out, slot_of, picks = take(5)
    xlow, qkv, lse, ctx, nmid, imid, mlow, act, slope, nout, iout, res, summ, prod = take(14)
    bias, stats, acc, cot, pos, vec, wqkv, wo, wi, wu, wc, sems = take(12)
    doc_buf, stage, docs, docs_sib, tok, tok_sib, req, got, got_s = take(9)
    req_send, req_recv, doc_send, doc_recv, fwd_send, fwd_recv, sib_send, sib_recv, misc_sem = take(9)
    own = [cot_in, pos_in, vec_own] + weights_in
    b = pl.program_id(0)
    rows = pl.num_programs(0)
    me = lax.axis_index("dp")
    core = lax.axis_index("mp")
    sibling = (me, 1 - core)
    seq, full = acc.shape
    row_count, _, half = tok_in.shape
    all_rows = row_count // 2
    early = SLOTS - row_count + 2
    halves = Halves(sems)
    spread_halves(halves, own, theirs, pos=pos, vec=vec, wqkv=wqkv, wo=wo, wi=wi, wu=wu, wc=wc, cot=cot)
    fresh = b == 0

    def request(slot):
        return pltpu.make_async_remote_copy(
            src_ref=req.at[slot], dst_ref=got.at[slot], send_sem=req_send.at[slot], recv_sem=req_recv.at[slot],
            device_id=(lax.rem(me + OFFSETS[slot] + n, n), core), device_id_type=MESH,
        )

    def document(slot):
        return pltpu.make_async_remote_copy(
            src_ref=stage.at[slot], dst_ref=docs.at[slot], send_sem=doc_send.at[slot], recv_sem=doc_recv.at[slot],
            device_id=(lax.rem(me - OFFSETS[slot] + n, n), core), device_id_type=MESH,
        )

    def pass_on(slot):
        return pltpu.make_async_remote_copy(
            src_ref=docs.at[slot], dst_ref=docs_sib.at[slot], send_sem=fwd_send.at[slot], recv_sem=fwd_recv.at[slot],
            device_id=sibling, device_id_type=MESH,
        )

    sources = [tok_in, pos_in, vec_own] + weights_in + [cot_in]
    targets = [tok_sib] + theirs[1:] + [theirs[0]]

    def share(index):
        return pltpu.make_async_remote_copy(
            src_ref=sources[index], dst_ref=targets[index], send_sem=sib_send.at[index], recv_sem=sib_recv.at[index],
            device_id=sibling, device_id_type=MESH,
        )

    doc_load = pltpu.make_async_copy(docs_in, doc_buf, misc_sem.at[0])
    tok_load = pltpu.make_async_copy(tok_in, tok, misc_sem.at[1])
    to_scalar = pltpu.make_async_copy(got, got_s, misc_sem.at[2])

    @pl.when(fresh)
    def _():
        doc_load.start()
        one = jnp.int32(1)
        zero = jnp.int32(0)
        offsets = [lax.rem(owner[0, k] - me + REACH + n, n) - REACH for k in range(row_count)]
        slots = [sum(jnp.where(o == OFFSETS[slot], slot * one, zero) for slot in range(SLOTS)) for o in offsets]
        ranks = []
        for k in range(row_count):
            ranks.append(sum(jnp.where(slots[j] < slots[k], one, zero) for j in range(row_count) if j != k))
            rank_out[k] = ranks[k]
        for slot in range(SLOTS):
            asked_for = sum(jnp.where(slots[k] == slot, doc_slot[0, k] + 1, zero) for k in range(row_count)) - 1
            req[slot] = jnp.full(req.shape[1:], asked_for, jnp.int32)
        vec_own[...] = jnp.zeros_like(vec_own)
        for index, vector in enumerate(vectors):
            for i in range(vector.shape[0] // half):
                vec_own[index + i] = vector[i * half:(i + 1) * half]
        greet(ring_partners(me, core, n) + [sibling])
        for slot in REMOTE:
            request(slot).start()
        for index in range(len(sources)):
            share(index).start()
        tok_load.start()
        halves.start_own()
        for rank in range(row_count):
            slot = sum(jnp.where(ranks[k] == rank, slots[k], zero) for k in range(row_count))
            row = sum(jnp.where(ranks[k] == rank, k * one, zero) for k in range(row_count))
            slot_of[rank] = slot
            picks[rank] = slot
            picks[row_count + rank] = jnp.minimum(row, row_count - 1)
        got[LOCAL] = req[LOCAL]
        for slot in REMOTE:
            request(slot).wait()
        to_scalar.start()
        doc_load.wait()
        to_scalar.wait()
        for slot in range(SLOTS):
            want[slot] = got_s[slot, 0, 0]
        for slot in REMOTE[:early - 1]:
            stage[slot] = doc_buf[jnp.clip(got_s[slot, 0, 0], 0, doc_buf.shape[0] - 1)]
            document(slot).start()
        docs[LOCAL] = doc_buf[jnp.clip(got_s[LOCAL, 0, 0], 0, doc_buf.shape[0] - 1)]
        pass_on(LOCAL).start()
        for slot in range(early, SLOTS):
            stage[slot] = doc_buf[jnp.clip(got_s[slot, 0, 0], 0, doc_buf.shape[0] - 1)]
        for index in range(len(sources)):
            share(index).wait()
        halves.start_theirs()
        tok_load.wait()
        for slot in REMOTE[:early - 1]:
            document(slot).wait_recv()
            pass_on(slot).start()
            if slot == LATE_START:
                for late in range(early, early + LATE_FIRST):
                    document(late).start()
        for slot in range(early):
            pass_on(slot).wait_recv()

    for step in range(1, all_rows):

        @pl.when(b == step)
        def _(step=step):
            for slot in range(early + 2 * step - 2, early + 2 * step):
                pass_on(slot).wait_recv()

    def take_late(step):
        for slot in range(early + 2 * step, early + 2 * step + 2):
            document(slot).wait_recv()
            pass_on(slot).start()
        for slot in range(early + LATE_FIRST + 2 * step, min(SLOTS, early + LATE_FIRST + 2 * step + 2)):
            document(slot).start()

    def need(*names):
        @pl.when(fresh)
        def _():
            for name in names:
                halves.wait(name)

    first = core == 0
    my_rank = 2 * b + core

    def join(a, b):
        a, b = a.astype(F32), b.astype(F32)
        return jnp.concatenate([jnp.where(first, a, b), jnp.where(first, b, a)], axis=1)

    def chosen(held):
        value = held[my_rank]
        for i in range(1, SLOTS - row_count + 1):
            value = jnp.where(picks[my_rank] == my_rank + i, held[my_rank + i], value)
        return value

    need("pos", "vec")
    table = pos.shape[0]
    row = picks[row_count + my_rank]
    seg_row = segments[pl.ds(row, 1), :]
    one_hot = (column(places[pl.ds(row, 1), :]) == lax.broadcasted_iota(jnp.int32, (seq, table), 1)).astype(F32).astype(BF)
    embedded = join(tok[row], tok_sib[row]) + mm(one_hot, pos[...]) + join(chosen(docs), chosen(docs_sib))
    low = embedded.astype(BF)
    xlow[0] = low
    acc[...] = embedded
    need("qkv")
    q = (mm(low, wqkv[:, 0:full]) + wide(vec, VQ)).astype(BF)
    qkv[0, :, 0:full] = q * jnp.asarray(HEAD_DIM ** -0.5, BF)
    qkv[0, :, full:2 * full] = mm(low, wqkv[:, full:2 * full]).astype(BF)
    qkv[0, :, 2 * full:] = (mm(low, wqkv[:, 2 * full:]) + wide(vec, VV)).astype(BF)
    bias[...] = jnp.where(column(seg_row) == seg_row, 0.0, NEGATIVE)
    stats[...] = jnp.zeros_like(stats)
    masks = head_masks(GANG)
    wide_gang = GANG * HEAD_DIM

    def heads(p):
        at = p * wide_gang
        queries = qkv[0, :, pl.ds(at, wide_gang)]
        keys = qkv[0, :, pl.ds(full + at, wide_gang)]
        values = qkv[0, :, pl.ds(2 * full + at, wide_gang)]
        lane = lax.broadcasted_iota(jnp.int32, (seq, wide_gang), 1)
        small_lane = lax.broadcasted_iota(jnp.int32, (seq, 128), 1)
        s = nt(jnp.concatenate([queries * m for m in masks], axis=0), keys)
        es, totals = [], []
        for h in range(GANG):
            sh = s[h * seq:(h + 1) * seq] + bias[...]
            top = jnp.max(sh, axis=1, keepdims=True)
            e = jnp.exp(sh - top)
            total = jnp.sum(e, axis=1, keepdims=True)
            es.append(e.astype(BF))
            totals.append(1.0 / total)
            stats[0:seq, :] = jnp.where(small_lane == GANG * p + h, top + jnp.log(total), stats[0:seq, :])
        out = mm(jnp.concatenate(es, axis=0), values)
        joined = out[0:seq] * totals[0]
        for h in range(1, GANG):
            joined = jnp.where(lane < h * HEAD_DIM, joined, out[h * seq:(h + 1) * seq] * totals[h])
        ctx[0, :, pl.ds(at, wide_gang)] = joined.astype(BF)

    for p in range(full // wide_gang):
        heads(p)
    lse[0] = jnp.transpose(stats[...])[0:lse.shape[1], 0:seq]
    need("wo")
    normed, inverse = normalize(acc[...] + mm(ctx[0], wo[...]) + wide(vec, VO))
    middle = normed * wide(vec, VGA) + wide(vec, VSA)
    nmid[0] = normed.astype(BF)
    imid[0] = inverse
    acc[...] = middle + wide(vec, VBO)
    mlow[0] = middle.astype(BF)
    need("wi", "wu", "wc", "cot")
    for j in range(wi.shape[0]):
        if j == LATE_AT:
            for step in range(all_rows - 1):

                @pl.when(b == step)
                def _(step=step):
                    take_late(step)

        pre = mm(mlow[0], wi[j]) + wide(vec, VIN + j)
        phi = 0.5 + 0.5 * lax.erf(pre * (0.5 ** 0.5))
        act[0, j] = (pre * phi).astype(BF)
        slope[0, j] = (phi + pre * (jnp.exp(-0.5 * pre * pre) * 0.3989422804014327)).astype(BF)
        acc[...] += mm(act[0, j], wu[j])
    normed, inverse = normalize(acc[...])
    nout[0] = normed.astype(BF)
    iout[0] = inverse
    result = (normed * wide(vec, VGF) + wide(vec, VSF)).astype(BF)
    res[0] = result
    summ[0] = mm(res[0, 0:16, :], wc[...])[0:8]
    product = jnp.sum(cot[...].astype(F32) * result.astype(F32))
    prod[0] = jnp.full(prod.shape[1:], product, F32)

    @pl.when(b == rows - 1)
    def _():
        for slot in REMOTE:
            document(slot).wait_send()
        for slot in range(SLOTS):
            pass_on(slot).wait_send()


def forward(n, owner, doc_slot, places, segments, vectors, doc_store, tokens, cot, pos, weights):
    all_rows, seq, half = tokens.shape
    rows = all_rows // 2
    full = 2 * half
    hidden = 2 * weights[4].shape[1]
    shape = jax.ShapeDtypeStruct
    heads = full // HEAD_DIM
    lse_rows = (heads + 7) // 8 * 8
    vec = shape((VROWS, half), F32)
    own = (cot, pos, vec) + weights
    acts = [
        ((seq, full), BF), ((seq, 3 * full), BF), ((lse_rows, seq), F32), ((seq, full), BF),
        ((seq, full), BF), ((seq, 1), F32), ((seq, full), BF), ((hidden // full, seq, full), BF), ((hidden // full, seq, full), BF),
        ((seq, full), BF), ((seq, 1), F32), ((seq, full), BF), ((8, PROJ), F32), ((8, PROJ), F32),
    ]
    acts = [shape((rows,) + dims, kind) for dims, kind in acts]
    smem = pl.BlockSpec(memory_space=pltpu.SMEM)
    dma = pltpu.SemaphoreType.DMA
    outs = [shape(o.shape, o.dtype) for o in own] + [vec]
    outs += [shape((count,), jnp.int32) for count in (SLOTS, all_rows, all_rows, 2 * all_rows)]
    result = pl.pallas_call(
        functools.partial(forward_kernel, n),
        out_shape=tuple(outs + acts),
        grid=(rows,),
        in_specs=[smem, smem] + [whole_block(a) for a in (places, segments) + tuple(vectors)] + any_spec(11),
        out_specs=tuple(any_spec(10) + [whole_block(vec)] + [smem] * 4 + [row_block(a) for a in acts]),
        scratch_shapes=[
            pltpu.VMEM((seq, seq), F32), pltpu.VMEM((384, 128), F32), pltpu.VMEM((seq, full), F32),
        ] + whole_scratch(own, "cot", "pos", "vec", "wqkv", "wo", "wi", "wu", "wc") + [
            pltpu.VMEM(doc_store.shape, BF), pltpu.VMEM((SLOTS, seq, half), BF),
            pltpu.VMEM((SLOTS, seq, half), BF), pltpu.VMEM((SLOTS, seq, half), BF),
            pltpu.VMEM(tokens.shape, BF), pltpu.VMEM(tokens.shape, BF),
            pltpu.VMEM((SLOTS, 8, 128), jnp.int32), pltpu.VMEM((SLOTS, 8, 128), jnp.int32),
            pltpu.SMEM((SLOTS, 8, 128), jnp.int32),
            dma((SLOTS,)), dma((SLOTS,)), dma((SLOTS,)), dma((SLOTS,)), dma((SLOTS,)), dma((SLOTS,)),
            dma((11,)), dma((11,)), dma((3,)),
        ],
        compiler_params=pltpu.CompilerParams(
            collective_id=0, has_side_effects=True, vmem_limit_bytes=VMEM_LIMIT
        ),
        name="forward",
    )(owner, doc_slot, places, segments, *vectors, doc_store, tokens, cot, pos, *weights)
    return result[:10], result[10], result[11:15], result[15:]


def norm_back(upstream, normed, inverse, gain):
    scaled = upstream * gain
    first = jnp.mean(scaled, axis=-1, keepdims=True)
    second = jnp.mean(scaled * normed, axis=-1, keepdims=True)
    return inverse * (scaled - first - normed * second)


def add_vec(vecs, row, value):
    half = value.shape[1] // 2
    vecs[0, row:row + 1, :] += value[:, :half]
    vecs[1, row:row + 1, :] += value[:, half:]


def token_sum(values):
    return jnp.sum(values, axis=0, keepdims=True)


def spread(value, target):
    _, n, depth, width = target.shape
    for side in range(2):
        for i in range(n):
            target[side, i] = value[i * depth:(i + 1) * depth, side * width:(side + 1) * width].astype(target.dtype)


def shares_kernel(summ, prod, qv, iout, nout_in, res_in, *refs):
    own, theirs = refs[:10], refs[10:20]
    douter, mixed, vecs, dw_cls, gq = refs[20:25]
    mine, got, nout, res, cot, vec, wc, halves_sem, send_sem, recv_sem, load_sem = refs[25:]
    me = lax.axis_index("dp")
    core = lax.axis_index("mp")
    sibling = (me, 1 - core)
    rows = summ.shape[0]
    halves = Halves(halves_sem)
    spread_halves(halves, own, theirs, vec=vec, cot=cot, wc=wc)
    halves.start()
    loads = [
        pltpu.make_async_copy(res_in, res, load_sem.at[0]),
        pltpu.make_async_copy(nout_in, nout, load_sem.at[1]),
    ]
    for load in loads:
        load.start()
    greet([sibling])
    mine[...] = jnp.concatenate([summ[b, 0:1, :] for b in range(rows)] + [prod[b, 0:1, :] for b in range(rows)], axis=0)
    copy = pltpu.make_async_remote_copy(
        src_ref=mine, dst_ref=got, send_sem=send_sem, recv_sem=recv_sem,
        device_id=sibling, device_id_type=MESH,
    )
    copy.start()
    vecs[...] = jnp.zeros_like(vecs)
    copy.wait()
    first = core == 0
    low = jnp.where(first, mine[...], got[...])
    high = jnp.where(first, got[...], mine[...])
    summary = jnp.concatenate([low[:rows], high[:rows]], axis=0)
    product = jnp.concatenate([low[rows:], high[rows:]], axis=0)
    inv_root = PROJ ** (-0.5)
    logits = jnp.sum(summary * qv[...], axis=1, keepdims=True) * inv_root
    e = jnp.exp(logits - jnp.max(logits, axis=0, keepdims=True))
    share = e / jnp.sum(e, axis=0, keepdims=True)
    dlogits = share * (product - jnp.sum(share * product, axis=0, keepdims=True))
    gq[...] = jnp.sum(dlogits * summary, axis=0, keepdims=True) * inv_root
    ds = dlogits * qv[...] * inv_root
    wide_share = share + jnp.zeros_like(ds)
    shares = jnp.where(first, wide_share, jnp.concatenate([wide_share[rows:], wide_share[:rows]], axis=0))
    dsum = jnp.where(first, ds, jnp.concatenate([ds[rows:], ds[:rows]], axis=0))
    halves.wait("vec")
    halves.wait("cot")
    halves.wait("wc")
    extra = lax.dot_general(
        dsum, wc[...].astype(F32), (((1,), (1,)), ((), ())), preferred_element_type=F32, precision=PRECISE
    )
    for load in loads:
        load.wait()
    seq, full = cot.shape
    heads = jnp.concatenate([res[b, 0:1, :].astype(F32) for b in range(rows)], axis=0)
    heads = jnp.concatenate([heads, jnp.zeros_like(heads)], axis=0)
    product = lax.dot_general(dsum, heads, (((0,), (0,)), ((), ())), preferred_element_type=F32, precision=PRECISE)
    spread(product, dw_cls)
    row = lax.broadcasted_iota(jnp.int32, (seq, 1), 0)
    for b in range(rows):
        share_b = shares[b:b + 1, 0:1]
        part = share_b * res[b].astype(F32)
        mixed[...] = part if b == 0 else mixed[...] + part
        upstream = share_b * cot[...].astype(F32) + jnp.where(row == 0, extra[b:b + 1], 0.0)
        upstream = upstream.astype(BF).astype(F32)
        normed = nout[b].astype(F32)
        dout = norm_back(upstream, normed, iout[b], wide(vec, VGF))
        add_vec(vecs, VGF, token_sum(upstream * normed))
        add_vec(vecs, VSF, token_sum(upstream))
        add_vec(vecs, VBO, token_sum(dout))
        douter[b] = dout.astype(BF)


def share_out(n, summ, prod, qv, iout, nout, res, own, theirs):
    rows, seq, full = res.shape
    shape = jax.ShapeDtypeStruct
    return pl.pallas_call(
        shares_kernel,
        out_shape=(
            shape((rows, seq, full), BF), shape((seq, full), F32), shape((2, VROWS, full // 2), F32),
            shape((2, n, PROJ // n, full // 2), F32), shape((1, PROJ), F32),
        ),
        in_specs=vmem_spec(4) + any_spec(22),
        out_specs=tuple(vmem_spec(5)),
        scratch_shapes=[
            pltpu.VMEM((2 * rows, PROJ), F32), pltpu.VMEM((2 * rows, PROJ), F32),
            pltpu.VMEM(nout.shape, BF), pltpu.VMEM(res.shape, BF),
        ] + whole_scratch(own, "cot", "vec", "wc") + [
            pltpu.SemaphoreType.DMA, pltpu.SemaphoreType.DMA, pltpu.SemaphoreType.DMA((2,)),
        ],
        compiler_params=pltpu.CompilerParams(collective_id=1, has_side_effects=True, vmem_limit_bytes=VMEM_LIMIT),
        name="shares",
    )(summ, prod, qv, iout, nout, res, *own, *theirs)


def with_bit(index, position, bit):
    low = 1 << position
    return (index // low) * (2 * low) + bit * low + index % low


def across(bit):
    me = lax.axis_index("dp")
    here = (me // (1 << bit)) % 2
    return here, (me + (1 - 2 * here) * (1 << bit), lax.axis_index("mp"))


HANDED = 2


class Group:
    def __init__(self, n, bits, bufs, sems, index, near, start=0):
        self.n, self.bits, self.near, self.start = n, bits, near, start
        bufs = list(bufs)
        self.mine = bufs.pop(0)
        self.theirs = bufs.pop(0) if start == 0 else None
        self.out, self.came = [None] * start + bufs[0::2], [None] * start + bufs[1::2]
        self.send_sem, self.recv_sem, self.own_sem, self.index = sems[0], sems[1], sems[2], index
        self.levels = len(bits)

    @staticmethod
    def scratch(n, rows, width, kind, start=0):
        levels = n.bit_length() - 1
        shapes = [(n >> start, rows, width)] * (2 if start == 0 else 1)
        for level in range(start, levels):
            shapes += [(n >> (level + 1), rows, width)] * 2
        return [pltpu.VMEM(s, kind) for s in shapes]

    @staticmethod
    def size(n, start=0):
        return (2 if start == 0 else 1) + 2 * (n.bit_length() - 1 - start)

    def remote(self, level, src, dst, target):
        return pltpu.make_async_remote_copy(
            src_ref=src, dst_ref=dst, send_sem=self.send_sem.at[self.index, level],
            recv_sem=self.recv_sem.at[self.index, level], device_id=target, device_id_type=MESH,
        )

    @staticmethod
    def handing_scratch(n, rows, width, kind):
        shapes = [(2, n, rows, width), (n, rows, width)]
        for level in range(HANDED):
            shapes += [(n >> (level + 1), rows, width)] * 2
        return [pltpu.VMEM(s, kind) for s in shapes]

    def first(self, src):
        return self.remote(0, src, self.theirs, self.near["sibling"])

    def load_own(self, src):
        return pltpu.make_async_copy(src, self.mine, self.own_sem.at[self.index])

    def hop(self, level):
        return self.remote(level + 1, self.out[level], self.came[level], self.near[self.bits[level]][1])

    def left(self, level):
        return [bit for bit in range(self.levels) if bit not in self.bits[:level]]

    def places(self, level, t, side=0):
        digit = {bit: self.near[bit][0] for bit in self.bits[self.start:level]}
        if level < self.levels:
            digit[self.bits[level]] = side
        for k, bit in enumerate(self.left(level + 1)):
            digit[bit] = (t >> k) & 1
        held = sum(digit[bit] * (1 << k) for k, bit in enumerate(self.left(self.start)))
        came = sum(digit[bit] * (1 << k) for k, bit in enumerate(self.left(level)))
        return held, came

    def advance(self, level):
        came = self.theirs if level == 0 else self.came[level - 1]
        here = self.near[self.bits[level]][0]
        count = self.n >> (level + 1)
        handed = self.start > 0 and level == self.start
        for t in range(count):
            at, of = self.places(level, t, 1 - here)
            self.out[level][t] = self.mine[at] if handed else self.mine[at] + came[of]
        self.hop(level).start()
        if not handed:
            for t in range(count):
                at, of = self.places(level, t, here)
                self.mine[at] = self.mine[at] + came[of]

    def hand_on(self, level, target):
        for t in range(self.n >> level):
            digit = {bit: self.near[bit][0] for bit in self.bits[:level]}
            for k, bit in enumerate(self.left(level)):
                digit[bit] = (t >> k) & 1
            at = sum(digit[bit] * (1 << bit) for bit in range(self.levels))
            target[t] = self.mine[at] + self.came[level - 1][t]

    def total(self):
        at, _ = self.places(self.levels, 0)
        return self.mine[at].astype(F32) + self.came[-1][0].astype(F32)


def bit_orders(n):
    rest = tuple(range(3, n.bit_length() - 1))
    return (0, 1, 2) + rest, (1, 2, 0) + rest, (2, 0, 1) + rest


def neighbours(n):
    near = {bit: across(bit) for bit in range(n.bit_length() - 1)}
    near["core"] = lax.axis_index("mp")
    near["sibling"] = (lax.axis_index("dp"), 1 - near["core"])
    return near


def bit_partners(n, near):
    return [near["sibling"]] + [near[bit][1] for bit in range(n.bit_length() - 1)]


class Reducer:
    @staticmethod
    def plan(n, mats):
        pieces = []
        for index, mat in enumerate(mats):
            if mat.shape[1] == n:
                pieces.append((index, 0, mat.shape[3], 0, index % 3))
            else:
                pieces += [(index, g * mat.shape[3], mat.shape[3], HANDED, g % 3) for g in range(mat.shape[0])]
        return pieces

    @staticmethod
    def scratch(n, mats):
        shapes = []
        pieces = Reducer.plan(n, mats)
        for index, _, width, start, _ in pieces:
            shapes += Group.scratch(n, mats[index].shape[-2], width, mats[index].dtype, start)
        dma = pltpu.SemaphoreType.DMA
        levels = n.bit_length()
        return shapes + [dma((len(pieces), levels)), dma((len(pieces), levels)), dma((len(pieces),))]

    def __init__(self, n, mats, outs, refs, near):
        self.mats, self.outs, self.near = mats, outs, near
        self.pieces = Reducer.plan(n, mats)
        orders = bit_orders(n)
        refs = list(refs)
        self.groups = []
        for index, (_, begin, width, start, order) in enumerate(self.pieces):
            size = Group.size(n, start)
            self.groups.append(Group(n, orders[order], refs[:size], refs[-3:], index, near, start))
            del refs[:size]

    def source(self, index, side):
        mat, begin, width, start, _ = self.pieces[index]
        return self.mats[mat].at[begin // width if start else side]

    def start(self):
        core = self.near["core"]
        for index, group in enumerate(self.groups):
            if not group.start:
                group.first(self.source(index, 1 - core)).start()
            group.load_own(self.source(index, core)).start()

    def move(self, mat, level):
        core = self.near["core"]
        for index, group in enumerate(self.groups):
            at, begin, width, start, _ = self.pieces[index]
            if at != mat:
                continue
            if level == start:
                group.load_own(self.source(index, core)).wait()
                if not start:
                    group.first(self.source(index, 1 - core)).wait()
            else:
                group.hop(level - 1).wait()
            if level < group.levels:
                group.advance(level)
            else:
                self.outs[mat][:, begin:begin + width] = group.total()


def middle_kernel(n, handed_count, summed, vecs_in, imid, *refs):
    refs = list(refs)

    def take(count):
        taken = refs[:count]
        del refs[:count]
        return taken

    own, theirs = take(10), take(10)
    douter_in, act_in, slope_in, mlow_in, nmid_in, ctx_in = take(6)
    dattn_out, vecs = take(2)
    handed, late_inner, late_last, dw_out = take(4) if summed else (None,) * 4
    dinner_out = None if summed else take(1)[0]
    douter, dinner, mlow, nmid, ctx, dattn, acts, slopes, acc, vec, wi, wu, halves_sem, load_sem = take(14)
    rows, seq, full = acc.shape
    half = full // 2
    chunks = wi.shape[0]
    near = neighbours(n)
    core = near["core"]
    halves = Halves(halves_sem)
    spread_halves(halves, own, theirs, vec=vec, wu=wu, wi=wi)

    def chunk_load(source, target, j, base):
        return pltpu.make_async_copy(source.at[:, j], target.at[j % 2], load_sem.at[base + j])

    def act_load(j):
        return chunk_load(act_in, acts, j, 8)

    def slope_load(j):
        return chunk_load(slope_in, slopes, j, 8 + chunks)

    pairs = ((douter_in, douter), (mlow_in, mlow), (nmid_in, nmid), (ctx_in, ctx))
    plain = [pltpu.make_async_copy(src, dst, load_sem.at[index]) for index, (src, dst) in enumerate(pairs)]
    plain[0].start()
    if summed:
        act_load(0).start()
        act_load(1).start()
    slope_load(0).start()
    halves.start()
    slope_load(1).start()
    for load in plain[1:]:
        load.start()
    vecs[...] = vecs_in[...]
    groups = []
    if summed:
        orders = bit_orders(n)
        size = 2 + 2 * HANDED
        sems = refs[-2:] + [None]
        pair_of = []
        for index in range(handed_count):
            pair, *bufs = take(size)
            pair_of.append(pair)
            groups.append(Group(n, orders[index % 3], [pair.at[core]] + bufs, sems, index, near))
        greet(bit_partners(n, near))
    plain[0].wait()

    def flat(ref):
        return ref[...].reshape(rows * seq, full)

    def begin(index, left, right):
        spread(tn(left, right), pair_of[index])
        groups[index].first(pair_of[index].at[1 - core]).start()

    def move(index, level):
        if level == 0:
            groups[index].first(pair_of[index].at[1 - core]).wait()
        else:
            groups[index].hop(level - 1).wait()
        groups[index].advance(level)

    if summed:
        for j in range(chunks):
            act_load(j).wait()
            if j >= 2:
                move(j - 2, 0)
            begin(j, flat(douter), acts[j % 2].reshape(rows * seq, full))
            if j + 2 < chunks:
                act_load(j + 2).start()
    moves = {
        (0, 0): ((2, 0),), (0, 1): ((3, 0),), (0, 2): ((0, 1),), (1, 1): ((1, 1), (4, 0)), (1, 2): ((2, 1),),
        (2, 1): ((3, 1), (5, 0)), (2, 2): ((4, 1),), (3, 2): ((5, 1),),
    }

    def moved(j, point):
        for index, level in moves.get((j, point), ()) if summed else ():
            move(index, level)

    acc[...] = douter[...].astype(F32)
    halves.wait("vec")
    halves.wait("wu")
    halves.wait("wi")
    plain[1].wait()
    for j in range(chunks):
        slope_load(j).wait()
        for m in range(0, rows, 2):
            moved(j, m // 2)
            part = nt(douter[m:m + 2].reshape(2 * seq, full), wu[j])
            part = part * slopes[j % 2, m:m + 2].reshape(2 * seq, full).astype(F32)
            low = part.astype(BF)
            dinner[m:m + 2] = low.reshape(2, seq, full)
            sums = token_sum(part)
            for side in range(2):
                vecs[side, VIN + j:VIN + j + 1, :] += sums[:, side * half:(side + 1) * half]
            acc[m:m + 2] += nt(low, wi[j]).reshape(2, seq, full)
        if j + 2 < chunks:
            slope_load(j + 2).start()
        moved(j, 2)
        if not summed:
            copy = pltpu.make_async_copy(dinner, dinner_out.at[j], load_sem.at[4])
            copy.start()
            copy.wait()
        elif chunks + j < handed_count:
            begin(chunks + j, flat(mlow), flat(dinner))
        else:
            spread(tn(flat(mlow), flat(dinner)), (late_inner, late_last)[chunks + j - handed_count])
    plain[2].wait()
    for r in range(rows):
        upstream = acc[r]
        normed = nmid[r].astype(F32)
        middle = norm_back(upstream, normed, imid[r], wide(vec, VGA))
        add_vec(vecs, VGA, token_sum(upstream * normed))
        add_vec(vecs, VSA, token_sum(upstream))
        add_vec(vecs, VO, token_sum(middle))
        dattn[r] = middle.astype(BF)
    done = pltpu.make_async_copy(dattn, dattn_out, load_sem.at[5])
    done.start()
    plain[3].wait()
    if summed:
        spread(tn(flat(dattn), flat(ctx)), dw_out)
        for index, group in enumerate(groups):
            group.hop(HANDED - 1).wait()
            group.hand_on(HANDED, handed.at[index])
    done.wait()


def middle(n, summed, douter, act, slope, mlow, nmid, imid, ctx, vecs, own, theirs):
    rows, seq, full = douter.shape
    half = full // 2
    chunks = act.shape[1]
    shape = jax.ShapeDtypeStruct
    dma = pltpu.SemaphoreType.DMA
    outs = [shape((rows, seq, full), BF), shape(vecs.shape, F32)]
    specs = any_spec(1) + vmem_spec(1)
    handed_count = chunks + 2
    depth = full // n
    scratch = [pltpu.VMEM((rows, seq, full), BF)] * 6 + [pltpu.VMEM((2, rows, seq, full), BF)] * 2
    scratch += [pltpu.VMEM((rows, seq, full), F32)] + whole_scratch(own, "vec", "wi", "wu") + [dma((8 + 2 * chunks,))]
    params = dict(vmem_limit_bytes=VMEM_LIMIT)
    if summed:
        outs.append(shape((handed_count, n >> HANDED, depth, half), BF))
        outs += [shape((2, n, depth, half), BF)] * 3
        specs += vmem_spec(4)
        for _ in range(handed_count):
            scratch += Group.handing_scratch(n, depth, half, BF)
        scratch += [dma((handed_count, HANDED + 1))] * 2
        params.update(collective_id=3, has_side_effects=True)
    else:
        outs.append(shape((chunks, rows, seq, full), BF))
        specs += any_spec(1)
    return pl.pallas_call(
        functools.partial(middle_kernel, n, handed_count, summed),
        out_shape=tuple(outs),
        in_specs=vmem_spec(2) + any_spec(26),
        out_specs=tuple(specs),
        scratch_shapes=scratch,
        compiler_params=pltpu.CompilerParams(**params),
        name="middle",
    )(vecs, imid, *own, *theirs, douter, act, slope, mlow, nmid, ctx)


SEND_AT = 2
VEC_AT = 1
TAIL_TIMES = (
    (3, 0, 2), (7, 0, 3), (7, 1, 0), (8, 2, 0), (8, 3, 0), (8, 4, 0), (14, 0, 4),
    (15, 1, 1), (15, 2, 1), (15, 3, 1), (15, 4, 1), (22, 1, 2), (22, 2, 2), (22, 3, 2), (22, 4, 2),
)


def tail_kernel(n, mat_count, slot_row, picks, vecs_in, places, segments, dattn, qkv, lse, mixed_in, xlow, *refs):
    refs = list(refs)

    def take(count):
        taken = refs[:count]
        del refs[:count]
        return taken

    own, theirs, mats = take(10), take(10), take(mat_count)
    gt, arrived, mixed, vec_out = take(4)
    spare = [] if mats else take(2)
    sums_out = take(mat_count)
    small_out = take(4) if mats else []
    bias, grads, dqkv, dstart, gt_v, stage, mix_own, mix_got, late, late_far, late_all, vec_far, vec_rows, vec_got, vec_sums, wqkv, wo, halves_sem = take(18)
    own_sem, sib_send, sib_recv, doc_send, doc_recv, vec_send, vec_recv, late_send, late_recv = take(9)
    x_v = outgoing = None
    small = []
    near = neighbours(n)
    if mats:
        x_v, *outgoing = take(5)
        orders = bit_orders(n)
        count = 4 * Group.size(n) + 3
        small_refs = take(count)
        for index in range(4):
            size = Group.size(n)
            bufs = small_refs[index * size:(index + 1) * size]
            small.append(Group(n, orders[(0, 1, 2, 0)[index]], bufs, small_refs[-3:], index, near))
        summer = Reducer(n, mats, sums_out, refs, near)
    b = pl.program_id(0)
    rows = pl.num_programs(0)
    me = lax.axis_index("dp")
    core = near["core"]
    other = 1 - core
    sibling = near["sibling"]
    levels = n.bit_length() - 1
    row_count, _, half = gt_v.shape
    all_rows = row_count // 2
    seq, full = grads.shape
    gang = GANG
    pair = gang * HEAD_DIM
    pairs = full // pair
    halves = Halves(halves_sem)
    spread_halves(halves, own, theirs, wo=wo)
    for index in range(3):
        halves.add("qkv", own[3 + index], theirs[3 + index], wqkv, 1, index * half, 3 * half)
    here_cols = pl.ds(pl.multiple_of(core * half, half), half)
    there_cols = pl.ds(pl.multiple_of(other * half, half), half)
    first_core = core == 0

    def push(row):
        at = pl.ds(pl.multiple_of(row * seq, seq), seq)
        return pltpu.make_async_remote_copy(
            src_ref=dstart.at[at, there_cols], dst_ref=gt_v.at[2 * row + core],
            send_sem=sib_send.at[row], recv_sem=sib_recv.at[row], device_id=sibling, device_id_type=MESH,
        )

    def document(slot):
        if slot == LOCAL:
            return pltpu.make_async_copy(stage.at[slot], arrived.at[slot], own_sem.at[2])
        return pltpu.make_async_remote_copy(
            src_ref=stage.at[slot], dst_ref=arrived.at[slot], send_sem=doc_send.at[slot], recv_sem=doc_recv.at[slot],
            device_id=(lax.rem(me + OFFSETS[slot] + n, n), core), device_id_type=MESH,
        )

    def pack(slot):
        lowest, highest = max(0, slot - (SLOTS - row_count)), min(row_count - 1, slot)
        value = gt_v[lowest]
        for rank in range(lowest + 1, highest + 1):
            value = jnp.where(slot_row[rank] == slot, gt_v[rank], value)
        stage[slot] = value

    mix_far = pltpu.make_async_remote_copy(
        src_ref=mixed_in.at[:, there_cols], dst_ref=mix_got, send_sem=sib_send.at[all_rows],
        recv_sem=sib_recv.at[all_rows], device_id=sibling, device_id_type=MESH,
    )
    mix_load = pltpu.make_async_copy(mixed_in.at[:, here_cols], mix_own, own_sem.at[0])
    vec_copy = pltpu.make_async_remote_copy(
        src_ref=vecs_in.at[other], dst_ref=vec_far, send_sem=vec_send.at[0], recv_sem=vec_recv.at[0],
        device_id=sibling, device_id_type=MESH,
    )

    def vec_hop(again, step):
        to = lax.rem(me + step, n)
        src, dst = (vec_sums.at[me], vec_sums.at[me]) if again else (vec_rows.at[to], vec_got.at[me])
        return pltpu.make_async_remote_copy(
            src_ref=src, dst_ref=dst, send_sem=vec_send.at[again * n + step], recv_sem=vec_recv.at[again * n + step],
            device_id=(to, core), device_id_type=MESH,
        )

    def vec_out_rows():
        vec_copy.wait()
        held = vecs_in[core] + vec_far[...]
        depth = held.shape[0] // n
        for i in range(n):
            vec_rows[i] = held[i * depth:(i + 1) * depth]
        for step in range(1, n):
            vec_hop(0, step).start()

    def vec_sum_rows():
        for step in range(1, n):
            vec_hop(0, step).wait()
        total = vec_rows[me]
        for step in range(1, n):
            total = total + vec_got[lax.rem(me + step, n)]
        vec_sums[me] = total
        for step in range(1, n):
            vec_hop(1, step).start()

    late_copy = pltpu.make_async_remote_copy(
        src_ref=late.at[other], dst_ref=late_far, send_sem=late_send.at[0], recv_sem=late_recv.at[0],
        device_id=sibling, device_id_type=MESH,
    )

    def late_hop(step):
        return pltpu.make_async_remote_copy(
            src_ref=late_all.at[me], dst_ref=late_all.at[me], send_sem=late_send.at[step], recv_sem=late_recv.at[step],
            device_id=(lax.rem(me + step, n), core), device_id_type=MESH,
        )

    x_loads = []
    if mats:
        for r in range(all_rows):
            x_loads.append(pltpu.make_async_copy(xlow.at[r], x_v.at[pl.ds(r * seq, seq)], own_sem.at[3 + r]))

    @pl.when(b == 0)
    def _():
        halves.start()
        late[...] = jnp.zeros_like(late)
        everyone = [(lax.rem(me + step, n), core) for step in range(1, n)]
        greet((everyone if mats else ring_partners(me, core, n)) + [sibling])
        if mats:
            summer.start()
        vec_copy.start()
        mix_far.start()
        mix_load.start()
        for load in x_loads:
            load.start()
        halves.wait("wo")
        halves.wait("qkv")

    grads[...] = nt(dattn[0], wo[...]).astype(BF)
    turn = rows - 1 - b
    seg_row = segments[pl.ds(picks[row_count + 2 * turn + core], 1), :]
    bias[...] = jnp.where(column(seg_row) == seg_row, 0.0, NEGATIVE)
    masks = head_masks(gang)
    my_rows = pl.ds(pl.multiple_of(turn * seq, seq), seq)

    def heads(p):
        for step, mat, level in TAIL_TIMES if mats else ():
            if step % pairs == p:

                @pl.when(b == step // pairs)
                def _(mat=mat, level=level):
                    summer.move(mat, level)

        if p == SEND_AT and mats:

            @pl.when(b == 0)
            def _():
                vec_out_rows()

        if p == VEC_AT and mats:

            @pl.when(b == 1)
            def _():
                vec_sum_rows()

        if p == SEND_AT:
            for row in range(1, all_rows):

                @pl.when(b == row)
                def _(row=row):
                    push(all_rows - row).wait()
                    for slot in (SLOTS - 2 * row, SLOTS - 2 * row + 1):
                        pack(slot)
                        document(slot).start()

        at = p * pair
        queries = qkv[0, :, pl.ds(at, pair)]
        keys = qkv[0, :, pl.ds(full + at, pair)]
        values = qkv[0, :, pl.ds(2 * full + at, pair)]
        dctx = grads[:, pl.ds(at, pair)]
        lane = lax.broadcasted_iota(jnp.int32, (seq, pair), 1)
        keys_all = jnp.concatenate([keys * m for m in masks], axis=0)
        s = nt(keys_all, queries)
        dw = nt(jnp.concatenate([values * m for m in masks], axis=0), dctx)
        ws, dss = [], []
        for h in range(gang):
            w = jnp.exp(s[h * seq:(h + 1) * seq] + bias[...] - lse[0, gang * p + h:gang * p + h + 1, :])
            prod = w * dw[h * seq:(h + 1) * seq]
            dss.append((prod - w * token_sum(prod)).astype(BF))
            ws.append(w.astype(BF))
        ds = jnp.concatenate(dss, axis=0)
        dv = mm(jnp.concatenate(ws, axis=0), dctx)
        dk = mm(ds, queries)
        dq = tn(ds, keys_all) * HEAD_DIM ** -0.5

        def join(parts):
            joined = parts[0:seq]
            for h in range(1, gang):
                joined = jnp.where(lane < h * HEAD_DIM, joined, parts[h * seq:(h + 1) * seq])
            return joined

        for t, value in enumerate((dq, join(dk), join(dv))):
            for i in range(0, pair, 128):
                column = at + i
                out_at = (column // half) * (3 * half) + column % half + t * half
                dqkv[my_rows, pl.ds(out_at, 128)] = value[:, i:i + 128].astype(BF)

    for p in range(pairs):
        heads(p)
    total = dattn[0].astype(F32) + nt(dqkv[my_rows, :], wqkv[...])
    for h in range(2):
        for t in (0, 2):
            source = dqkv[my_rows, (3 * h + t) * half:(3 * h + t + 1) * half]
            late[h, t // 2:t // 2 + 1, :] += token_sum(source.astype(F32))
    low = total.astype(BF)
    dstart[my_rows, :] = low
    gt_v[2 * turn + core] = jnp.where(first_core, total[:, :half], total[:, half:]).astype(BF)
    push(turn).start()

    @pl.when(b == rows - 1)
    def _():
        late_copy.start()
        late_copy.wait()
        late_all[me] = late[core] + late_far[...]
        if mats:
            for step in range(1, n):
                late_hop(step).start()
        push(0).wait()
        tok_out = pltpu.make_async_copy(gt_v, gt, own_sem.at[1])
        tok_out.start()
        for slot in reversed(range(SLOTS - 2 * all_rows + 2)):
            pack(slot)
        for slot in reversed(range(SLOTS - 2 * all_rows + 2)):
            document(slot).start()

        if not mats:
            vec_copy.wait()
            vec_out[...] = vecs_in[core] + vec_far[...]
            vec_out[VQ:VV + 1] = late_all[me]
            for source, target in ((dqkv, spare[0]), (dstart, spare[1])):
                copy = pltpu.make_async_copy(source, target, own_sem.at[3])
                copy.start()
                copy.wait()
        else:
            for load in x_loads:
                load.wait()
            table = small_out[3].shape[0] * n
            one_hots = []
            for r in range(all_rows):
                place = places[pl.ds(picks[row_count + 2 * r + core], 1), :]
                here = place == lax.broadcasted_iota(jnp.int32, (table, seq), 0)
                one_hots.append(here.astype(F32).astype(BF))

            def product(index, side, target):
                if index < 3:
                    at = pl.ds(pl.multiple_of(side * 3 * half + index * half, half), half)
                    value = tn(x_v[...], dqkv[:, at])
                else:
                    at = pl.ds(pl.multiple_of(side * half, half), half)
                    value = sum(mm(one_hots[r], dstart[r * seq:(r + 1) * seq, at]) for r in range(all_rows))
                depth = target.shape[1]
                for i in range(n):
                    target[i] = value[i * depth:(i + 1) * depth].astype(target.dtype)

            firsts = []

            def begin(index):
                product(index, other, outgoing[index])
                copy = small[index].first(outgoing[index])
                copy.start()
                firsts.append(copy)
                product(index, core, small[index].mine)

            def step(index, level):
                if level == 0:
                    firsts[index].wait()
                else:
                    small[index].hop(level - 1).wait()
                if level < levels:
                    small[index].advance(level)
                else:
                    small_out[index][...] = small[index].total()

            taken = {}
            for _, mat, level in TAIL_TIMES:
                taken[mat] = max(taken.get(mat, -1), level)
            left = [(mat, level) for level in range(levels + 1) for mat in range(mat_count) if level > taken.get(mat, -1)]

            def some(mat):
                for at, (m, level) in enumerate(left):
                    if m == mat:
                        del left[at]
                        summer.move(mat, level)
                        return

            for index in range(4):
                begin(index)
                step(index, 0)
                if index == 1:
                    for mat in range(1, mat_count):
                        some(mat)
            while left:
                some(left[0][0])
            for level in range(1, levels + 1):
                for index in range(4):
                    step(index, level)
            for step_to in range(1, n):
                vec_hop(1, step_to).wait()
                late_hop(step_to).wait()
            vec_out[...] = jnp.concatenate([vec_sums[i] for i in range(n)], axis=0)
            total = late_all[0]
            for i in range(1, n):
                total = total + late_all[i]
            vec_out[VQ:VV + 1] = total
        mix_load.wait()
        mix_far.wait()
        mixed[...] = (mix_own[...] + mix_got[...]).astype(BF)
        tok_out.wait()
        for slot in range(SLOTS):
            document(slot).wait()


def tail(n, table, slot_of, picks, vecs, places, segments, dattn, qkv, lse, mixed, xlow, own, theirs, mats):
    rows, seq, full = dattn.shape
    half = full // 2
    tokens = rows * seq
    levels = n.bit_length() - 1
    shape = jax.ShapeDtypeStruct
    outs = [shape((2 * rows, seq, half), BF), shape((SLOTS, seq, half), BF), shape((seq, half), BF), shape(vecs.shape[1:], F32)]
    if not mats:
        outs += [shape((tokens, 3 * full), BF), shape((tokens, full), BF)]
    out_specs = any_spec(2) + [whole_block(o) for o in outs[2:4]] + any_spec(len(outs) - 4)
    by_row = (dattn, qkv, lse)
    dma = pltpu.SemaphoreType.DMA
    scratch = [
        pltpu.VMEM((seq, seq), F32), pltpu.VMEM((seq, full), BF), pltpu.VMEM((tokens, 3 * full), BF),
        pltpu.VMEM((tokens, full), BF), pltpu.VMEM((2 * rows, seq, half), BF), pltpu.VMEM((SLOTS, seq, half), BF),
        pltpu.VMEM((seq, half), F32), pltpu.VMEM((seq, half), F32), pltpu.VMEM((2, 2, half), F32),
        pltpu.VMEM((2, half), F32), pltpu.VMEM((n, 2, half), F32), pltpu.VMEM(vecs.shape[1:], F32),
    ] + [pltpu.VMEM((n, max(1, vecs.shape[1] // n), half), F32)] * 3 + whole_scratch(own, "wqkv", "wo") + [
        dma((3 + rows,)), dma((rows + 1,)), dma((rows + 1,)), dma((SLOTS,)), dma((SLOTS,)), dma((2 * n,)), dma((2 * n,)), dma((n,)), dma((n,)),
    ]
    if mats:
        depths = [full // n] * 3 + [table // n]
        scratch += [pltpu.VMEM((tokens, full), BF)] + [pltpu.VMEM((n, depth, half), BF) for depth in depths]
        for depth in depths:
            scratch += Group.scratch(n, depth, half, BF)
        scratch += [dma((4, levels + 1)), dma((4, levels + 1)), dma((4,))]
        scratch += Reducer.scratch(n, mats)
        sums = [shape((m.shape[2], m.shape[3] * (1 if m.shape[1] == n else m.shape[0])), F32) for m in mats] + [shape((depth, half), F32) for depth in depths]
        outs += sums
        out_specs += [whole_block(o) for o in sums]
    return pl.pallas_call(
        functools.partial(tail_kernel, n, len(mats)),
        out_shape=tuple(outs),
        grid=(rows,),
        in_specs=[pl.BlockSpec(memory_space=pltpu.SMEM)] * 2 + [whole_block(a) for a in (vecs, places, segments)]
        + [row_back(a) for a in by_row] + any_spec(22 + len(mats)),
        out_specs=tuple(out_specs),
        scratch_shapes=scratch,
        compiler_params=pltpu.CompilerParams(
            collective_id=2, has_side_effects=True, vmem_limit_bytes=VMEM_LIMIT
        ),
        name="tail",
    )(slot_of, picks, vecs, places, segments, *by_row, mixed, xlow, *own, *theirs, *mats)


PIECES = 1
FINISHED = ("mixed", "pos", "wq", "wk", "wv", "wo", "cls", "gq")


def finish_kernel(names, want, rank, arrived, gt, vec_sum, *refs):
    refs = list(refs)

    def take(count):
        taken = refs[:count]
        del refs[:count]
        return taken

    ins, handed, lates, (docs_out, tokens_out) = take(len(names)), take(1)[0], take(2), take(2)
    outs, (outer, inner), vectors = take(len(names)), take(2), take(9)
    got, total, tok, sems, in_sem, out_sem, *held = refs
    docs = docs_out.shape[0]
    row_count, _, half = tokens_out.shape
    loads = [pltpu.make_async_copy(arrived.at[slot], got.at[slot], sems.at[slot]) for slot in range(SLOTS)]
    tok_loads = [pltpu.make_async_copy(gt.at[jnp.minimum(rank[k], row_count - 1)], tok.at[k], sems.at[SLOTS + PIECES + k]) for k in range(row_count)]
    for load in tok_loads + loads:
        load.start()

    small = [
        pltpu.make_async_copy(source, buffer, in_sem.at[index])
        for index, (source, buffer) in enumerate(zip(ins + [handed] + lates, held))
    ]
    for load in small:
        load.start()
    for index, vector in enumerate(vectors):
        for i in range(vector.shape[0] // half):
            vector[i * half:(i + 1) * half] = vec_sum[index + i]
    for load in tok_loads:
        load.wait()
    tok_done = pltpu.make_async_copy(tok, tokens_out, sems.at[SLOTS + PIECES])
    tok_done.start()
    for load in small:
        load.wait()
    hidden = outer.shape[1]
    first_inner = handed.shape[1] - hidden
    both = held[len(names)]
    moves = [(buffer, target.at[0] if name == "mixed" else target) for name, buffer, target in zip(names, held, outs)]
    moves.append((both.at[:, pl.ds(0, hidden)], outer))
    moves.append((both.at[:, pl.ds(hidden, first_inner)], inner.at[:, pl.ds(0, first_inner)]))
    for index, buffer in enumerate(held[len(names) + 1:]):
        moves.append((buffer, inner.at[:, pl.ds(first_inner + index * half, half)]))
    stores = [pltpu.make_async_copy(src, dst, out_sem.at[index]) for index, (src, dst) in enumerate(moves)]
    for store in stores:
        store.start()
    for load in loads:
        load.wait()
    size = got.shape[1] // PIECES
    done = []
    for piece in range(PIECES):
        rows = pl.ds(piece * size, size)

        def clear(d, carry, rows=rows):
            total[d, rows] = jnp.zeros((size, half), F32)
            return carry

        lax.fori_loop(0, docs, clear, 0)
        for slot in range(SLOTS):
            at = jnp.where(want[slot] < 0, docs, jnp.minimum(want[slot], docs))
            total[at, rows] += got[slot, rows].astype(F32)
        copy = pltpu.make_async_copy(total.at[pl.ds(0, docs), rows], docs_out.at[:, rows], sems.at[SLOTS + piece])
        copy.start()
        done.append(copy)
    tok_done.wait()
    for copy in stores + done:
        copy.wait()


def finish(docs, want, rank, arrived, gt, vec_sum, named, handed, lates):
    _, seq, half = arrived.shape
    shape = jax.ShapeDtypeStruct
    names = tuple(named)
    outs = [shape((docs, seq, half), F32), shape(gt.shape, BF)]
    for name, value in named.items():
        outs.append(shape(((1,) if name == "mixed" else ()) + value.shape, value.dtype))
    hidden = (handed.shape[1] + 2 * half) // 2
    outs += [shape((handed.shape[0], hidden), F32)] * 2
    outs += [shape((half * (hidden // half if index == VIN else 1),), F32) for index in range(9)]
    smem = pl.BlockSpec(memory_space=pltpu.SMEM)
    grad_docs, grad_tokens, *rest = pl.pallas_call(
        functools.partial(finish_kernel, names),
        out_shape=tuple(outs),
        in_specs=[smem, smem] + any_spec(2) + vmem_spec(1) + any_spec(3 + len(names)),
        out_specs=tuple(any_spec(4 + len(names)) + vmem_spec(9)),
        scratch_shapes=[
            pltpu.VMEM(arrived.shape, BF), pltpu.VMEM((docs + 1, seq, half), F32), pltpu.VMEM(gt.shape, BF),
            pltpu.SemaphoreType.DMA((SLOTS + PIECES + gt.shape[0],)),
            pltpu.SemaphoreType.DMA((len(names) + 3,)), pltpu.SemaphoreType.DMA((len(names) + 4,)),
        ] + [pltpu.VMEM(a.shape, a.dtype) for a in (*named.values(), handed, *lates)],
        compiler_params=pltpu.CompilerParams(vmem_limit_bytes=VMEM_LIMIT),
        name="finish",
    )(want, rank, arrived, gt, vec_sum, *named.values(), handed, *lates)
    return grad_docs, grad_tokens, dict(zip(names + ("outer", "inner"), rest)), rest[len(names) + 2:]


def body(
    tokens, segment_ids, positions, query_vectors, doc_owner, doc_slot, doc_store, pos_table,
    w_query, w_key, w_value, b_query, b_value, w_out, b_out, gain_attn, shift_attn,
    w_inner, b_inner, w_outer, b_outer, gain_ffn, shift_ffn, w_cls, cotangent,
):
    n = lax.axis_size("dp")
    core = lax.axis_index("mp")
    row_count, _, half = tokens.shape
    full = 2 * half
    weights = (w_query, w_key, w_value, w_out, w_inner, w_outer, w_cls)
    vectors = (b_query, b_value, b_out, gain_attn, shift_attn, b_outer, gain_ffn, shift_ffn, b_inner)
    theirs, vec_own, (want, rank, slot_of, picks), acts = forward(
        n, doc_owner, doc_slot, positions, segment_ids, vectors, doc_store, tokens, cotangent[0], pos_table, weights
    )
    own = (cotangent[0], pos_table, vec_own) + weights
    xlow, qkv, lse, ctx, nmid, imid, mlow, act, slope, nout, iout, res, summ, prod = acts

    douter, mixed, vecs, dw_cls, grad_query = share_out(n, summ, prod, query_vectors, iout, nout, res, own, theirs)

    def cross(left, right):
        left = left.reshape(-1, left.shape[-1])
        right = right.reshape(-1, right.shape[-1])
        return tn(left, right)

    summed = full // n % 16 == 0
    table = pos_table.shape[0]
    dattn, vecs, *parts = middle(n, summed, douter, act, slope, mlow, nmid, imid, ctx, vecs, own, theirs)
    mats = parts + [dw_cls] if summed else []
    grad_tokens, arrived, mixed_out, vec_sum, *sums = tail(
        n, table, slot_of, picks, vecs, positions, segment_ids, dattn, qkv, lse, mixed, xlow, own, theirs, mats
    )
    if summed:
        handed, late_inner, late_last, g_wo, g_cls, g_q, g_k, g_v, g_pos = sums
    else:
        vec_sum = lax.psum(vec_sum, "dp")
        dqkv, dstart = sums
        place = jnp.take(positions, picks[row_count:].reshape(-1, 2)[:, core], axis=0, mode="clip")
        one_hot = (place.reshape(-1)[:, None] == jnp.arange(table, dtype=jnp.int32)[None, :]).astype(BF)

        def scatter(part):
            part = lax.psum_scatter(part.astype(F32), "mp", scatter_dimension=1, tiled=True)
            return lax.psum_scatter(part, "dp", scatter_dimension=0, tiled=True)

        def in_order(part):
            return part.reshape(full, -1, 2, half).swapaxes(1, 2).reshape(full, -1)

        dinner = parts[0].transpose(1, 2, 0, 3)
        dw_outer = in_order(cross(douter, act.transpose(0, 2, 1, 3).reshape(-1, act.shape[1] * full)))
        dw_inner = in_order(cross(mlow, dinner.reshape(-1, act.shape[1] * full)))
        dw_cls = dw_cls.transpose(1, 2, 0, 3).reshape(PROJ, full)
        g_outer, g_inner, g_wo, g_qkv, g_cls, g_pos = [
            scatter(p) for p in (dw_outer, dw_inner, cross(dattn, ctx), cross(xlow, dqkv), dw_cls, cross(one_hot, dstart))
        ]
        g_q, g_k, g_v = g_qkv[:, :half], g_qkv[:, half:2 * half], g_qkv[:, 2 * half:]
        handed = jnp.concatenate([g_outer, g_inner[:, :-2 * half]], axis=1)
        late_inner, late_last = g_inner[:, -2 * half:-half], g_inner[:, -half:]
    named = dict(zip(FINISHED, (mixed_out, g_pos, g_q, g_k, g_v, g_wo, g_cls, grad_query)))
    grad_docs, grad_tokens, out, vec = finish(
        doc_store.shape[0], want, rank, arrived, grad_tokens, vec_sum, named, handed, (late_inner, late_last)
    )
    return (
        out["mixed"], grad_tokens, out["gq"], grad_docs, out["pos"], out["wq"], out["wk"], out["wv"], vec[VQ], vec[VV],
        out["wo"].T, vec[VO], vec[VGA], vec[VSA], out["inner"], vec[VIN], out["outer"].T, vec[VBO], vec[VGF], vec[VSF],
        out["cls"].T,
    )


def solution(mesh):
    rows = P("dp", None, "mp")
    ids = P("dp", None)
    cols = P(None, "mp")
    vec = P("mp")
    deep = P("mp", None)
    in_specs = (
        rows, ids, ids, ids, ids, ids, rows, cols, cols, cols, cols, vec, vec, deep, vec, vec, vec,
        cols, vec, deep, vec, vec, vec, deep, rows,
    )
    near = P("dp", "mp")
    turned = P("mp", "dp")
    out_specs = (
        rows, rows, ids, rows, near, near, near, near, vec, vec, turned, vec, vec, vec, near, vec,
        turned, vec, vec, vec, turned,
    )
    return jax.shard_map(body, mesh=mesh, in_specs=in_specs, out_specs=out_specs, check_vma=False)
```
